32 devices in a mesh: exp: 8 (over z, x), row: 2 (over y), col: 2 (over core).
Axes of the slice: x: 2, y: 2, z: 4, core: 2. Of those that a mesh axis runs over, the one named last changes fastest.
Arguments:
- layer_input: bfloat16 [2048, 2048], P(('exp', 'row'), 'col'), may hold values from -6 to 6
- attention_gain: bfloat16 [2048], P('col'), may hold values from 0.5 to 1.5
- query_weight: bfloat16 [2048, 3072], P('col', 'row'), may hold values from -0.125 to 0.125
- latent_weight: bfloat16 [2048, 576], P('col'), may hold values from -0.125 to 0.125
- latent_gain: bfloat16 [512], replicated, may hold values from 0.5 to 1.5
- keyvalue_weight: bfloat16 [512, 4096], P(None, ('row', 'col')), may hold values from -0.25 to 0.25
- output_weight: bfloat16 [2048, 2048], P(('row', 'col')), may hold values from -0.375 to 0.375
- feedforward_gain: bfloat16 [2048], P('col'), may hold values from 0.5 to 1.5
- shared_gate: bfloat16 [2048, 2816], P('col', 'row'), may hold values from -0.125 to 0.125
- shared_up: bfloat16 [2048, 2816], P('col', 'row'), may hold values from -0.125 to 0.125
- shared_down: bfloat16 [2816, 2048], P(('row', 'col')), may hold values from -0.109375 to 0.109375
- expert_gate: bfloat16 [16, 2048, 1408], P('exp', 'col', 'row'), may hold values from -0.125 to 0.125
- expert_up: bfloat16 [16, 2048, 1408], P('exp', 'col', 'row'), may hold values from -0.125 to 0.125
- expert_down: bfloat16 [16, 1408, 2048], P('exp', ('row', 'col')), may hold values from -0.15625 to 0.15625
- sequence_lengths: int32 [8, 3], P('exp'), may hold values from 1 to 192, 256 in all within a row
- expert_ids: int32 [2048, 6], P('exp'), may hold values from 0 to 15, all different within a row; in each aligned block of 128 rows (0 to 127, 128 to 255, ...) at most 96 rows name the same one
- expert_weights: float32 [2048, 6], P('exp'), may hold values from 0.06 to 0.28
- output_grad: bfloat16 [2048, 2048], P(('exp', 'row'), 'col'), may hold values from -6 to 6
Outputs:
- layer_output: bfloat16 [2048, 2048], P(('exp', 'row'), 'col')
- input_grad: float32 [2048, 2048], P(('exp', 'row'), 'col')
- attention_gain_grad: float32 [2048], P('col')
- query_weight_grad: float32 [2048, 3072], P('col', 'row')
- latent_weight_grad: float32 [2048, 576], P('col')
- latent_gain_grad: float32 [512], replicated
- keyvalue_weight_grad: float32 [512, 4096], P(None, ('row', 'col'))
- output_weight_grad: float32 [2048, 2048], P(('row', 'col'))
- feedforward_gain_grad: float32 [2048], P('col')
- shared_gate_grad: float32 [2048, 2816], P('col', 'row')
- shared_up_grad: float32 [2048, 2816], P('col', 'row')
- shared_down_grad: float32 [2816, 2048], P(('row', 'col'))
- expert_gate_grad: float32 [16, 2048, 1408], P('exp', 'col', 'row')
- expert_up_grad: float32 [16, 2048, 1408], P('exp', 'col', 'row')
- expert_down_gradient: float32 [16, 1408, 2048], P('exp', ('row', 'col'))
The draws below stay inside these ranges and needn't reach their ends.
Inputs may be any that keep to these rules, and one draw needn't show every extreme that they name: `sequence_lengths`: each row holds the lengths of the 3 sequences of one data group, in order; they sum to 256 and the largest is 192. `expert_ids`: each row names 6 different experts. Within each aligned block of 128 rows no expert is named by more than 96 rows, and in every draw some expert is named by exactly 96 rows of some block.
All inputs are finite; a program needn't handle non-finite values.
Results may differ from the reference program's by a relative error of at most 0.02.
Values may be sent and summed in bfloat16 or wider, within the bound.
A program may use at most 384 MiB of HBM per device.

```python
import math
import jax
import jax.numpy as jnp
import numpy as np
from jax import lax

D = 2048
H = 16
DN = 128
DR = 64
DV = 128
R = 512
FE = 1408
FS = 2816
TOP = 6
TOK_DEV = 128
SEQS = 3
EXPERTS = 16
GROUP = 256
TOKENS = 2048
LONGEST = 192
CAP = 96
N_EXP = 8


def shard_levels(rng, dims, cuts, smallest, top_value):
    loudness, own = 1.0, jax.random.fold_in(rng, 6)
    for dim, blocks in cuts:
        draws = jnp.exp(jax.random.uniform(jax.random.fold_in(own, dim), (blocks,), jnp.float32, smallest / len(cuts), top_value / len(cuts)))
        loudness = loudness * jnp.repeat(draws, dims[dim] // blocks).reshape([-1 if axis == dim else 1 for axis in range(len(dims))])
    return loudness


def profile(count, total, reach, skew):
    weights = [(1 << 20) // math.isqrt(grade ** skew) + 1 for grade in range(2, count + 1)]
    spare, holding = total - reach - (count - 1), [1] * (count - 1)
    while spare > 0:
        candidates = [i for i in range(count - 1) if holding[i] < reach]
        whole, left = sum([weights[i] for i in candidates]), spare
        for i in candidates:
            addition = min(reach - holding[i], max(1, left * weights[i] // whole), spare)
            holding[i] = holding[i] + addition
            spare = spare - addition
    return np.array([reach] + holding)


def uneven(own_key, number_of, total, reach, slope):
    if number_of == 2:
        one = jax.random.randint(own_key, (), max(1, total - reach), min(reach, total - 1) + 1)
        return jnp.stack([one, total - one])
    sizes = jnp.asarray(profile(number_of, total, reach, slope), jnp.int32)
    couples = (number_of - 1) // 2
    giver, receiver = sizes[1:1 + 2 * couples:2], sizes[2:2 + 2 * couples:2]
    margin = jnp.minimum(giver - 1, reach - receiver)
    passed = jax.random.randint(jax.random.fold_in(own_key, 1), (couples,), 0, 1 << 20) % (margin + 1)
    sizes = sizes.at[1:1 + 2 * couples:2].set(giver - passed).at[2:2 + 2 * couples:2].set(receiver + passed)
    return sizes[jax.random.permutation(jax.random.fold_in(own_key, 2), number_of)]


def routed_block(rng, own, number, rows, number_of, top, limit, slope):
    sequence = jax.random.permutation(rng, number_of)
    heavy_load, usual = shares(number_of, rows * top, limit, slope, True), shares(number_of, rows * top, limit, slope, False)
    places = jnp.arange(number_of)

    def named(sizes, turn):
        used = int((sizes > 0).sum())
        fixed = max(1, used // 4)
        moved = fixed + (places - fixed + turn * (used - fixed)) % max(1, number_of - fixed)
        return jnp.zeros((number_of,), jnp.int32).at[sequence[jnp.where(places < fixed, places, moved)]].set(jnp.asarray(sizes, jnp.int32))

    sizes = jnp.where(number % 4 == 0, named(heavy_load, number // 4), named(usual, number - number // 4 - 1))
    mixed = jax.random.permutation(jax.random.fold_in(own, 3), number_of)
    donor, sink = mixed[0:number_of // 2 * 2:2], mixed[1:number_of // 2 * 2:2]
    room = jnp.minimum(sizes[donor] - 1, limit - sizes[sink]) // 2
    room = jnp.where((donor == sequence[0]) | (sink == sequence[0]) | (sizes[sink] == 0), 0, jnp.maximum(room, 0))
    moved = jax.random.randint(jax.random.fold_in(own, 4), (number_of // 2,), 0, 1 << 20) % (room + 1)
    sizes = sizes.at[donor].add(-moved).at[sink].add(moved)
    items = jnp.searchsorted(jnp.cumsum(sizes), jnp.arange(rows * top), side="right").astype(jnp.int32)
    grid = items.reshape(top, rows).T
    grid = grid[jax.random.permutation(jax.random.fold_in(own, 1), rows)]
    turn = jax.random.randint(jax.random.fold_in(own, 2), (rows, 1), 0, top)
    return jnp.take_along_axis(grid, (jnp.arange(top)[None, :] + turn) % top, axis=1)


def shares(count, total, most, lean, full):
    portions = [(1 << 20) // math.isqrt(standing ** lean) + 1 for standing in range(1, count + 1)]
    largest = most if full else min(most, max(-(-total // count), total * portions[0] // sum(portions)))
    least = 1 if total - largest >= count - 1 else 0
    counts, rest = [largest] + [least] * (count - 1), total - largest - least * (count - 1)
    while rest > 0:
        free = [i for i in range(1, count) if counts[i] < largest] or [i for i in range(1, count) if counts[i] < most]
        mass, remaining = sum([portions[i] for i in free]), rest
        for i in free:
            extra = min(most - counts[i], max(1, remaining * portions[i] // mass), rest)
            counts[i] = counts[i] + extra
            rest = rest - extra
    return np.array(counts)


def centred(stream_key, shape, spread, bound, cuts=(), kind=jnp.bfloat16):
    drawn = jax.random.normal(stream_key, shape, jnp.float32) * spread
    if len(cuts) > 0:
        drawn = shard_levels(stream_key, shape, cuts, -0.22, 0.18) * drawn
    return jnp.clip(drawn, min=-bound, max=bound).astype(kind)


def setup_inputs(seed: int = 0) -> dict:
    arg_keys = jax.random.split(jax.random.key(seed), 19)
    layer_input = centred(arg_keys[0], (TOKENS, D), 1.0, 6.0, ((0, 16), (1, 2)))
    attention_gain = jnp.clip(1.0 + 0.1 * jax.random.normal(arg_keys[1], (D,), jnp.float32), 0.5, 1.5).astype(jnp.bfloat16)
    query_weight = centred(arg_keys[2], (D, H * (DN + DR)), D ** -0.5, 0.125, ((0, 2), (1, 2)))
    latent_weight = centred(arg_keys[3], (D, R + DR), D ** -0.5, 0.125, ((0, 2),))
    latent_gain = jnp.clip(1.0 + 0.1 * jax.random.normal(arg_keys[4], (R,), jnp.float32), 0.5, 1.5).astype(jnp.bfloat16)
    keyvalue_weight = centred(arg_keys[5], (R, H * (DN + DV)), R ** -0.5, 0.25, ((1, 4),))
    output_weight = centred(arg_keys[6], (H * DV, D), (H * DV // 8) ** -0.5, 0.375, ((0, 4),))
    feedforward_gain = jnp.clip(1.0 + 0.1 * jax.random.normal(arg_keys[7], (D,), jnp.float32), 0.5, 1.5).astype(jnp.bfloat16)
    shared_gate = centred(arg_keys[8], (D, FS), D ** -0.5, 0.125, ((0, 2), (1, 2)))
    shared_up = centred(arg_keys[9], (D, FS), D ** -0.5, 0.125, ((0, 2), (1, 2)))
    shared_down = centred(arg_keys[10], (FS, D), FS ** -0.5, 0.109375, ((0, 4),))
    expert_gate = centred(arg_keys[11], (EXPERTS, D, FE), D ** -0.5, 0.125, ((0, 8), (1, 2), (2, 2)))
    expert_up = centred(arg_keys[12], (EXPERTS, D, FE), D ** -0.5, 0.125, ((0, 8), (1, 2), (2, 2)))
    expert_down = centred(arg_keys[13], (EXPERTS, FE, D), FE ** -0.5, 0.15625, ((0, 8), (1, 4)))
    sequence_lengths = jax.vmap(lambda own: uneven(own, SEQS, GROUP, LONGEST, 2))(jax.random.split(arg_keys[14], N_EXP)).reshape((N_EXP, SEQS)).astype(jnp.int32)
    expert_ids_keys = jax.random.split(jax.random.fold_in(arg_keys[15], 1), TOKENS // TOK_DEV)
    expert_ids_turns = jax.random.permutation(jax.random.fold_in(arg_keys[15], 3), TOKENS // TOK_DEV)
    expert_ids = jax.vmap(lambda own, number: routed_block(jax.random.fold_in(arg_keys[15], 2), own, number, TOK_DEV, EXPERTS, TOP, CAP, 1))(expert_ids_keys, expert_ids_turns).reshape((TOKENS, TOP))
    expert_weights = jnp.clip(0.06 + 0.22 * jax.random.uniform(arg_keys[16], (TOKENS, TOP), jnp.float32) ** shard_levels(arg_keys[16], (TOKENS, TOP), ((0, 8),), -0.2, 0.2), 0.06, 0.28)
    output_grad = centred(arg_keys[17], (TOKENS, D), 1.0, 6.0, ((0, 16), (1, 2)))
    return dict(layer_input=layer_input, attention_gain=attention_gain, query_weight=query_weight, latent_weight=latent_weight, latent_gain=latent_gain, keyvalue_weight=keyvalue_weight, output_weight=output_weight, feedforward_gain=feedforward_gain, shared_gate=shared_gate, shared_up=shared_up, shared_down=shared_down, expert_gate=expert_gate, expert_up=expert_up, expert_down=expert_down, sequence_lengths=sequence_lengths, expert_ids=expert_ids, expert_weights=expert_weights, output_grad=output_grad)


EPSILON = 1e-06
ROPE_BASE = 50000.0
NEGATIVE = -1e+30
HIGHEST = lax.Precision.HIGHEST

@jax.custom_vjp
def low(v):
    return lax.optimization_barrier(v.astype(jnp.bfloat16)).astype(jnp.float32)

@jax.custom_vjp
def low_back(v):
    return v

def low_keep(v):
    return (low(v), None)

def low_pass(kept, grad):
    return (grad,)

def back_keep(v):
    return (v, None)

def back_low(kept, grad):
    return (low(grad),)
low.defvjp(low_keep, low_pass)
low_back.defvjp(back_keep, back_low)

def matmul(former, latter):
    return jnp.dot(former, latter, precision=HIGHEST, preferred_element_type=jnp.float32)

def rms_scale(values, gain_vector):
    return values * lax.rsqrt(lax.optimization_barrier(jnp.mean(values * values, axis=-1, keepdims=True)) + EPSILON) * gain_vector

def rotate(values, cosine_table, sine_table):
    half_width = values.shape[-1] // 2
    former, latter = (values[..., :half_width], values[..., half_width:])
    return jnp.concatenate([former * cosine_table - latter * sine_table, latter * cosine_table + former * sine_table], axis=-1)

def sequence_layout(lengths, group_size):
    seq_ends = jnp.cumsum(lengths).astype(jnp.int32)
    token_order = jnp.arange(group_size, dtype=jnp.int32)
    segment = lax.optimization_barrier(jnp.sum((token_order[:, None] >= seq_ends[None, :]).astype(jnp.int32), axis=1)).astype(jnp.int32)
    seq_starts = (seq_ends - lengths).astype(jnp.int32)
    own_start = lax.optimization_barrier(jnp.sum(jnp.where(segment[:, None] == jnp.arange(lengths.shape[0], dtype=jnp.int32)[None, :], seq_starts[None, :], 0), axis=1)).astype(jnp.int32)
    return (segment, token_order - own_start)

def group_attention(pieces):
    queries, keys_all, values, segment = pieces
    group_size = keys_all.shape[0]
    token_order = jnp.arange(group_size, dtype=jnp.int32)
    scores = low_back(jnp.einsum('qhd,khd->hqk', queries, keys_all, precision=HIGHEST) * (DN + DR) ** (-0.5))
    allowed = (segment[:, None] == segment[None, :]) & (token_order[None, :] <= token_order[:, None])
    scores = jnp.where(allowed[None], scores, NEGATIVE)
    row_peak = lax.optimization_barrier(jnp.max(scores, axis=-1, keepdims=True))
    exponent = jnp.exp(scores - row_peak)
    weights = low(exponent / lax.optimization_barrier(jnp.sum(exponent, axis=-1, keepdims=True)))
    return jnp.einsum('hqk,khd->qhd', weights, values, precision=HIGHEST)

def layer_forward(layer_input, attention_gain, query_weight, latent_weight, latent_gain, keyvalue_weight, output_weight, feedforward_gain, shared_gate, shared_up, shared_down, expert_gate, expert_up, expert_down, segment, cosine_table, sine_table, gate_matrix):
    tokens_all = layer_input.shape[0]
    attention_input = low(rms_scale(layer_input, attention_gain))
    query = low_back(matmul(attention_input, query_weight)).reshape(tokens_all, H, DN + DR)
    latent = low_back(matmul(attention_input, latent_weight))
    compressed = low(rms_scale(latent[:, :R], latent_gain))
    rope_key = low(rotate(latent[:, R:], cosine_table, sine_table))
    keyvalue = low(low_back(matmul(compressed, keyvalue_weight))).reshape(tokens_all, H, DN + DV)
    queries = low(jnp.concatenate([query[..., :DN], rotate(query[..., DN:], cosine_table[:, None, :], sine_table[:, None, :])], axis=-1))
    keys_all = jnp.concatenate([keyvalue[..., :DN], jnp.broadcast_to(rope_key[:, None, :], (tokens_all, H, DR))], axis=-1)
    values = keyvalue[..., DN:]

    def grouped(array):
        return array.reshape((N_EXP, GROUP) + array.shape[1:])
    attended = lax.map(jax.checkpoint(group_attention), (grouped(queries), grouped(keys_all), grouped(values), grouped(segment)))
    attention_out = low(low_back(attended.reshape(tokens_all, H * DV)))
    hidden_state = layer_input + low_back(matmul(attention_out, output_weight))
    mixer_input = low(rms_scale(hidden_state, feedforward_gain))
    gating = low_back(matmul(mixer_input, shared_gate))
    upward = low_back(matmul(mixer_input, shared_up))
    shared_out = low_back(matmul(low(jax.nn.silu(gating) * upward), shared_down))

    def one_expert(carried, pieces):
        w_gate, w_up, w_down, share_column = pieces
        expert_input = low_back(mixer_input)
        expert_gating = low_back(matmul(expert_input, w_gate))
        expert_upward = low_back(matmul(expert_input, w_up))
        produced = low(low_back(matmul(low(jax.nn.silu(expert_gating) * expert_upward), w_down)))
        return (carried + share_column[:, None] * produced, None)
    routed, leftover = lax.scan(jax.checkpoint(one_expert), jnp.zeros(layer_input.shape, jnp.float32), (expert_gate, expert_up, expert_down, gate_matrix.T))
    return hidden_state + shared_out + routed

def reference(layer_input, attention_gain, query_weight, latent_weight, latent_gain, keyvalue_weight, output_weight, feedforward_gain, shared_gate, shared_up, shared_down, expert_gate, expert_up, expert_down, sequence_lengths, expert_ids, expert_weights, output_grad):

    def layout_row(lengths):
        return sequence_layout(lengths, GROUP)
    segments, places = jax.vmap(layout_row)(sequence_lengths)
    segment = segments.reshape(-1)
    inverse_frequency = ROPE_BASE ** (-(jnp.arange(DR // 2, dtype=jnp.float32) * 2.0 / DR))
    angles = places.reshape(-1).astype(jnp.float32)[:, None] * inverse_frequency[None, :]
    cosine_table, sine_table = (jnp.cos(angles), jnp.sin(angles))
    chosen = (expert_ids[:, :, None] == jnp.arange(EXPERTS, dtype=jnp.int32)[None, None, :]).astype(jnp.float32)
    gate_matrix = lax.optimization_barrier(jnp.sum(expert_weights[:, :, None] * chosen, axis=1))
    arrays = tuple((array.astype(jnp.float32) for array in (layer_input, attention_gain, query_weight, latent_weight, latent_gain, keyvalue_weight, output_weight, feedforward_gain, shared_gate, shared_up, shared_down, expert_gate, expert_up, expert_down)))

    def forward(*inputs):
        return layer_forward(*inputs, segment, cosine_table, sine_table, gate_matrix)
    output, pullback = jax.vjp(forward, *arrays)
    gradients = pullback(output_grad.astype(jnp.float32))
    return (output.astype(jnp.bfloat16), gradients[0], gradients[1], gradients[2], gradients[3], gradients[4], gradients[5], gradients[6], gradients[7], gradients[8], gradients[9], gradients[10], gradients[11], gradients[12], gradients[13])
```

```python
import functools

import jax
import jax.numpy as jnp
from jax import lax
from jax.experimental import pallas as pl
from jax.experimental.pallas import tpu as pltpu
from jax.sharding import PartitionSpec as P

DN = 128
DR = 64
DV = 128
R = 512
TOP = 6


EPSILON = 1e-06
ROPE_BASE = 50000.0
NEGATIVE = -1e30


def matmul(former, latter):
    return jnp.dot(former, latter, preferred_element_type=jnp.float32)


def matmul_left(former, latter):
    return lax.dot_general(
        former, latter, (((0,), (0,)), ((), ())), preferred_element_type=jnp.float32
    )


def matmul_right(former, latter):
    return lax.dot_general(
        former, latter, (((1,), (1,)), ((), ())), preferred_element_type=jnp.float32
    )


def sequence_layout(lengths, group_size):
    seq_ends = jnp.cumsum(lengths)
    token_order = jnp.arange(group_size, dtype=jnp.int32)
    segment = jnp.sum((token_order[:, None] >= seq_ends[None, :]).astype(jnp.int32), axis=1)
    seq_starts = seq_ends - lengths
    own_start = jnp.sum(
        jnp.where(
            segment[:, None] == jnp.arange(lengths.shape[0], dtype=jnp.int32)[None, :],
            seq_starts[None, :],
            0,
        ),
        axis=1,
    )
    return (segment, token_order - own_start)


def rope_tables(places):
    inverse_frequency = ROPE_BASE ** (-(jnp.arange(DR // 2, dtype=jnp.float32) * 2.0 / DR))
    angles = places.astype(jnp.float32)[:, None] * inverse_frequency[None, :]
    return (jnp.cos(angles), jnp.sin(angles))


MESH = pl.DeviceIdType.MESH
VMEM_LIMIT = 60 * 1024 * 1024
HALF = 2


def full_spec(array):
    zeros = (0,) * array.ndim
    return pl.BlockSpec(array.shape, lambda *_: zeros)


ANY_SPEC = pl.BlockSpec(memory_space=pl.ANY)


def swap_core(values):
    return lax.ppermute(values, "col", [(0, 1), (1, 0)])


def half_sums(values):
    return lax.psum(values, "col")


def norm_backward(gradient, normed, inverse_rms, gain_vector):
    full_width = normed.shape[1] * lax.axis_size("col")
    scaled = gradient * gain_vector
    inner_sum = half_sums(jnp.sum(scaled * normed, axis=1)) / full_width
    return (
        inverse_rms * (scaled - normed * inner_sum[:, None]),
        jnp.sum(gradient * normed, axis=0),
    )


def rotary(values, cosine_both, sine_signed):
    half = values.shape[-1] // 2
    swapped = jnp.concatenate([values[:, half:], values[:, :half]], axis=-1)
    return values * cosine_both + swapped * sine_signed


def project_kernel(
    _, own, other, gain_own, gain_other, query_own, query_other, latent_own, latent_other,
    latent_gain, keyvalue_weight, cosine_both, sine_signed, query, keyvalue, rope_key, *rest,
    everyone
):
    rows_own = own[...].astype(jnp.float32)
    rows_other = other[...].astype(jnp.float32)
    total = jnp.sum(rows_own * rows_own, axis=1, keepdims=True)
    total = total + jnp.sum(rows_other * rows_other, axis=1, keepdims=True)
    scale = lax.rsqrt(total / (2 * own.shape[1]) + EPSILON)
    rows_own = (rows_own * scale * gain_own[:1]).astype(jnp.bfloat16)
    rows_other = (rows_other * scale * gain_other[:1]).astype(jnp.bfloat16)
    queries = matmul(rows_own, query_own[...]) + matmul(rows_other, query_other[...])
    cosine, sine = cosine_both[...], sine_signed[...]
    for first in range(0, query.shape[1], DN + DR):
        rope = rotary(queries[:, first + DN : first + DN + DR], cosine, sine)
        query[:, first : first + DN + DR] = jnp.concatenate(
            [queries[:, first : first + DN], rope], axis=1
        ).astype(jnp.bfloat16)
    latent = matmul_right(rows_own, latent_own[...]) + matmul_right(rows_other, latent_other[...])
    raw = latent[:, :R]
    latent_scale = lax.rsqrt(jnp.mean(raw * raw, axis=1, keepdims=True) + EPSILON)
    latent_normed = raw * latent_scale
    compressed = (latent_normed * latent_gain[...]).astype(jnp.bfloat16)
    keyvalue[...] = matmul(compressed, keyvalue_weight[...]).astype(jnp.bfloat16)
    rope_key[...] = rotary(latent[:, R:], cosine, sine).astype(jnp.bfloat16)
    if everyone:
        rest[0][...] = rows_own.T
        rest[1][...] = compressed.T
    else:
        rest[0][...] = latent_normed
        rest[1][...] = latent_scale


def project(col, own, other, cosine_both, sine_signed, weights, everyone):
    count, width = own.shape
    tile = min(256, count)
    query_width = weights[3].shape[1]
    keyvalue_width = weights[7].shape[1]

    def rows(columns):
        return pl.BlockSpec((tile, columns), lambda step, col: (step, 0))

    def turned(features):
        return pl.BlockSpec((features, tile), lambda step, col: (0, step))

    shapes = [
        ((count, query_width), jnp.bfloat16, rows(query_width)),
        ((count, keyvalue_width), jnp.bfloat16, rows(keyvalue_width)),
        ((count, DR), jnp.bfloat16, rows(DR)),
    ]
    if everyone:
        shapes += [
            ((width, count), jnp.bfloat16, turned(width)),
            ((R, count), jnp.bfloat16, turned(R)),
        ]
    else:
        shapes += [((count, R), jnp.float32, rows(R)), ((count, 1), jnp.float32, rows(1))]
    weight_specs = [full_spec(array) for array in weights]
    weight_specs[2] = pl.BlockSpec((width, query_width), lambda step, col: (0, col[0]))
    flops = 2 * count * (2 * width * (query_width + R + DR) + R * keyvalue_width)
    return pl.pallas_call(
        functools.partial(project_kernel, everyone=everyone),
        out_shape=[jax.ShapeDtypeStruct(shape, kind) for shape, kind, _ in shapes],
        grid_spec=pltpu.PrefetchScalarGridSpec(
            num_scalar_prefetch=1,
            grid=(count // tile,),
            in_specs=[rows(width), rows(width)] + weight_specs + [rows(DR), rows(DR)],
            out_specs=[spec for _, _, spec in shapes],
        ),
        compiler_params=pltpu.CompilerParams(vmem_limit_bytes=VMEM_LIMIT),
        cost_estimate=pl.CostEstimate(
            flops=flops, bytes_accessed=count * 12000 + 7 * 1024 * 1024, transcendentals=0
        ),
    )(col, own, other, *weights, cosine_both, sine_signed)


def attention_kernel(
    lengths, query, keyvalue, rope_key, *rest, backward
):
    if backward:
        cosine_both, sine_signed, grad_out, attended, grad_query, grad_keyvalue, grad_rope = rest
        cosine, sine = cosine_both[...], sine_signed[...]
    else:
        (attended,) = rest
    group = pl.program_id(0)
    size = query.shape[0]
    heads = query.shape[1] // (DN + DR)
    factor = (DN + DR) ** (-0.5)
    row = lax.broadcasted_iota(jnp.int32, (size, size), 0)
    column = lax.broadcasted_iota(jnp.int32, (size, size), 1)
    allowed = column <= row
    end = jnp.int32(0)
    for number in range(lengths.shape[1] - 1):
        end = end + lengths[group, number]
        allowed = allowed & ((row < end) == (column < end))
    rope_keys = rope_key[...]
    rope_total = jnp.zeros((size, DR), jnp.float32)
    for head in range(heads):
        first = head * (DN + DR)
        queries = query[:, first : first + DN + DR]
        first_key = head * (DN + DV)
        keys = jnp.concatenate([keyvalue[:, first_key : first_key + DN], rope_keys], axis=1)
        values = keyvalue[:, first_key + DN : first_key + DN + DV]
        scores = jnp.where(allowed, matmul_right(queries, keys) * factor, NEGATIVE)
        exponent = jnp.exp(scores - jnp.max(scores, axis=1, keepdims=True))
        probabilities = exponent / jnp.sum(exponent, axis=1, keepdims=True)
        weights = probabilities.astype(jnp.bfloat16)
        result = matmul(weights, values).astype(jnp.bfloat16)
        if backward:
            attended[head * DV : (head + 1) * DV, :] = result.T
        else:
            attended[:, head * DV : (head + 1) * DV] = result
        if backward:
            grad_head = grad_out[:, head * DV : (head + 1) * DV]
            grad_probs = matmul_right(grad_head, values)
            inner = jnp.sum(probabilities * grad_probs, axis=1, keepdims=True)
            grad_scores = (probabilities * (grad_probs - inner)).astype(jnp.bfloat16)
            grad_queries = matmul(grad_scores, keys) * factor
            grad_keys = matmul_left(grad_scores, queries) * factor
            unrotated = rotary(grad_queries[:, DN:], cosine, -sine)
            grad_query[:, first : first + DN + DR] = jnp.concatenate(
                [grad_queries[:, :DN], unrotated], axis=1
            ).astype(jnp.bfloat16)
            grad_keyvalue[:, first_key : first_key + DN] = grad_keys[:, :DN].astype(jnp.bfloat16)
            grad_keyvalue[:, first_key + DN : first_key + DN + DV] = matmul_left(
                weights, grad_head
            ).astype(jnp.bfloat16)
            rope_total = rope_total + grad_keys[:, DN:]
    if backward:
        grad_rope[...] = rotary(rope_total, cosine, -sine)


def attend(
    lengths, query, keyvalue, rope_key, cosine_both=None, sine_signed=None, grad_out=None
):
    groups = lengths.shape[0]
    size = query.shape[0] // groups
    heads = query.shape[1] // (DN + DR)

    def block(width):
        return pl.BlockSpec((size, width), lambda group, lengths: (group, 0))

    def result(width, kind):
        return jax.ShapeDtypeStruct((groups * size, width), kind)

    operands = [query, keyvalue, rope_key]
    results = [result(heads * DV, jnp.bfloat16)]
    out_specs = [block(heads * DV)]
    if grad_out is not None:
        results = [jax.ShapeDtypeStruct((heads * DV, groups * size), jnp.bfloat16)]
        out_specs = [pl.BlockSpec((heads * DV, size), lambda group, lengths: (0, group))]
        operands += [cosine_both, sine_signed, grad_out]
        results += [
            result(heads * (DN + DR), jnp.bfloat16),
            result(heads * (DN + DV), jnp.bfloat16),
            result(DR, jnp.float32),
        ]
        out_specs += [block(array.shape[1]) for array in results[1:]]
    products = 7 if grad_out is not None else 2
    return pl.pallas_call(
        functools.partial(attention_kernel, backward=grad_out is not None),
        out_shape=results,
        grid_spec=pltpu.PrefetchScalarGridSpec(
            num_scalar_prefetch=1,
            grid=(groups,),
            in_specs=[block(array.shape[1]) for array in operands],
            out_specs=out_specs,
        ),
        compiler_params=pltpu.CompilerParams(vmem_limit_bytes=VMEM_LIMIT),
        cost_estimate=pl.CostEstimate(
            flops=groups * heads * products * 2 * size * size * 160,
            bytes_accessed=groups * size * heads * (1024 + 512 + 2000),
            transcendentals=groups * heads * size * size,
        ),
    )(lengths, *operands)


def positions():
    exp_count = lax.axis_size("exp")
    slow = min(4, exp_count)
    fast = exp_count // slow
    row_count = lax.axis_size("row")
    exp_index = lax.axis_index("exp")
    place = (exp_index // fast, exp_index % fast, lax.axis_index("row"), lax.axis_index("col"))
    return place, (slow, fast, row_count)


def peers(with_core):
    (slow_at, fast_at, row_at, col_at), (slow, fast, row_count) = positions()
    slow_ids = [
        {"exp": (slow_at + step) % slow * fast + fast_at} for step in range(1, slow)
    ]
    fast_ids = [
        {"exp": slow_at * fast + (fast_at + step) % fast} for step in range(1, fast)
    ]
    row_ids = [{"row": (row_at + step) % row_count} for step in range(1, row_count)]
    core_ids = [{"col": 1 - col_at}] if with_core else []
    return slow_ids, fast_ids, row_ids, core_ids


def enter(groups):
    barrier = pltpu.get_barrier_semaphore()
    count = 0
    for group in groups:
        for device in group:
            pl.semaphore_signal(barrier, inc=1, device_id=device, device_id_type=MESH)
            count += 1
    pl.semaphore_wait(barrier, count)


def remote(src, dst, sems, index, device):
    copy = pltpu.make_async_remote_copy(
        src_ref=src,
        dst_ref=dst,
        send_sem=sems.at[(0, *index)],
        recv_sem=sems.at[(1, *index)],
        device_id=device,
        device_id_type=MESH,
    )
    copy.start()
    return copy


def wait_arrived(dst, sems, index):
    pltpu.make_async_copy(dst, dst, sems.at[(1, *index)]).wait()


def start_kernel(
    rows, tables, query, latent, gain,
    rows_own, rows_other, tables_all, query_other, latent_other, gain_other,
    local_sems, row_sems, core_rows, slow_sems, fast_sems, core_sems
):
    (slow_at, fast_at, row_at, col_at), (slow, fast, row_count) = positions()
    slow_ids, fast_ids, row_ids, core_ids = peers(True)
    core = core_ids[0]
    width = query_other.shape[1]
    mine = slow_at * fast + fast_at
    given = pl.ds(pl.multiple_of((1 - col_at) * width, width), width)
    enter((slow_ids, fast_ids, row_ids, core_ids))
    kept = [
        pltpu.make_async_copy(rows, rows_own.at[row_at], local_sems.at[0]),
        pltpu.make_async_copy(tables, tables_all.at[mine], local_sems.at[1]),
    ]
    for copy in kept:
        copy.start()
    started = [
        remote(rows, rows_own.at[row_at], row_sems, (number,), device)
        for number, device in enumerate(row_ids)
    ]
    started.append(remote(rows, rows_other.at[row_at], core_rows, (0,), core))
    started.append(remote(gain, gain_other, core_sems, (0,), core))
    started.append(remote(query.at[:, given], query_other, core_sems, (1,), core))
    started.append(remote(latent, latent_other, core_sems, (2,), core))
    for number, device in enumerate(slow_ids):
        started.append(remote(tables, tables_all.at[mine], slow_sems, (number,), device))
    for number, device in enumerate(fast_ids):
        started.append(remote(tables, tables_all.at[mine], fast_sems, (number, 0), device))
    for offset in range(1, row_count):
        index = (row_at + row_count - offset) % row_count
        wait_arrived(rows_own.at[index], row_sems, (offset - 1,))
        started.append(
            remote(rows_own.at[index], rows_other.at[index], core_rows, (offset,), core)
        )
    for offset in range(1, slow):
        index = (slow_at + slow - offset) % slow * fast + fast_at
        wait_arrived(tables_all.at[index], slow_sems, (offset - 1,))
        for number, device in enumerate(fast_ids):
            started.append(
                remote(
                    tables_all.at[index], tables_all.at[index], fast_sems, (number, offset), device
                )
            )
    for offset in range(slow):
        for number in range(1, fast):
            index = (slow_at + slow - offset) % slow * fast + (fast_at + fast - number) % fast
            wait_arrived(tables_all.at[index], fast_sems, (number - 1, offset))
    for offset in range(row_count):
        index = (row_at + row_count - offset) % row_count
        wait_arrived(rows_other.at[index], core_rows, (offset,))
    for number, target in enumerate((gain_other, query_other, latent_other)):
        wait_arrived(target, core_sems, (number,))
    for copy in started:
        copy.wait_send()
    for copy in kept:
        copy.wait()


def begin(rows, tables, query, latent, gain, collective_id):
    exp_count, row_count = lax.axis_size("exp"), lax.axis_size("row")
    slow = min(4, exp_count)
    fast = exp_count // slow

    def like(*shape, array):
        return jax.ShapeDtypeStruct(shape, array.dtype)

    return pl.pallas_call(
        start_kernel,
        out_shape=[
            like(row_count, *rows.shape, array=rows),
            like(row_count, *rows.shape, array=rows),
            like(exp_count, *tables.shape, array=tables),
            like(query.shape[0], query.shape[1] // 2, array=query),
            like(*latent.shape, array=latent),
            like(*gain.shape, array=gain),
        ],
        in_specs=[ANY_SPEC] * 5,
        out_specs=[ANY_SPEC] * 6,
        scratch_shapes=[
            pltpu.SemaphoreType.DMA((2,)),
            pltpu.SemaphoreType.DMA((2, row_count - 1)),
            pltpu.SemaphoreType.DMA((2, row_count)),
            pltpu.SemaphoreType.DMA((2, slow - 1)),
            pltpu.SemaphoreType.DMA((2, fast - 1, slow)),
            pltpu.SemaphoreType.DMA((2, 3)),
        ],
        compiler_params=pltpu.CompilerParams(
            collective_id=collective_id, has_side_effects=True
        ),
    )(rows, tables, query, latent, gain)


def mix_kernel(
    attended, weight, rows, gain, hidden, normed, inverse, mixer,
    given, from_core, rows_out, from_rows, squares, squares_in, core_sems, row_sems
):
    (_, _, row_at, col_at), (_, _, row_count) = positions()
    _, _, row_ids, core_ids = peers(True)
    core = core_ids[0]
    count, width = rows.shape
    enter((row_ids, core_ids))
    own_half = pl.ds(pl.multiple_of(col_at * width, width), width)
    other_half = pl.ds(pl.multiple_of((1 - col_at) * width, width), width)
    given[...] = matmul(attended[...], weight[:, other_half]).astype(jnp.bfloat16)
    started = [remote(given, from_core, core_sems, (0,), core)]
    total = matmul(attended[...], weight[:, own_half])
    wait_arrived(from_core, core_sems, (0,))
    total = total + from_core[...].astype(jnp.float32)
    rows_out[...] = total.astype(jnp.bfloat16).reshape(rows_out.shape)
    for number, device in enumerate(row_ids):
        goal = (row_at + number + 1) % row_count
        started.append(remote(rows_out.at[goal], from_rows.at[number], row_sems, (number,), device))
    state = rows[...].astype(jnp.float32) + rows_out[row_at].astype(jnp.float32)
    for number in range(row_count - 1):
        wait_arrived(from_rows.at[number], row_sems, (number,))
        state = state + from_rows[number].astype(jnp.float32)
    hidden[...] = state
    own_squares = jnp.sum(state * state, axis=1, keepdims=True)
    squares[...] = jnp.broadcast_to(own_squares, squares.shape)
    started.append(remote(squares, squares_in, core_sems, (1,), core))
    wait_arrived(squares_in, core_sems, (1,))
    scale = lax.rsqrt((squares[...] + squares_in[...]) / (2 * width) + EPSILON)
    inverse[...] = scale
    unit = state * scale[:, :1]
    normed[...] = unit
    mixer[...] = (unit * gain[...]).astype(jnp.bfloat16)
    for copy in started:
        copy.wait_send()


def mix(attended, weight, rows, gain, collective_id):
    row_count = lax.axis_size("row")
    count, width = rows.shape
    vmem = pl.BlockSpec(memory_space=pltpu.VMEM)
    wide = jax.ShapeDtypeStruct((count, width), jnp.float32)
    return pl.pallas_call(
        mix_kernel,
        out_shape=[
            wide,
            wide,
            jax.ShapeDtypeStruct((count, 128), jnp.float32),
            jax.ShapeDtypeStruct((count, width), jnp.bfloat16),
        ],
        in_specs=[vmem] * 4,
        out_specs=[vmem] * 4,
        scratch_shapes=[
            pltpu.VMEM((row_count * count, width), jnp.bfloat16),
            pltpu.VMEM((row_count * count, width), jnp.bfloat16),
            pltpu.VMEM((row_count, count, width), jnp.bfloat16),
            pltpu.VMEM((row_count - 1, count, width), jnp.bfloat16),
            pltpu.VMEM((count, 128), jnp.float32),
            pltpu.VMEM((count, 128), jnp.float32),
            pltpu.SemaphoreType.DMA((2, 2)),
            pltpu.SemaphoreType.DMA((2, row_count - 1)),
        ],
        compiler_params=pltpu.CompilerParams(
            collective_id=collective_id, has_side_effects=True, vmem_limit_bytes=VMEM_LIMIT
        ),
    )(attended, weight, rows, gain)


def gather_kernel(
    source, own, other, local_sem, slow_sems, fast_sems, row_sems, low_sems, high_sems,
    core_sems, core_half_sems
):
    (slow_at, fast_at, row_at, _), (slow, fast, row_count) = positions()
    slow_ids, fast_ids, row_ids, core_ids = peers(True)
    core = core_ids[0]
    half = source.shape[0] // 2
    low, high = pl.ds(0, half), pl.ds(half, half)
    started = []

    def block(slow_off, fast_off, row_off):
        slow_index = (slow_at + slow - slow_off) % slow
        fast_index = (fast_at + fast - fast_off) % fast
        return (slow_index * fast + fast_index) * row_count + (row_at + row_count - row_off) % row_count

    def send(src, dst, sems, index, device):
        copy = pltpu.make_async_remote_copy(
            src_ref=src,
            dst_ref=dst,
            send_sem=sems.at[(0, *index)],
            recv_sem=sems.at[(1, *index)],
            device_id=device,
            device_id_type=MESH,
        )
        copy.start()
        started.append(copy)

    def arrived(dst, sems, index):
        pltpu.make_async_copy(dst, dst, sems.at[(1, *index)]).wait()

    enter((slow_ids, fast_ids, row_ids, core_ids))
    mine = block(0, 0, 0)
    keep = pltpu.make_async_copy(source, own.at[mine], local_sem)
    keep.start()
    for number, device in enumerate(slow_ids):
        send(source, own.at[mine], slow_sems, (number,), device)

    def forward_line(src, index, line):
        for number, device in enumerate(fast_ids):
            send(src, own.at[index], fast_sems, (number, line), device)
        for number, device in enumerate(row_ids):
            send(src, own.at[index], row_sems, (number, line), device)
        send(src, other.at[index], core_sems, (0, 0, line), core)

    forward_line(source, mine, 0)
    for line in range(1, slow):
        index = block(line, 0, 0)
        arrived(own.at[index], slow_sems, (line - 1,))
        forward_line(own.at[index], index, line)
    for line in range(slow):
        for fast_off in range(1, fast):
            index = block(line, fast_off, 0)
            arrived(own.at[index], fast_sems, (fast_off - 1, line))
            for number, device in enumerate(row_ids):
                send(
                    own.at[index, low], own.at[index, low], low_sems,
                    (fast_off - 1, number, line), device,
                )
            send(own.at[index], other.at[index], core_sems, (fast_off, 0, line), core)
        for row_off in range(1, row_count):
            index = block(line, 0, row_off)
            arrived(own.at[index], row_sems, (row_off - 1, line))
            for number, device in enumerate(fast_ids):
                send(
                    own.at[index, high], own.at[index, high], high_sems,
                    (number, row_off - 1, line), device,
                )
            send(own.at[index], other.at[index], core_sems, (0, row_off, line), core)
    for line in range(slow):
        for fast_off in range(1, fast):
            for row_off in range(1, row_count):
                index = block(line, fast_off, row_off)
                spot = (fast_off - 1, row_off - 1, line)
                for number, (rows, sems) in enumerate(((low, low_sems), (high, high_sems))):
                    arrived(own.at[index, rows], sems, spot)
                    send(
                        own.at[index, rows], other.at[index, rows], core_half_sems,
                        (number, *spot), core,
                    )
    for line in range(slow):
        for fast_off in range(fast):
            for row_off in range(row_count):
                index = block(line, fast_off, row_off)
                if fast_off and row_off:
                    spot = (fast_off - 1, row_off - 1, line)
                    for number, rows in enumerate((low, high)):
                        arrived(other.at[index, rows], core_half_sems, (number, *spot))
                else:
                    arrived(other.at[index], core_sems, (fast_off, row_off, line))
    for copy in started:
        copy.wait_send()
    keep.wait()


def gather_everywhere(values, collective_id):
    exp_count, row_count = lax.axis_size("exp"), lax.axis_size("row")
    slow = min(4, exp_count)
    fast = exp_count // slow
    rows, width = values.shape
    blocks = exp_count * row_count
    result = jax.ShapeDtypeStruct((blocks, rows, width), values.dtype)
    own, other = pl.pallas_call(
        gather_kernel,
        out_shape=[result, result],
        in_specs=[ANY_SPEC],
        out_specs=[ANY_SPEC, ANY_SPEC],
        scratch_shapes=[
            pltpu.SemaphoreType.DMA,
            pltpu.SemaphoreType.DMA((2, slow - 1)),
            pltpu.SemaphoreType.DMA((2, fast - 1, slow)),
            pltpu.SemaphoreType.DMA((2, row_count - 1, slow)),
            pltpu.SemaphoreType.DMA((2, fast - 1, row_count - 1, slow)),
            pltpu.SemaphoreType.DMA((2, fast - 1, row_count - 1, slow)),
            pltpu.SemaphoreType.DMA((2, fast, row_count, slow)),
            pltpu.SemaphoreType.DMA((2, 2, fast - 1, row_count - 1, slow)),
        ],
        compiler_params=pltpu.CompilerParams(
            collective_id=collective_id, has_side_effects=True
        ),
        cost_estimate=pl.CostEstimate(
            flops=0, bytes_accessed=4 * blocks * rows * width * 4, transcendentals=0
        ),
    )(values)
    return own.reshape(blocks * rows, width), other.reshape(blocks * rows, width)


def scatter_kernel(*refs, backward):
    if backward:
        gating, upward, gate, up, own_gating, own_upward, shared_gate, shared_up = refs[:8]
        lefts = [gating.at[0], gating.at[1], upward.at[0], upward.at[1]]
        refs = refs[8:]
    else:
        hidden, down, down_other, own_hidden, other_hidden, shared, shared_other = refs[:7]
        lefts = [hidden.at[0], hidden.at[1]]
        refs = refs[7:]
    count = len(lefts)
    (
        result, left_tiles, rights, extra_left, extra_right, part, from_row, from_fast,
        from_fast_late, from_row_late, from_slow,
        left_sems, right_sems, extra_sems, row_sems, fast_sems, fast_late_sems, row_late_sems,
        slow_sems,
    ) = refs
    (slow_at, fast_at, row_at, col_at), (slow, fast, row_count) = positions()
    slow_ids, fast_ids, row_ids, core_ids = peers(False)
    exp_count = slow * fast
    exp_index = lax.axis_index("exp")
    rows, width = result.shape
    half = rows // 2
    low, high = pl.ds(0, half), pl.ds(half, half)
    group = rows * row_count
    group_rows = pl.ds(pl.multiple_of(exp_index * group, group), group)
    own_half = pl.ds(pl.multiple_of(col_at * width, width), width)

    def slow_of(turn):
        return (slow_at + 1 + turn) % slow

    def order(step):
        return slow_of(step // fast) * fast + (fast_at + 1 + step % fast) % fast

    def loads(step, slot):
        first = pl.multiple_of(order(step) * group, group)
        return [
            pltpu.make_async_copy(
                left.at[:, pl.ds(first, group)], left_tiles.at[slot, number],
                left_sems.at[slot, number],
            )
            for number, left in enumerate(lefts)
        ]

    if backward:
        right_pairs = [(array.at[side], rights.at[2 * number + side])
                       for number, array in enumerate((gate, up)) for side in range(2)]
        extra_pairs = [
            (own_gating.at[group_rows], extra_left.at[0]),
            (own_upward.at[group_rows], extra_left.at[1]),
            (shared_gate, extra_right.at[0]),
            (shared_up, extra_right.at[1]),
        ]
        extra_product = matmul_right
    else:
        split = down.shape[1]
        right_pairs = []
        for side in range(2):
            for source, place in ((down, col_at), (down_other, 1 - col_at)):
                spot = pl.ds(pl.multiple_of(place * split, 16), split)
                right_pairs.append((source.at[side, :, own_half], rights.at[side, spot]))
        extra_pairs = [
            (own_hidden.at[:, group_rows], extra_left.at[0]),
            (other_hidden, extra_left.at[1]),
            (shared.at[:, own_half], extra_right.at[0]),
            (shared_other.at[:, own_half], extra_right.at[1]),
        ]
        extra_product = matmul_left
    prepared = [
        pltpu.make_async_copy(source, target, right_sems.at[number])
        for number, (source, target) in enumerate(right_pairs)
    ]
    extras = [
        pltpu.make_async_copy(source, target, extra_sems.at[number])
        for number, (source, target) in enumerate(extra_pairs)
    ]
    for copy in prepared + loads(0, 0) + extras:
        copy.start()
    enter((slow_ids, fast_ids, row_ids))
    for copy in prepared:
        copy.wait()

    def make(step):
        slot = step % 2

        @pl.when(step + 1 < exp_count)
        def _():
            for copy in loads(step + 1, 1 - slot):
                copy.start()

        for copy in loads(step, slot):
            copy.wait()
        index = order(step)
        total = matmul_left(left_tiles[slot, 0], rights[0])
        for number in range(1, count):
            total = total + matmul_left(left_tiles[slot, number], rights[number])
        part[index] = total.astype(jnp.bfloat16).reshape(row_count, rows, width)

        @pl.when(step == exp_count - 1)
        def _():
            for copy in extras:
                copy.wait()
            extra = extra_product(extra_left[0], extra_right[0])
            extra = extra + extra_product(extra_left[1], extra_right[1])
            before = part[index].astype(jnp.float32)
            part[index] = (before + extra.reshape(before.shape)).astype(jnp.bfloat16)

        for number, device in enumerate(row_ids):
            goal = (row_at + number + 1) % row_count
            remote(
                part.at[index, goal, low], from_row.at[number, index], row_sems,
                (number, index), device,
            )
        slow_index = index // fast
        for number, device in enumerate(fast_ids):

            @pl.when(index % fast == (fast_at + number + 1) % fast)
            def _():
                for goal in range(row_count):
                    remote(
                        part.at[index, goal, high], from_fast.at[number, slow_index, goal],
                        fast_sems, (number, slow_index, goal), device,
                    )

    def add_up(index, goal, span, arrivals):
        total = part[index, goal, span].astype(jnp.float32)
        for buffer, sems, spot in arrivals:
            wait_arrived(buffer.at[spot], sems, spot)
            total = total + buffer[spot].astype(jnp.float32)
        return total

    def of_rows(index):
        return [(from_row, row_sems, (number, index)) for number in range(row_count - 1)]

    def of_fasts(slow_index, goal):
        return [
            (from_fast, fast_sems, (number, slow_index, goal)) for number in range(fast - 1)
        ]

    def second(slow_index):
        for number, device in enumerate(fast_ids):
            index = slow_index * fast + (fast_at + number + 1) % fast
            part[index, row_at, low] = add_up(index, row_at, low, of_rows(index)).astype(
                jnp.bfloat16
            )
            remote(
                part.at[index, row_at, low], from_fast_late.at[number, slow_index],
                fast_late_sems, (number, slow_index), device,
            )
        mine = slow_index * fast + fast_at
        for number, device in enumerate(row_ids):
            goal = (row_at + number + 1) % row_count
            part[mine, goal, high] = add_up(
                mine, goal, high, of_fasts(slow_index, goal)
            ).astype(jnp.bfloat16)
            remote(
                part.at[mine, goal, high], from_row_late.at[number, slow_index],
                row_late_sems, (number, slow_index), device,
            )

    def finish(slow_index, span, late):
        mine = slow_index * fast + fast_at
        if late == 0:
            arrivals = of_rows(mine) + [
                (from_fast_late, fast_late_sems, (number, slow_index))
                for number in range(fast - 1)
            ]
        else:
            arrivals = of_fasts(slow_index, row_at) + [
                (from_row_late, row_late_sems, (number, slow_index))
                for number in range(row_count - 1)
            ]
        return add_up(mine, row_at, span, arrivals)

    def third(number):
        slow_index = slow_of(number)
        mine = slow_index * fast + fast_at
        for late, span in enumerate((low, high)):
            part[mine, row_at, span] = finish(slow_index, span, late).astype(jnp.bfloat16)
            remote(
                part.at[mine, row_at, span], from_slow.at[late, number], slow_sems,
                (late, number), slow_ids[number],
            )

    for turn in range(slow + 1):
        if turn < slow:
            pl.loop(turn * fast, turn * fast + fast)(make)
        if turn >= 1:
            second(slow_of(turn - 1))
        if turn >= 2:
            third(turn - 2)
    for late, span in enumerate((low, high)):
        total = finish(slow_at, span, late)
        for number in range(slow - 1):
            wait_arrived(from_slow.at[late, number], slow_sems, (late, number))
            total = total + from_slow[late, number].astype(jnp.float32)
        result[span, :] = total

    def sent(src, sems, index):
        pltpu.make_async_copy(src, src, sems.at[(0, *index)]).wait()

    @pl.loop(0, exp_count)
    def _(index):
        for number in range(row_count - 1):
            sent(from_row.at[number, index], row_sems, (number, index))

    @pl.loop(0, slow)
    def _(slow_index):
        for number in range(fast - 1):
            for goal in range(row_count):
                spot = (number, slow_index, goal)
                sent(from_fast.at[spot], fast_sems, spot)
            sent(from_fast_late.at[number, slow_index], fast_late_sems, (number, slow_index))
        for number in range(row_count - 1):
            sent(from_row_late.at[number, slow_index], row_late_sems, (number, slow_index))

    for number in range(slow - 1):
        for late in range(2):
            sent(from_slow.at[late, number], slow_sems, (late, number))


def scatter_products(operands, backward, collective_id):
    exp_count, row_count = lax.axis_size("exp"), lax.axis_size("row")
    slow = min(4, exp_count)
    fast = exp_count // slow
    _, units, tokens = operands[0].shape
    rows = tokens // exp_count // row_count
    group = rows * row_count
    half = rows // 2
    kind = jnp.bfloat16
    if backward:
        count, (width, shared_units) = 4, operands[6].shape
        extra_shapes = [(2, group, shared_units), (2, width, shared_units)]
    else:
        count, shared_units, width = 2, operands[5].shape[0], operands[1].shape[2] // 2
        extra_shapes = [(2, shared_units, group), (2, shared_units, width)]
    return pl.pallas_call(
        functools.partial(scatter_kernel, backward=backward),
        out_shape=jax.ShapeDtypeStruct((rows, width), jnp.float32),
        in_specs=[ANY_SPEC] * len(operands),
        out_specs=pl.BlockSpec(memory_space=pltpu.VMEM),
        scratch_shapes=[
            pltpu.VMEM((2, count, units, group), kind),
            pltpu.VMEM((count, units, width), kind),
            pltpu.VMEM(extra_shapes[0], kind),
            pltpu.VMEM(extra_shapes[1], kind),
            pltpu.VMEM((exp_count, row_count, rows, width), kind),
            pltpu.VMEM((row_count - 1, exp_count, half, width), kind),
            pltpu.VMEM((fast - 1, slow, row_count, half, width), kind),
            pltpu.VMEM((fast - 1, slow, half, width), kind),
            pltpu.VMEM((row_count - 1, slow, half, width), kind),
            pltpu.VMEM((2, slow - 1, half, width), kind),
            pltpu.SemaphoreType.DMA((2, count)),
            pltpu.SemaphoreType.DMA((4,)),
            pltpu.SemaphoreType.DMA((4,)),
            pltpu.SemaphoreType.DMA((2, row_count - 1, exp_count)),
            pltpu.SemaphoreType.DMA((2, fast - 1, slow, row_count)),
            pltpu.SemaphoreType.DMA((2, fast - 1, slow)),
            pltpu.SemaphoreType.DMA((2, row_count - 1, slow)),
            pltpu.SemaphoreType.DMA((2, 2, slow - 1)),
        ],
        compiler_params=pltpu.CompilerParams(
            collective_id=collective_id, has_side_effects=True, vmem_limit_bytes=VMEM_LIMIT
        ),
        cost_estimate=pl.CostEstimate(
            flops=2 * tokens * units * width * count,
            bytes_accessed=tokens * units * count * 2 + 60 * 1024 * 1024,
            transcendentals=0,
        ),
    )(*operands)


def unit_grads(gating, upward, grad_hidden):
    sigmoid = jax.nn.sigmoid(gating)
    silu = gating * sigmoid
    grad_upward = (grad_hidden * silu).astype(jnp.bfloat16)
    grad_gating = (grad_hidden * upward * sigmoid * (1.0 + gating * (1.0 - sigmoid))).astype(
        jnp.bfloat16
    )
    return silu * upward, grad_gating, grad_upward


def units_kernel(
    mixer_own, mixer_other, grad_own, grad_other, token_weight,
    expert_gate, gate_other, expert_up, up_other, expert_down, down_other,
    shared_gate, shared_gate_other, shared_up, shared_up_other, shared_down, shared_down_other,
    all_mixer_own, all_mixer_other, all_grad_own, all_grad_other,
    expert_hidden, expert_gating, expert_upward, shared_hidden, shared_gating, shared_upward,
    mixer_turned,
    gates, ups, downs, shared_gates, shared_ups, shared_downs, tiles, shared_tiles,
    shared_turned, shared_rows,
    weight_sems, local_sems, send_sems, recv_sems, shared_local, shared_send, shared_recv,
    row_sems,
):
    step = pl.program_id(0)
    steps = pl.num_programs(0)
    col = lax.axis_index("col")
    core = {"col": 1 - col}
    tile, width = mixer_own.shape
    split = expert_down.shape[1]
    shared_split = shared_down.shape[0]
    shared_steps = steps // 2
    halves = [pl.ds(pl.multiple_of(side * width, width), width) for side in (col, 1 - col)]
    targets = [expert_hidden, expert_gating, expert_upward]
    shared_targets = [shared_gating, shared_upward]

    def weight_copies():
        pairs = [
            (expert_gate.at[col], gates.at[0]),
            (gate_other, gates.at[1]),
            (expert_up.at[col], ups.at[0]),
            (up_other, ups.at[1]),
        ]
        own_rows = pl.ds(pl.multiple_of(col * split, 16), split)
        other_rows = pl.ds(pl.multiple_of((1 - col) * split, 16), split)
        shared_own = pl.ds(pl.multiple_of(col * shared_split, 16), shared_split)
        shared_other = pl.ds(pl.multiple_of((1 - col) * shared_split, 16), shared_split)
        for side in range(2):
            pairs += [
                (expert_down.at[col, :, halves[side]], downs.at[side, own_rows]),
                (down_other.at[col, :, halves[side]], downs.at[side, other_rows]),
            ]
        pairs += [
            (shared_gate, shared_gates.at[0]),
            (shared_gate_other, shared_gates.at[1]),
            (shared_up, shared_ups.at[0]),
            (shared_up_other, shared_ups.at[1]),
        ]
        for side in range(2):
            pairs += [
                (shared_down.at[:, halves[side]], shared_downs.at[side, shared_own]),
                (shared_down_other.at[:, halves[side]], shared_downs.at[side, shared_other]),
            ]
        return [
            pltpu.make_async_copy(src, dst, weight_sems.at[number])
            for number, (src, dst) in enumerate(pairs)
        ]

    def row_copies(turn, slot):
        first = pl.multiple_of((col * shared_steps + turn) * tile, tile)
        arrays = (all_mixer_own, all_mixer_other, all_grad_own, all_grad_other)
        return [
            pltpu.make_async_copy(
                array.at[pl.ds(first, tile)], shared_rows.at[slot, number],
                row_sems.at[slot, number],
            )
            for number, array in enumerate(arrays)
        ]

    def results(at, slot):
        columns = pl.ds(pl.multiple_of(at * tile, tile), tile)
        local, far = [], []
        for number, target in enumerate(targets):
            spot = target.at[col, :, columns]
            local.append(
                pltpu.make_async_copy(tiles.at[slot, number], spot, local_sems.at[slot, number])
            )
            far.append(
                pltpu.make_async_remote_copy(
                    src_ref=tiles.at[slot, number],
                    dst_ref=spot,
                    send_sem=send_sems.at[slot, number],
                    recv_sem=recv_sems.at[number, at],
                    device_id=core,
                    device_id_type=MESH,
                )
            )
        return local, far

    def shared_results(turn, slot):
        first = pl.multiple_of((col * shared_steps + turn) * tile, tile)
        span = pl.ds(first, tile)
        own_rows = pl.ds(pl.multiple_of(col * shared_split, 16), shared_split)
        other_rows = pl.ds(pl.multiple_of((1 - col) * shared_split, 16), shared_split)
        pairs = [
            (shared_tiles.at[slot, number], target.at[span], shared_tiles.at[slot, number])
            for number, target in enumerate(shared_targets)
        ]
        pairs.append(
            (
                shared_turned.at[slot, own_rows], shared_hidden.at[:, span],
                shared_turned.at[slot, other_rows],
            )
        )
        local = [
            pltpu.make_async_copy(src, dst, shared_local.at[slot, number])
            for number, (src, dst, _) in enumerate(pairs)
        ]
        far = [
            pltpu.make_async_remote_copy(
                src_ref=src,
                dst_ref=dst,
                send_sem=shared_send.at[slot, number],
                recv_sem=shared_recv.at[number, turn],
                device_id=core,
                device_id_type=MESH,
            )
            for number, (_, dst, src) in enumerate(pairs)
        ]
        return local, far

    def wait_out(pair):
        local, far = pair
        for copy in local:
            copy.wait()
        for copy in far:
            copy.wait_send()

    weights_early = 8

    @pl.when(step == 0)
    def _():
        for copy in weight_copies() + row_copies(0, 0):
            copy.start()
        enter(([core],))
        for copy in weight_copies()[:weights_early]:
            copy.wait()

    slot = step % 2

    @pl.when(step >= 2)
    def _():
        wait_out(results(step - 2, slot))

    mixers = (mixer_own[...], mixer_other[...])
    grads = (grad_own[...], grad_other[...])
    mixer_turned[...] = mixers[0].T

    def both(pair, weights, product):
        return product(pair[0], weights[0]) + product(pair[1], weights[1])

    def turned(weights, pair):
        return matmul_right(weights[0], pair[0]) + matmul_right(weights[1], pair[1])

    scale = token_weight[:1, :]
    hidden, gating, upward = unit_grads(
        turned(gates, mixers), turned(ups, mixers), turned(downs, grads) * scale
    )
    tiles[slot, 0] = (hidden * scale).astype(jnp.bfloat16)
    tiles[slot, 1] = gating
    tiles[slot, 2] = upward
    local, far = results(step, slot)
    for copy in local + far:
        copy.start()

    @pl.when(step == 0)
    def _():
        for copy in weight_copies()[weights_early:]:
            copy.wait()

    @pl.when(step % 2 == 0)
    def _():
        turn = step // 2
        turn_slot = turn % 2

        @pl.when(turn >= 2)
        def _():
            wait_out(shared_results(turn - 2, turn_slot))

        for copy in row_copies(turn, turn_slot):
            copy.wait()

        @pl.when(turn + 1 < shared_steps)
        def _():
            for copy in row_copies(turn + 1, 1 - turn_slot):
                copy.start()

        rows = [shared_rows[turn_slot, number] for number in range(4)]
        hidden, gating, upward = unit_grads(
            both(rows[:2], shared_gates, matmul),
            both(rows[:2], shared_ups, matmul),
            both(rows[2:], shared_downs, matmul_right),
        )
        shared_tiles[turn_slot, 0] = gating
        shared_tiles[turn_slot, 1] = upward
        shared_turned[turn_slot] = hidden.astype(jnp.bfloat16).T
        local, far = shared_results(turn, turn_slot)
        for copy in local + far:
            copy.start()

    @pl.when(step == steps - 1)
    def _():
        for back in range(2):
            at = steps - 1 - back
            wait_out(results(at, at % 2))
            turn = shared_steps - 1 - back
            wait_out(shared_results(turn, turn % 2))

        @pl.loop(0, steps)
        def _(at):
            columns = pl.ds(pl.multiple_of(at * tile, tile), tile)
            for number, target in enumerate(targets):
                spot = target.at[1 - col, :, columns]
                pltpu.make_async_copy(spot, spot, recv_sems.at[number, at]).wait()

        @pl.loop(0, shared_steps)
        def _(turn):
            first = pl.multiple_of(((1 - col) * shared_steps + turn) * tile, tile)
            span = pl.ds(first, tile)
            for number, target in enumerate(shared_targets):
                pltpu.make_async_copy(
                    target.at[span], target.at[span], shared_recv.at[number, turn]
                ).wait()
            spot = shared_hidden.at[:, span]
            pltpu.make_async_copy(spot, spot, shared_recv.at[2, turn]).wait()


def run_units(mixer, grad, token_weight, weights, collective_id):
    tokens, width = mixer[0].shape
    tile = 256
    units = weights[0].shape[1]
    shared_units = weights[6].shape[1]
    rows = pl.BlockSpec((tile, width), lambda step: (step, 0))
    kind = jnp.bfloat16
    pair = jax.ShapeDtypeStruct((2, units, tokens), kind)
    shared = jax.ShapeDtypeStruct((tokens, shared_units), kind)
    half = jax.ShapeDtypeStruct((shared_units // 2, tokens), kind)
    steps = tokens // tile
    return pl.pallas_call(
        units_kernel,
        out_shape=[
            pair, pair, pair, half, shared, shared, jax.ShapeDtypeStruct((width, tokens), kind)
        ],
        grid=(steps,),
        in_specs=[rows] * 4
        + [pl.BlockSpec((8, tile), lambda step: (0, step))]
        + [ANY_SPEC] * (len(weights) + 4),
        out_specs=[ANY_SPEC] * 6 + [pl.BlockSpec((width, tile), lambda step: (0, step))],
        scratch_shapes=[
            pltpu.VMEM((2, units, width), kind),
            pltpu.VMEM((2, units, width), kind),
            pltpu.VMEM((2, units, width), kind),
            pltpu.VMEM((2, width, shared_units), kind),
            pltpu.VMEM((2, width, shared_units), kind),
            pltpu.VMEM((2, shared_units, width), kind),
            pltpu.VMEM((2, 3, units, tile), kind),
            pltpu.VMEM((2, 2, tile, shared_units), kind),
            pltpu.VMEM((2, shared_units, tile), kind),
            pltpu.VMEM((2, 4, tile, width), kind),
            pltpu.SemaphoreType.DMA((16,)),
            pltpu.SemaphoreType.DMA((2, 3)),
            pltpu.SemaphoreType.DMA((2, 3)),
            pltpu.SemaphoreType.DMA((3, steps)),
            pltpu.SemaphoreType.DMA((2, 3)),
            pltpu.SemaphoreType.DMA((2, 3)),
            pltpu.SemaphoreType.DMA((3, steps // 2)),
            pltpu.SemaphoreType.DMA((2, 4)),
        ],
        compiler_params=pltpu.CompilerParams(
            collective_id=collective_id, has_side_effects=True, vmem_limit_bytes=VMEM_LIMIT
        ),
        cost_estimate=pl.CostEstimate(
            flops=2 * tokens * units * width * 2 * 6,
            bytes_accessed=50 * 1024 * 1024,
            transcendentals=2 * tokens * units,
        ),
    )(*mixer, *grad, token_weight, *weights, *mixer, *grad)


def product_kernel(left, right, result):
    product = matmul(left[...].reshape(left.shape[-2:]), right[...])
    result[...] = product.reshape(result.shape)


def product_cost(tokens, left_rows, width, parts):
    return pl.CostEstimate(
        flops=2 * tokens * left_rows * width * parts,
        bytes_accessed=tokens * (left_rows * parts + width) * 2 + left_rows * width * parts * 4,
        transcendentals=0,
    )


def stacked_grads(left, right):
    parts, units, tokens = left.shape
    width = right.shape[1]
    return pl.pallas_call(
        product_kernel,
        out_shape=jax.ShapeDtypeStruct((parts, units, width), jnp.float32),
        grid=(parts,),
        in_specs=[
            pl.BlockSpec((1, units, tokens), lambda part: (part, 0, 0)),
            full_spec(right),
        ],
        out_specs=pl.BlockSpec((1, units, width), lambda part: (part, 0, 0)),
        compiler_params=pltpu.CompilerParams(vmem_limit_bytes=VMEM_LIMIT),
        cost_estimate=product_cost(tokens, units, width, parts),
    )(left, right)


def row_grads(left, right):
    features, tokens = left.shape
    units = right.shape[1]
    block = min(256, features)
    return pl.pallas_call(
        product_kernel,
        out_shape=jax.ShapeDtypeStruct((features, units), jnp.float32),
        grid=(features // block,),
        in_specs=[pl.BlockSpec((block, tokens), lambda step: (step, 0)), full_spec(right)],
        out_specs=pl.BlockSpec((block, units), lambda step: (step, 0)),
        compiler_params=pltpu.CompilerParams(vmem_limit_bytes=VMEM_LIMIT),
        cost_estimate=product_cost(tokens, features, units, 1),
    )(left, right)


def down_kernel(_, left, own, other, result):
    @pl.when(pl.program_id(1) == 0)
    def _():
        result[0] = matmul(left[0], own[...])

    @pl.when(pl.program_id(1) == 1)
    def _():
        result[0] = matmul(left[0], other[...])


def sided_grads(col, left, own, other, halved):
    parts, units, tokens = left.shape
    units = units // 2 if halved else units
    width = own.shape[1]
    whole = pl.BlockSpec((tokens, width), lambda part, side, col: (0, 0))
    return pl.pallas_call(
        down_kernel,
        out_shape=jax.ShapeDtypeStruct((parts, units, 2 * width), jnp.float32),
        grid_spec=pltpu.PrefetchScalarGridSpec(
            num_scalar_prefetch=1,
            grid=(parts, 2),
            in_specs=[
                pl.BlockSpec(
                    (1, units, tokens),
                    lambda part, side, col: (part, col[0] if halved else 0, 0),
                ),
                whole,
                whole,
            ],
            out_specs=pl.BlockSpec(
                (1, units, width), lambda part, side, col: (part, 0, (col[0] + side) % 2)
            ),
        ),
        compiler_params=pltpu.CompilerParams(vmem_limit_bytes=VMEM_LIMIT),
        cost_estimate=product_cost(tokens, units, 2 * width, parts),
    )(col, left, own, other)


def sums_kernel(
    source, result, running, slow_in, fast_in, row_in, core_in,
    slow_sems, fast_sems, row_sems, core_sems,
):
    slow_ids, fast_ids, row_ids, core_ids = peers(True)
    enter((slow_ids, fast_ids, row_ids, core_ids))
    total = source[...]
    stages = (
        (slow_ids, slow_in, slow_sems),
        (fast_ids, fast_in, fast_sems),
        (row_ids, row_in, row_sems),
        (core_ids, core_in, core_sems),
    )
    last = lax.broadcasted_iota(jnp.int32, source.shape, 0) == 2
    for stage, (devices, buffer, sems) in enumerate(stages):
        running[stage] = total
        copies = [
            pltpu.make_async_remote_copy(
                src_ref=running.at[stage],
                dst_ref=buffer.at[number],
                send_sem=sems.at[0, number],
                recv_sem=sems.at[1, number],
                device_id=device,
                device_id_type=MESH,
            )
            for number, device in enumerate(devices)
        ]
        for copy in copies:
            copy.start()
        for number, copy in enumerate(copies):
            copy.wait_recv()
            arrived = buffer[number]
            total = total + (jnp.where(last, arrived, 0.0) if stage == 3 else arrived)
        for copy in copies:
            copy.wait_send()
    result[...] = total


def sum_everywhere(values, collective_id):
    exp_count, row_count = lax.axis_size("exp"), lax.axis_size("row")
    slow = min(4, exp_count)
    fast = exp_count // slow
    counts = (slow - 1, fast - 1, row_count - 1, 1)
    vmem = pl.BlockSpec(memory_space=pltpu.VMEM)
    return pl.pallas_call(
        sums_kernel,
        out_shape=jax.ShapeDtypeStruct(values.shape, values.dtype),
        in_specs=[vmem],
        out_specs=vmem,
        scratch_shapes=[pltpu.VMEM((4, *values.shape), values.dtype)]
        + [pltpu.VMEM((count, *values.shape), values.dtype) for count in counts]
        + [pltpu.SemaphoreType.DMA((2, count)) for count in counts],
        compiler_params=pltpu.CompilerParams(
            collective_id=collective_id, has_side_effects=True
        ),
    )(values)


def local(
    layer_input,
    attention_gain,
    query_weight,
    latent_weight,
    latent_gain,
    keyvalue_weight,
    output_weight,
    feedforward_gain,
    shared_gate,
    shared_up,
    shared_down,
    expert_gate,
    expert_up,
    expert_down,
    sequence_lengths,
    expert_ids,
    expert_weights,
    output_grad,
):
    exp_index, row_index, col_index = (
        lax.axis_index("exp"),
        lax.axis_index("row"),
        lax.axis_index("col"),
    )
    exp_count = lax.axis_size("exp")
    local_tokens, half_width = layer_input.shape
    full_width = 2 * half_width
    per_device = expert_gate.shape[0]
    group_size = local_tokens * lax.axis_size("row")
    tokens = group_size * exp_count
    group_start = exp_index * group_size

    def part_of(array, side, axis):
        width = array.shape[axis] // 2
        return lax.dynamic_slice_in_dim(array, side * width, width, axis)

    def split_exchange(array, axis):
        return part_of(array, col_index, axis), swap_core(part_of(array, 1 - col_index, axis))

    def own_rows(array):
        return lax.dynamic_slice_in_dim(array, group_start, group_size, 0)

    col = col_index.reshape(1)
    top = expert_ids.shape[1]
    tables = jnp.concatenate(
        [
            expert_ids.astype(jnp.float32),
            expert_weights,
            jnp.broadcast_to(
                sequence_lengths.astype(jnp.float32), (group_size, sequence_lengths.shape[1])
            ),
        ],
        axis=1,
    )
    tables = jnp.pad(tables, ((0, 0), (0, 128 - tables.shape[1])))
    latent_turned = latent_weight.T
    gate_turned, up_turned = expert_gate.swapaxes(1, 2), expert_up.swapaxes(1, 2)
    gain_own = jnp.broadcast_to(attention_gain.astype(jnp.float32), (8, half_width))
    rows_own, rows_other, tables_all, query_other, latent_other, gain_other = begin(
        layer_input, tables, query_weight, latent_turned, gain_own, 6
    )
    rows_own = rows_own.reshape(group_size, half_width)
    rows_other = rows_other.reshape(group_size, half_width)
    tables_all = tables_all.reshape(tokens, -1)
    gate_other = swap_core(lax.dynamic_index_in_dim(gate_turned, 1 - col_index, 0, keepdims=False))
    up_other = swap_core(lax.dynamic_index_in_dim(up_turned, 1 - col_index, 0, keepdims=False))
    down_other = swap_core(expert_down)
    shared_gate_other = swap_core(shared_gate)
    shared_up_other = swap_core(shared_up)
    shared_down_other = swap_core(shared_down)
    weights = (
        gain_own, gain_other, query_weight, query_other, latent_turned, latent_other,
        latent_gain.astype(jnp.float32)[None], keyvalue_weight,
    )
    grad_own = lax.all_gather(output_grad, ("exp", "row"), axis=0, tiled=True)

    ids_all = tables_all[:, :top].astype(jnp.int32)
    router_all = tables_all[:, top : 2 * top]
    sequences = sequence_lengths.shape[1]
    lengths_all = tables_all[::group_size, 2 * top : 2 * top + sequences].astype(jnp.int32)

    def tables_of(lengths):
        _, places = jax.vmap(lambda one: sequence_layout(one, group_size))(lengths)
        cosine, sine = rope_tables(places.reshape(-1))
        return jnp.concatenate([cosine, cosine], axis=1), jnp.concatenate([-sine, sine], axis=1)

    own_cosine, own_sine = tables_of(sequence_lengths)
    cosine_all, sine_all = tables_of(lengths_all)

    query, keyvalue, rope_key, own_normed, own_scale = project(
        col, rows_own, rows_other, own_cosine, own_sine, weights, False
    )
    (attended,) = attend(sequence_lengths, query, keyvalue, rope_key)
    gain_two = feedforward_gain.astype(jnp.float32)
    residual = layer_input.astype(jnp.float32)
    hidden_state, normed_two, scale_two, mixer_input = mix(
        attended, output_weight, layer_input, gain_two[None], 7
    )
    scale_two = scale_two[:, :1]
    grad_own, mixer_input = lax.optimization_barrier((grad_own, mixer_input))
    grad_other = swap_core(grad_own)
    mixer = gather_everywhere(mixer_input, 0)
    late_input, mixer = lax.optimization_barrier((layer_input, mixer))
    input_own = lax.all_gather(late_input, ("exp", "row"), axis=0, tiled=True)

    own_expert = exp_index * per_device + col_index
    token_weight = jnp.sum(jnp.where(ids_all == own_expert, router_all, 0.0), axis=1)
    token_weight = jnp.broadcast_to(token_weight[None], (8, tokens))
    (
        both_hidden, both_gating, both_upward, shared_hidden, shared_gating, shared_upward,
        mixer_turned,
    ) = run_units(
        mixer,
        (grad_own, grad_other),
        token_weight,
        (
            gate_turned, gate_other, up_turned, up_other, expert_down, down_other,
            shared_gate, shared_gate_other, shared_up, shared_up_other,
            shared_down, shared_down_other,
        ),
        1,
    )
    mixer_grad = scatter_products(
        (
            both_gating, both_upward, gate_turned, up_turned, shared_gating, shared_upward,
            shared_gate, shared_up,
        ),
        True,
        2,
    )

    upstream = output_grad.astype(jnp.float32)
    grad_norm_two, gain_two_grad = norm_backward(mixer_grad, normed_two, scale_two, gain_two)
    grad_hidden = upstream + grad_norm_two
    stream_own, stream_other = gather_everywhere(grad_hidden.astype(jnp.bfloat16), 3)

    input_own, stream_own = lax.optimization_barrier((input_own, stream_own))
    input_other = swap_core(input_own)
    query_all, keyvalue_all, rope_key_all, attention_turned, compressed_turned = project(
        col, input_own, input_other, cosine_all, sine_all, weights, True
    )
    output_own, output_other = (
        part_of(output_weight, col_index, 1),
        part_of(output_weight, 1 - col_index, 1),
    )
    grad_heads = (
        matmul_right(stream_own, output_own) + matmul_right(stream_other, output_other)
    ).astype(jnp.bfloat16)
    attended_turned, grad_query, grad_keyvalue, grad_rope = attend(
        lengths_all, query_all, keyvalue_all, rope_key_all, cosine_all, sine_all, grad_heads
    )
    grad_query_other = swap_core(grad_query)

    grad_compressed = matmul_right(own_rows(grad_keyvalue), keyvalue_weight)
    scaled_latent = grad_compressed * latent_gain.astype(jnp.float32)
    latent_inner = jnp.mean(scaled_latent * own_normed, axis=1, keepdims=True)
    grad_craw = own_scale * (scaled_latent - own_normed * latent_inner)
    latent_gain_part = jnp.sum(grad_compressed * own_normed, axis=0)
    grad_latent = lax.psum(
        jnp.concatenate([grad_craw, own_rows(grad_rope)], axis=1), ("row", "col")
    ).astype(jnp.bfloat16)
    own_latent = lax.dynamic_slice_in_dim(grad_latent, row_index * local_tokens, local_tokens, 0)
    latent_all = lax.all_gather(own_latent, ("exp", "row"), axis=0, tiled=True)
    own_query = part_of(query_weight, col_index, 1)
    rows_query = matmul_right(own_rows(grad_query), own_query) + swap_core(
        matmul_right(own_rows(grad_query), query_other)
    )
    grad_rows_query = lax.psum_scatter(rows_query, "row", scatter_dimension=0, tiled=True)
    grad_attention_input = grad_rows_query + matmul_right(own_latent, latent_weight)
    inverse_one = lax.rsqrt(
        half_sums(jnp.sum(residual * residual, axis=1)) / full_width + EPSILON
    )[:, None]
    normed_one = residual * inverse_one
    gain_one = attention_gain.astype(jnp.float32)
    grad_norm_one, gain_one_grad = norm_backward(
        grad_attention_input, normed_one, inverse_one, gain_one
    )
    input_grad = grad_hidden + grad_norm_one

    other_hidden = swap_core(
        lax.dynamic_slice_in_dim(shared_hidden, group_start, group_size, 1)
    )
    produced = scatter_products(
        (
            both_hidden, expert_down, down_other, shared_hidden, other_hidden,
            shared_down, shared_down_other,
        ),
        False,
        4,
    )
    layer_result = (hidden_state + produced).astype(jnp.bfloat16)

    expert_gate_grad = stacked_grads(both_gating, mixer[0]).swapaxes(1, 2)
    expert_up_grad = stacked_grads(both_upward, mixer[0]).swapaxes(1, 2)
    expert_down_grad = sided_grads(col, both_hidden, grad_own, grad_other, True)
    shared_gate_grad = row_grads(mixer_turned, shared_gating)
    shared_up_grad = row_grads(mixer_turned, shared_upward)
    shared_down_grad = sided_grads(col, shared_hidden[None], grad_own, grad_other, False)[0]
    output_weight_grad = sided_grads(
        col, attended_turned[None], stream_own, stream_other, False
    )[0]
    keyvalue_weight_grad = matmul(compressed_turned, grad_keyvalue)
    query_weight_grad = sided_grads(
        col, attention_turned[None], grad_query, grad_query_other, False
    )[0]
    latent_weight_grad = matmul(attention_turned, latent_all)
    padded = jnp.pad(latent_gain_part, (0, half_width - latent_gain_part.shape[0]))
    sums = sum_everywhere(
        jnp.pad(jnp.stack([gain_one_grad, gain_two_grad, padded]), ((0, 5), (0, 0))), 5
    )
    return (
        layer_result,
        input_grad,
        sums[0],
        query_weight_grad,
        latent_weight_grad,
        sums[2, : latent_gain_part.shape[0]],
        keyvalue_weight_grad,
        output_weight_grad,
        sums[1],
        shared_gate_grad,
        shared_up_grad,
        shared_down_grad,
        expert_gate_grad,
        expert_up_grad,
        expert_down_grad,
    )


def solution(mesh):
    in_specs = (
        P(("exp", "row"), "col"),
        P("col"),
        P("col", "row"),
        P("col", None),
        P(),
        P(None, ("row", "col")),
        P(("row", "col"), None),
        P("col"),
        P("col", "row"),
        P("col", "row"),
        P(("row", "col"), None),
        P("exp", "col", "row"),
        P("exp", "col", "row"),
        P("exp", ("row", "col"), None),
        P("exp", None),
        P("exp", None),
        P("exp", None),
        P(("exp", "row"), "col"),
    )
    out_specs = (
        P(("exp", "row"), "col"),
        P(("exp", "row"), "col"),
        P("col"),
        P("col", "row"),
        P("col", None),
        P(),
        P(None, ("row", "col")),
        P(("row", "col"), None),
        P("col"),
        P("col", "row"),
        P("col", "row"),
        P(("row", "col"), None),
        P("exp", "col", "row"),
        P("exp", "col", "row"),
        P("exp", ("row", "col"), None),
    )
    return jax.shard_map(local, mesh=mesh, in_specs=in_specs, out_specs=out_specs, check_vma=False)
```

```python
import functools

import jax
import jax.numpy as jnp
from jax import lax
from jax.experimental import pallas as pl
from jax.experimental.pallas import tpu as pltpu
from jax.sharding import PartitionSpec as P

DN = 128
DR = 64
DV = 128
R = 512
TOP = 6


EPSILON = 1e-06
ROPE_BASE = 50000.0
NEGATIVE = -1e30


def matmul(former, latter):
    return jnp.dot(former, latter, preferred_element_type=jnp.float32)


def matmul_left(former, latter):
    return lax.dot_general(
        former, latter, (((0,), (0,)), ((), ())), preferred_element_type=jnp.float32
    )


def matmul_right(former, latter):
    return lax.dot_general(
        former, latter, (((1,), (1,)), ((), ())), preferred_element_type=jnp.float32
    )


def sequence_layout(lengths, group_size):
    seq_ends = jnp.cumsum(lengths)
    token_order = jnp.arange(group_size, dtype=jnp.int32)
    segment = jnp.sum((token_order[:, None] >= seq_ends[None, :]).astype(jnp.int32), axis=1)
    seq_starts = seq_ends - lengths
    own_start = jnp.sum(
        jnp.where(
            segment[:, None] == jnp.arange(lengths.shape[0], dtype=jnp.int32)[None, :],
            seq_starts[None, :],
            0,
        ),
        axis=1,
    )
    return (segment, token_order - own_start)


def rope_tables(places):
    inverse_frequency = ROPE_BASE ** (-(jnp.arange(DR // 2, dtype=jnp.float32) * 2.0 / DR))
    angles = places.astype(jnp.float32)[:, None] * inverse_frequency[None, :]
    return (jnp.cos(angles), jnp.sin(angles))


MESH = pl.DeviceIdType.MESH
VMEM_LIMIT = 60 * 1024 * 1024
LOG2_E = 1.4426950408889634


def full_spec(array):
    zeros = (0,) * array.ndim
    return pl.BlockSpec(array.shape, lambda *_: zeros)


ANY_SPEC = pl.BlockSpec(memory_space=pl.ANY)


def swap_core(values):
    return lax.ppermute(values, "col", [(0, 1), (1, 0)])


def half_sums(values):
    return lax.psum(values, "col")


def norm_backward(gradient, normed, inverse_rms, gain_vector):
    full_width = normed.shape[1] * lax.axis_size("col")
    scaled = gradient * gain_vector
    inner_sum = half_sums(jnp.sum(scaled * normed, axis=1)) / full_width
    return (
        inverse_rms * (scaled - normed * inner_sum[:, None]),
        jnp.sum(gradient * normed, axis=0),
    )


TABLE = dict(ids=0, router=8, first=16, cosine=32, sine=64)


def rotary_tables(table):
    cosine = table[:, TABLE["cosine"] : TABLE["cosine"] + DR // 2]
    sine = table[:, TABLE["sine"] : TABLE["sine"] + DR // 2]
    return jnp.concatenate([cosine, cosine], axis=1), jnp.concatenate([-sine, sine], axis=1)


def first_keys(table):
    return table[:, TABLE["first"] : TABLE["first"] + 1].astype(jnp.int32)


def rotary(values, cosine_both, sine_signed):
    half = values.shape[-1] // 2
    swapped = jnp.concatenate([values[:, half:], values[:, :half]], axis=-1)
    return values * cosine_both + swapped * sine_signed


def project_rows(
    rows_own, rows_other, gain_own, gain_other, query_own, query_other, latent_own, latent_other,
    latent_gain, keyvalue_weight, table, query, keyvalue, rope_key
):
    rows_own = rows_own.astype(jnp.float32)
    rows_other = rows_other.astype(jnp.float32)
    total = jnp.sum(rows_own * rows_own, axis=1, keepdims=True)
    total = total + jnp.sum(rows_other * rows_other, axis=1, keepdims=True)
    scale = lax.rsqrt(total / (2 * rows_own.shape[1]) + EPSILON)
    rows_own = (rows_own * scale * gain_own[:1]).astype(jnp.bfloat16)
    rows_other = (rows_other * scale * gain_other[:1]).astype(jnp.bfloat16)
    queries = matmul(rows_own, query_own[...]) + matmul(rows_other, query_other[...])
    cosine, sine = rotary_tables(table)
    for first in range(0, query.shape[1], DN + DR):
        rope = rotary(queries[:, first + DN : first + DN + DR], cosine, sine)
        query[:, first : first + DN + DR] = jnp.concatenate(
            [queries[:, first : first + DN], rope], axis=1
        ).astype(jnp.bfloat16)
    latent = matmul_right(rows_own, latent_own[...]) + matmul_right(rows_other, latent_other[...])
    raw = latent[:, :R]
    latent_scale = lax.rsqrt(jnp.mean(raw * raw, axis=1, keepdims=True) + EPSILON)
    latent_normed = raw * latent_scale
    compressed = (latent_normed * latent_gain[:1]).astype(jnp.bfloat16)
    keyvalue[...] = matmul(compressed, keyvalue_weight[...]).astype(jnp.bfloat16)
    rope_key[...] = rotary(latent[:, R:], cosine, sine).astype(jnp.bfloat16)
    return rows_own, compressed, latent_normed, latent_scale, scale


def softmax_parts(queries, keys, bias):
    scores = matmul_right(queries, keys) * ((DN + DR) ** (-0.5) * LOG2_E) + bias
    exponent = jnp.exp2(scores - jnp.max(scores, axis=1, keepdims=True))
    return exponent * (1.0 / jnp.sum(exponent, axis=1, keepdims=True))


def mask_bias(first_key):
    size = first_key.shape[0]
    row = lax.broadcasted_iota(jnp.int32, (size, size), 0)
    column = lax.broadcasted_iota(jnp.int32, (size, size), 1)
    return jnp.where((column <= row) & (column >= first_key), 0.0, NEGATIVE)


def head_keys(keyvalue, rope_keys, head):
    first = head * (DN + DV)
    keys = jnp.concatenate([keyvalue[:, first : first + DN], rope_keys], axis=1)
    return keys, keyvalue[:, first + DN : first + DN + DV]


def attend_kernel(table, query, keyvalue, rope_key, attended):
    bias = mask_bias(first_keys(table))
    rope_keys = rope_key[...]
    for head in range(query.shape[1] // (DN + DR)):
        first = head * (DN + DR)
        keys, values = head_keys(keyvalue, rope_keys, head)
        weights = softmax_parts(query[:, first : first + DN + DR], keys, bias)
        attended[:, head * DV : (head + 1) * DV] = matmul(
            weights.astype(jnp.bfloat16), values
        ).astype(jnp.bfloat16)


def attention_body(
    table, query, keyvalue, rope_key, stream_own, stream_other,
    output_own, output_other, attended, grad_query, grad_keyvalue, grad_rope
):
    factor = (DN + DR) ** (-0.5)
    bias = mask_bias(first_keys(table))
    cosine, sine = rotary_tables(table)
    rope_keys = rope_key[...]
    size = query.shape[0]
    grad_heads = matmul_right(stream_own[0], output_own[...]) + matmul_right(
        stream_other[0], output_other[...]
    )
    grad_heads = grad_heads.astype(jnp.bfloat16)
    rope_total = jnp.zeros((size, DR), jnp.float32)
    for head in range(query.shape[1] // (DN + DR)):
        first = head * (DN + DR)
        first_kv = head * (DN + DV)
        queries = query[:, first : first + DN + DR]
        keys, values = head_keys(keyvalue, rope_keys, head)
        probabilities = softmax_parts(queries, keys, bias)
        weights = probabilities.astype(jnp.bfloat16)
        result = matmul(weights, values)
        attended[head * DV : (head + 1) * DV, :] = result.astype(jnp.bfloat16).T
        grad_head = grad_heads[:, head * DV : (head + 1) * DV]
        inner = jnp.sum(result * grad_head.astype(jnp.float32), axis=1, keepdims=True)
        grad_scores = (probabilities * (matmul_right(grad_head, values) - inner)).astype(
            jnp.bfloat16
        )
        grad_queries = matmul(grad_scores, keys) * factor
        grad_keys = matmul_left(grad_scores, queries) * factor
        unrotated = rotary(grad_queries[:, DN:], cosine, -sine)
        grad_query[:, first : first + DN + DR] = jnp.concatenate(
            [grad_queries[:, :DN], unrotated], axis=1
        ).astype(jnp.bfloat16)
        grad_keyvalue[:, first_kv : first_kv + DN] = grad_keys[:, :DN].astype(jnp.bfloat16)
        grad_keyvalue[:, first_kv + DN : first_kv + DN + DV] = matmul_left(
            weights, grad_head
        ).astype(jnp.bfloat16)
        rope_total = rope_total + grad_keys[:, DN:]
    grad_rope[...] = rotary(rope_total, cosine, -sine)


def positions():
    exp_count = lax.axis_size("exp")
    slow = min(4, exp_count)
    fast = exp_count // slow
    row_count = lax.axis_size("row")
    exp_index = lax.axis_index("exp")
    place = (exp_index // fast, exp_index % fast, lax.axis_index("row"), lax.axis_index("col"))
    return place, (slow, fast, row_count)


def peers(with_core):
    (slow_at, fast_at, row_at, col_at), (slow, fast, row_count) = positions()
    slow_ids = [
        {"exp": (slow_at + step) % slow * fast + fast_at} for step in range(1, slow)
    ]
    fast_ids = [
        {"exp": slow_at * fast + (fast_at + step) % fast} for step in range(1, fast)
    ]
    row_ids = [{"row": (row_at + step) % row_count} for step in range(1, row_count)]
    core_ids = [{"col": 1 - col_at}] if with_core else []
    return slow_ids, fast_ids, row_ids, core_ids


def enter(groups):
    barrier = pltpu.get_barrier_semaphore()
    count = 0
    for group in groups:
        for device in group:
            pl.semaphore_signal(barrier, inc=1, device_id=device, device_id_type=MESH)
            count += 1
    pl.semaphore_wait(barrier, count)


def remote(src, dst, sems, index, device):
    copy = pltpu.make_async_remote_copy(
        src_ref=src,
        dst_ref=dst,
        send_sem=sems.at[(0, *index)],
        recv_sem=sems.at[(1, *index)],
        device_id=device,
        device_id_type=MESH,
    )
    copy.start()
    return copy


def wait_arrived(dst, sems, index):
    pltpu.make_async_copy(dst, dst, sems.at[(1, *index)]).wait()


def sent(src, sems, index):
    pltpu.make_async_copy(src, src, sems.at[(0, *index)]).wait()


class Gather:
    def __init__(self, source, own, other, sems, by_core):
        self.source, self.own, self.other = source, own, other
        self.far = own if by_core else other
        self.place, self.sizes = positions()
        self.fast_ids, self.row_ids, core_ids = peers(True)[1:]
        self.core = core_ids[0]
        self.half = source.shape[0] // 2
        (
            self.local, self.up, self.down, self.fast, self.row, self.low, self.high,
            self.core_sems, self.core_half,
        ) = sems

    @staticmethod
    def sems():
        exp_count, row_count = lax.axis_size("exp"), lax.axis_size("row")
        slow = min(4, exp_count)
        fast = exp_count // slow
        corner = (fast - 1, row_count - 1, slow)
        return [pltpu.SemaphoreType.DMA] + [
            pltpu.SemaphoreType.DMA((2, *shape))
            for shape in (
                (slow - 1,), (slow - 1,), (fast - 1, slow), (row_count - 1, slow), corner, corner,
                (fast, row_count, slow), (2, *corner),
            )
        ]

    def index(self, line, fast_off, row_off):
        _, fast_at, row_at, _ = self.place
        _, fast, row_count = self.sizes
        fast_index = (fast_at + fast - fast_off) % fast
        return (line * fast + fast_index) * row_count + (row_at + row_count - row_off) % row_count

    def part(self, ref, number):
        return ref.at[pl.ds(number * self.half, self.half)]

    def keep(self):
        mine = self.index(self.place[0], 0, 0)
        return pltpu.make_async_copy(self.source, self.own(mine), self.local)

    def along(self, up, src, index, number):
        slow_at, fast_at = self.place[:2]
        slow, fast, _ = self.sizes

        @pl.when(slow_at < slow - 1 if up else slow_at > 0)
        def _():
            goal = (slow_at + 1 if up else slow_at - 1) * fast + fast_at
            remote(
                src, self.own(index), self.up if up else self.down, (number,), {"exp": goal}
            )

    def spread(self, src, line):
        index = self.index(line, 0, 0)
        for number, device in enumerate(self.fast_ids):
            remote(src, self.own(index), self.fast, (number, line), device)
        for number, device in enumerate(self.row_ids):
            remote(src, self.own(index), self.row, (number, line), device)
        remote(src, self.far(index), self.core_sems, (0, 0, line), self.core)

    def start(self):
        self.keep().start()
        mine = self.index(self.place[0], 0, 0)
        self.along(True, self.source, mine, 0)
        self.along(False, self.source, mine, 0)
        self.spread(self.source, self.place[0])

    def lines(self, number, act):
        slow_at, slow = self.place[0], self.sizes[0]
        if number == 0:
            act(slow_at, None)
            return

        @pl.when(slow_at >= number)
        def _():
            act(slow_at - number, True)

        @pl.when(slow_at + number < slow)
        def _():
            act(slow_at + number, False)

    def hop(self, number):
        def act(line, up):
            block = self.own(self.index(line, 0, 0))
            wait_arrived(block, self.up if up else self.down, (number - 1,))
            if number < self.sizes[0] - 1:
                self.along(up, block, self.index(line, 0, 0), number)
            self.spread(block, line)

        self.lines(number, act)

    def corner(self, number):
        _, fast, row_count = self.sizes

        def act(line, _):
            for fast_off in range(1, fast):
                index = self.index(line, fast_off, 0)
                block = self.own(index)
                wait_arrived(block, self.fast, (fast_off - 1, line))
                for count, device in enumerate(self.row_ids):
                    low = self.part(block, 0)
                    remote(low, low, self.low, (fast_off - 1, count, line), device)
                remote(block, self.far(index), self.core_sems, (fast_off, 0, line), self.core)
            for row_off in range(1, row_count):
                index = self.index(line, 0, row_off)
                block = self.own(index)
                wait_arrived(block, self.row, (row_off - 1, line))
                for count, device in enumerate(self.fast_ids):
                    high = self.part(block, 1)
                    remote(high, high, self.high, (count, row_off - 1, line), device)
                remote(block, self.far(index), self.core_sems, (0, row_off, line), self.core)

        self.lines(number, act)

    def last(self, number):
        _, fast, row_count = self.sizes

        def act(line, _):
            for fast_off in range(1, fast):
                for row_off in range(1, row_count):
                    index = self.index(line, fast_off, row_off)
                    spot = (fast_off - 1, row_off - 1, line)
                    for count, sems in enumerate((self.low, self.high)):
                        half = self.part(self.own(index), count)
                        wait_arrived(half, sems, spot)
                        remote(
                            half, self.part(self.far(index), count), self.core_half,
                            (count, *spot), self.core,
                        )

        self.lines(number, act)

    def ready(self, line, fast_off):
        row_count = self.sizes[2]

        @pl.when(fast_off == 0)
        def _():
            for row_off in range(row_count):
                block = self.other(self.index(line, 0, row_off))
                wait_arrived(block, self.core_sems, (0, row_off, line))

        @pl.when(fast_off > 0)
        def _():
            block = self.other(self.index(line, fast_off, 0))
            wait_arrived(block, self.core_sems, (fast_off, 0, line))
            for row_off in range(1, row_count):
                block = self.other(self.index(line, fast_off, row_off))
                for count in range(2):
                    spot = (count, fast_off - 1, row_off - 1, line)
                    wait_arrived(self.part(block, count), self.core_half, spot)

    def finish(self, all_ready=False):
        slow_at = self.place[0]
        slow, fast, row_count = self.sizes
        whole = self.own(self.index(slow_at, 0, 0))
        half = self.part(whole, 0)

        @pl.loop(0, slow)
        def _(line):
            for fast_off in range(fast):
                for row_off in range(row_count):
                    block = self.other(self.index(line, fast_off, row_off))
                    if fast_off and row_off:
                        spot = (fast_off - 1, row_off - 1, line)
                        for count in range(2):
                            if not all_ready:
                                wait_arrived(
                                    self.part(block, count), self.core_half, (count, *spot)
                                )
                            sent(half, self.core_half, (count, *spot))
                        sent(half, self.low, spot)
                        sent(half, self.high, spot)
                    else:
                        if not all_ready:
                            wait_arrived(block, self.core_sems, (fast_off, row_off, line))
                        sent(whole, self.core_sems, (fast_off, row_off, line))
            for count in range(fast - 1):
                sent(whole, self.fast, (count, line))
            for count in range(row_count - 1):
                sent(whole, self.row, (count, line))

        for number in range(slow - 1):

            @pl.when((slow_at >= number) & (slow_at < slow - 1))
            def _():
                sent(whole, self.up, (number,))

            @pl.when((slow_at + number < slow) & (slow_at > 0))
            def _():
                sent(whole, self.down, (number,))

        if not all_ready:
            self.keep().wait()

    def steps(self):
        slow = self.sizes[0]
        return (
            [functools.partial(self.hop, number) for number in range(1, slow)]
            + [functools.partial(self.corner, number) for number in range(slow)]
            + [functools.partial(self.last, number) for number in range(slow)]
        )


def prologue_kernel(
    rows, gain, latent_gain, keyvalue_weight, output_weight, table,
    gain_two, tables, query_weight, latent_weight, upstream, rows_source,
    gate, up, down, shared_gate, shared_up, shared_down,
    latent_normed, latent_scale, inverse_one, hidden, normed, inverse, mixer,
    tables_all, grad_all, rows_all, query_far, latent_far, gain_far,
    gate_far, up_far, down_far, shared_gate_far, shared_up_far, shared_down_far,
    rows_own, rows_other, query_own, query_other, latent_own, latent_other, gain_other,
    query, keyvalue, rope_key, attended, scales, given, from_core, rows_out, from_rows,
    squares, squares_in,
    local_sems, row_sems, core_rows, slow_sems, fast_sems, core_sems, mix_core, mix_rows,
    weight_sems, *gather_sems
):
    (slow_at, fast_at, row_at, col_at), (slow, fast, row_count) = positions()
    slow_ids, fast_ids, row_ids, core_ids = peers(True)
    core = core_ids[0]
    count, width = rows.shape
    mine = slow_at * fast + fast_at
    query_width = query_own.shape[1]
    own_heads = pl.ds(pl.multiple_of(col_at * query_width, query_width), query_width)
    given_heads = pl.ds(pl.multiple_of((1 - col_at) * query_width, query_width), query_width)
    gather = Gather(
        upstream, lambda index: grad_all.at[index, col_at],
        lambda index: grad_all.at[index, 1 - col_at], gather_sems[: len(gather_sems) // 2], True,
    )
    loads = [
        pltpu.make_async_copy(query_weight.at[:, own_heads], query_own, local_sems.at[0]),
        pltpu.make_async_copy(latent_weight, latent_own, local_sems.at[1]),
        pltpu.make_async_copy(tables, tables_all.at[mine], local_sems.at[2]),
    ]
    for copy in loads:
        copy.start()
    rows_own[row_at] = rows[...]
    enter((slow_ids, fast_ids, row_ids, core_ids))
    started = [
        remote(rows, rows_own.at[row_at], row_sems, (number,), device)
        for number, device in enumerate(row_ids)
    ]
    started.append(remote(rows, rows_other.at[row_at], core_rows, (0,), core))
    started.append(remote(gain, gain_other, core_sems, (0,), core))
    started.append(remote(query_weight.at[:, given_heads], query_other, core_sems, (1,), core))
    started.append(remote(latent_weight, latent_other, core_sems, (2,), core))
    for number, device in enumerate(slow_ids):
        started.append(remote(tables, tables_all.at[mine], slow_sems, (number,), device))
    for number, device in enumerate(fast_ids):
        started.append(remote(tables, tables_all.at[mine], fast_sems, (number, 0), device))
    gather.start()
    late = Gather(
        rows_source, lambda index: rows_all.at[index, col_at],
        lambda index: rows_all.at[index, 1 - col_at], gather_sems[len(gather_sems) // 2 :], True,
    )
    steps = gather.steps()
    late_steps = [late.start] + late.steps()
    for offset in range(1, row_count):
        index = (row_at + row_count - offset) % row_count
        wait_arrived(rows_own.at[index], row_sems, (offset - 1,))
        started.append(
            remote(rows_own.at[index], rows_other.at[index], core_rows, (offset,), core)
        )
    for offset in range(row_count):
        index = (row_at + row_count - offset) % row_count
        wait_arrived(rows_other.at[index], core_rows, (offset,))
    steps.pop(0)()
    for number, target in enumerate((gain_other, query_other, latent_other)):
        wait_arrived(target, core_sems, (number,))
    exchanged = [
        (gate.at[1 - col_at], gate_far), (up.at[1 - col_at], up_far), (down, down_far),
        (shared_gate, shared_gate_far), (shared_up, shared_up_far), (shared_down, shared_down_far),
    ]
    for number, (source, target) in enumerate(exchanged):
        started.append(remote(source, target, weight_sems, (number,), core))
    for copy in loads:
        copy.wait()
    steps.pop(0)()
    keeps = [
        pltpu.make_async_copy(source, target, local_sems.at[number])
        for number, (source, target) in enumerate(
            ((query_other, query_far), (latent_other, latent_far), (gain_other, gain_far))
        )
    ]
    for copy in keeps:
        copy.start()
    _, _, latent_unit, latent_rms, scale = project_rows(
        rows_own[...].reshape(row_count * count, width),
        rows_other[...].reshape(row_count * count, width),
        gain, gain_other, query_own, query_other, latent_own, latent_other, latent_gain,
        keyvalue_weight, table, query, keyvalue, rope_key,
    )
    latent_normed[...] = latent_unit
    latent_scale[...] = latent_rms
    scales[...] = jnp.broadcast_to(scale, scales.shape)
    inverse_one[...] = scales[pl.ds(pl.multiple_of(row_at * count, count), count), :]
    steps.pop(0)()
    attend_kernel(table, query, keyvalue, rope_key, attended)
    steps.pop(0)()
    for offset in range(1, slow):
        index = (slow_at + slow - offset) % slow * fast + fast_at
        wait_arrived(tables_all.at[index], slow_sems, (offset - 1,))
        for number, device in enumerate(fast_ids):
            started.append(
                remote(
                    tables_all.at[index], tables_all.at[index], fast_sems, (number, offset), device
                )
            )

    own_half = pl.ds(pl.multiple_of(col_at * width, width), width)
    other_half = pl.ds(pl.multiple_of((1 - col_at) * width, width), width)
    given[...] = matmul(attended[...], output_weight[:, other_half]).astype(jnp.bfloat16)
    started.append(remote(given, from_core, mix_core, (0,), core))
    total = matmul(attended[...], output_weight[:, own_half])
    wait_arrived(from_core, mix_core, (0,))
    total = total + from_core[...].astype(jnp.float32)
    rows_out[...] = total.astype(jnp.bfloat16).reshape(rows_out.shape)
    for number, device in enumerate(row_ids):
        goal = (row_at + number + 1) % row_count
        started.append(remote(rows_out.at[goal], from_rows.at[number], mix_rows, (number,), device))
    steps.pop(0)()
    state = rows[...].astype(jnp.float32) + rows_out[row_at].astype(jnp.float32)
    for number in range(row_count - 1):
        wait_arrived(from_rows.at[number], mix_rows, (number,))
        state = state + from_rows[number].astype(jnp.float32)
    hidden[...] = state
    own_squares = jnp.sum(state * state, axis=1, keepdims=True)
    squares[...] = jnp.broadcast_to(own_squares, squares.shape)
    started.append(remote(squares, squares_in, mix_core, (1,), core))
    steps.pop(0)()
    late_steps.pop(0)()
    wait_arrived(squares_in, mix_core, (1,))
    rms = lax.rsqrt((squares[...] + squares_in[...]) / (2 * width) + EPSILON)
    inverse[...] = rms
    unit = state * rms[:, :1]
    normed[...] = unit
    mixer[...] = (unit * gain_two[...]).astype(jnp.bfloat16)
    while steps or late_steps:
        for queue in (steps, late_steps):
            if queue:
                queue.pop(0)()
    for offset in range(slow):
        for number in range(1, fast):
            index = (slow_at + slow - offset) % slow * fast + (fast_at + fast - number) % fast
            wait_arrived(tables_all.at[index], fast_sems, (number - 1, offset))
    gather.finish()
    late.finish()
    for number, (_, target) in enumerate(exchanged):
        wait_arrived(target, weight_sems, (number,))
    for copy in started:
        copy.wait_send()
    for copy in keeps:
        copy.wait()


def prologue(
    rows, gain, latent_gain, keyvalue_weight, output_weight, gain_two, tables,
    query_weight, latent_weight, upstream, others, collective_id
):
    exp_count, row_count = lax.axis_size("exp"), lax.axis_size("row")
    slow = min(4, exp_count)
    fast = exp_count // slow
    count, width = rows.shape
    group = row_count * count
    query_width = query_weight.shape[1] // 2
    keyvalue_width = keyvalue_weight.shape[1]
    latent_width = latent_weight.shape[0]
    low = jnp.bfloat16
    high = jnp.float32
    vmem = pl.BlockSpec(memory_space=pltpu.VMEM)
    wide = jax.ShapeDtypeStruct((count, width), high)
    narrow = jax.ShapeDtypeStruct((count, 128), high)
    dma = pltpu.SemaphoreType.DMA
    return pl.pallas_call(
        prologue_kernel,
        out_shape=[
            jax.ShapeDtypeStruct((group, R), high),
            jax.ShapeDtypeStruct((group, 1), high),
            narrow, wide, wide, narrow,
            jax.ShapeDtypeStruct((count, width), low),
            jax.ShapeDtypeStruct((exp_count, *tables.shape), high),
            jax.ShapeDtypeStruct((exp_count * row_count, 2, count, width), low),
            jax.ShapeDtypeStruct((exp_count * row_count, 2, count, width), low),
            jax.ShapeDtypeStruct((width, query_width), low),
            jax.ShapeDtypeStruct(latent_weight.shape, low),
            jax.ShapeDtypeStruct(gain.shape, high),
            *[
                jax.ShapeDtypeStruct(array.shape[number < 2 :], low)
                for number, array in enumerate(others)
            ],
        ],
        in_specs=[vmem] * 7 + [ANY_SPEC] * 11,
        out_specs=[vmem] * 7 + [ANY_SPEC] * 12,
        scratch_shapes=[
            pltpu.VMEM((row_count, count, width), low),
            pltpu.VMEM((row_count, count, width), low),
            pltpu.VMEM((width, query_width), low),
            pltpu.VMEM((width, query_width), low),
            pltpu.VMEM((latent_width, width), low),
            pltpu.VMEM((latent_width, width), low),
            pltpu.VMEM(gain.shape, high),
            pltpu.VMEM((group, query_width), low),
            pltpu.VMEM((group, keyvalue_width), low),
            pltpu.VMEM((group, DR), low),
            pltpu.VMEM((group, keyvalue_width // 2), low),
            pltpu.VMEM((group, 128), high),
            pltpu.VMEM((group, width), low),
            pltpu.VMEM((group, width), low),
            pltpu.VMEM((row_count, count, width), low),
            pltpu.VMEM((row_count - 1, count, width), low),
            pltpu.VMEM((count, 128), high),
            pltpu.VMEM((count, 128), high),
            dma((3,)),
            dma((2, row_count - 1)),
            dma((2, row_count)),
            dma((2, slow - 1)),
            dma((2, fast - 1, slow)),
            dma((2, 3)),
            dma((2, 2)),
            dma((2, row_count - 1)),
            dma((2, 6)),
            *Gather.sems(),
            *Gather.sems(),
        ],
        compiler_params=pltpu.CompilerParams(
            collective_id=collective_id, has_side_effects=True, vmem_limit_bytes=VMEM_LIMIT
        ),
    )(
        rows, gain, latent_gain, keyvalue_weight, output_weight, tables, gain_two, tables,
        query_weight, latent_weight, upstream, rows, *others,
    )


def pipeline(body, grid, inputs, outputs):
    pltpu.emit_pipeline(
        body,
        grid=grid,
        in_specs=[pl.BlockSpec(block, place) for _, block, place in inputs],
        out_specs=[pl.BlockSpec(block, place) for _, block, place in outputs],
    )(*[ref for ref, _, _ in inputs], *[ref for ref, _, _ in outputs])


def product_body(total, axis, steps):
    def body(left, right, result):
        step = pl.program_id(axis)
        product = matmul(
            left[...].reshape(-1, left.shape[-1]), right[...].reshape(-1, right.shape[-1])
        )
        spot = total.at[pl.ds(0, product.shape[0]), pl.ds(0, product.shape[1])]

        @pl.when(step == 0)
        def _():
            spot[...] = product

        @pl.when((step > 0) & (step < steps - 1))
        def _():
            spot[...] += product

        @pl.when(step == steps - 1)
        def _():
            result[...] = (spot[...] + product).reshape(result.shape).astype(result.dtype)

    return body


DEPTH = 1024


def stacked_job(left, right, result, total):
    parts, units, tokens = left.shape
    width = right.shape[2]
    steps = tokens // DEPTH

    def run():
        pipeline(
            product_body(total, 1, steps),
            (parts, steps),
            [
                (left, (1, units, DEPTH), lambda part, step: (part, 0, step)),
                (right, (1, DEPTH, width), lambda part, step: (0, step, 0)),
            ],
            [(result, (1, units, width), lambda part, step: (part, 0, 0))],
        )

    return run


def row_job(left, right, result, total):
    features, tokens = left.shape
    units = right.shape[1]
    steps = tokens // DEPTH

    def run():
        pipeline(
            product_body(total, 0, steps),
            (steps,),
            [
                (left, (features, DEPTH), lambda step: (0, step)),
                (right, (DEPTH, units), lambda step: (step, 0)),
            ],
            [(result, (features, units), lambda step: (0, 0))],
        )

    return run


def expert_down_job(left, right, result, total):
    parts, units, tokens = left.shape
    _, _, rows, width = right.shape
    steps = tokens // DEPTH
    col = lax.axis_index("col")

    def run():
        pipeline(
            product_body(total, 1, steps),
            (2, steps),
            [
                (left, (parts, units // 2, DEPTH), lambda side, step: (0, col, step)),
                (right, (DEPTH // rows, 1, rows, width), lambda side, step: (step, side, 0, 0)),
            ],
            [(result, (parts, units // 2, width), lambda side, step: (0, 0, side))],
        )

    return run


def shared_down_job(left, right, result, total):
    units, tokens = left.shape
    _, _, rows, width = right.shape
    steps = tokens // DEPTH

    def run():
        pipeline(
            product_body(total, 1, steps),
            (2, steps),
            [
                (left, (units, DEPTH), lambda side, step: (0, step)),
                (right, (DEPTH // rows, 1, rows, width), lambda side, step: (step, side, 0, 0)),
            ],
            [(result, (units, width), lambda side, step: (0, side))],
        )

    return run


def sided_job(left, right, result, total):
    units, tokens = left.shape
    width = right.shape[2]
    steps = tokens // DEPTH
    col = lax.axis_index("col")

    def run():
        pipeline(
            product_body(total, 1, steps),
            (2, steps),
            [
                (left, (units, DEPTH), lambda side, step: (0, step)),
                (right, (1, DEPTH, width), lambda side, step: (side, step, 0)),
            ],
            [(result, (units, width), lambda side, step: (0, (col + side) % 2))],
        )

    return run


def project_body(own, other, *rest):
    rows, width = own.shape[0] * own.shape[2], own.shape[3]
    normed, compressed, _, _, _ = project_rows(
        own[...].reshape(rows, width), other[...].reshape(rows, width), *rest[:-2]
    )
    rest[-2][...] = normed.T
    rest[-1][...] = compressed.T


def project_jobs(values, weights, tables, results, parts):
    blocks, _, rows, width = values.shape
    tile_blocks = 256 // rows
    steps = blocks // tile_blocks // parts
    col = lax.axis_index("col")
    query_width = weights[3].shape[1]

    def job(part):
        def at(step):
            return part * steps + step

        def table(array):
            return (array, (256, array.shape[1]), lambda step: (at(step), 0))

        def whole(array):
            return (array, array.shape, lambda step: (0, 0))

        def run():
            inputs = [
                (values, (tile_blocks, 1, rows, width), lambda step: (at(step), col, 0, 0)),
                (values, (tile_blocks, 1, rows, width), lambda step: (at(step), 1 - col, 0, 0)),
            ]
            weight_inputs = [whole(array) for array in weights]
            weight_inputs[2] = (weights[2], (width, query_width), lambda step: (0, col))
            inputs += weight_inputs + [table(tables)]
            outputs = [table(array) for array in results[:3]]
            outputs += [
                (array, (array.shape[0], 256), lambda step: (0, at(step))) for array in results[3:]
            ]
            pipeline(project_body, (steps,), inputs, outputs)

        return run

    return [job(part) for part in range(parts)]


def attention_jobs(arrays, stream, output_weight, results, groups, parts):
    size = arrays[0].shape[0] // groups
    width = stream.shape[2]
    col = lax.axis_index("col")
    steps = groups // parts

    def job(part):
        def at(step):
            return part * steps + step

        def table(array):
            return (array, (size, array.shape[1]), lambda step: (at(step), 0))

        def run():
            inputs = [table(array) for array in arrays]
            inputs += [
                (stream, (1, size, width), lambda step: (0, at(step), 0)),
                (stream, (1, size, width), lambda step: (1, at(step), 0)),
                (output_weight, (output_weight.shape[0], width), lambda step: (0, col)),
                (output_weight, (output_weight.shape[0], width), lambda step: (0, 1 - col)),
            ]
            outputs = [
                (results[0], (results[0].shape[0], size), lambda step: (0, at(step)))
            ] + [table(array) for array in results[1:]]
            pipeline(attention_body, (steps,), inputs, outputs)

        return run

    return [job(part) for part in range(parts)]


TOTAL = (1024, 1408)


def jobs_kernel(*refs, make_jobs, inputs):
    for job in make_jobs(refs[:inputs], refs[inputs:-1], refs[-1]):
        job()


def run_jobs(make_jobs, operands, shapes):
    return pl.pallas_call(
        functools.partial(jobs_kernel, make_jobs=make_jobs, inputs=len(operands)),
        out_shape=shapes,
        in_specs=[ANY_SPEC] * len(operands),
        out_specs=[ANY_SPEC] * len(shapes),
        scratch_shapes=[pltpu.VMEM(TOTAL, jnp.float32)],
        compiler_params=pltpu.CompilerParams(vmem_limit_bytes=VMEM_LIMIT),
    )(*operands)


def no_jobs(inputs, outputs, total):
    return []


def gather_kernel(*refs, make_jobs, inputs, sems):
    source, job_inputs, target = refs[0], refs[1 : 1 + inputs], refs[1 + inputs]
    total, gather_sems = refs[-sems - 1], refs[-sems:]
    jobs = make_jobs(job_inputs, refs[2 + inputs : -sems - 1], total)
    gather = Gather(
        source, lambda index: target.at[0, index], lambda index: target.at[1, index], gather_sems,
        False,
    )

    def work():
        if jobs:
            jobs.pop(0)()

    enter(peers(True))
    gather.start()
    steps = gather.steps()
    slow = gather.sizes[0]
    for number, step in enumerate(steps):
        if number in (slow - 1, 2 * slow - 1):
            work()
        step()
    while jobs:
        work()
    gather.finish()


def gather_everywhere(values, collective_id, make_jobs=no_jobs, operands=(), shapes=()):
    exp_count, row_count = lax.axis_size("exp"), lax.axis_size("row")
    slow = min(4, exp_count)
    fast = exp_count // slow
    rows, width = values.shape
    blocks = exp_count * row_count
    result = jax.ShapeDtypeStruct((2, blocks, rows, width), values.dtype)
    sems = Gather.sems()
    gathered, *others = pl.pallas_call(
        functools.partial(
            gather_kernel, make_jobs=make_jobs, inputs=len(operands), sems=len(sems)
        ),
        out_shape=[result, *shapes],
        in_specs=[ANY_SPEC] * (1 + len(operands)),
        out_specs=[ANY_SPEC] * (1 + len(shapes)),
        scratch_shapes=[pltpu.VMEM(TOTAL, jnp.float32), *sems],
        compiler_params=pltpu.CompilerParams(
            collective_id=collective_id, has_side_effects=True, vmem_limit_bytes=VMEM_LIMIT
        ),
        cost_estimate=pl.CostEstimate(
            flops=0, bytes_accessed=4 * blocks * rows * width * 4, transcendentals=0
        ),
    )(values, *operands)
    return gathered.reshape(2, blocks * rows, width), others


def scatter_kernel(*refs, backward, make_jobs, inputs, outputs):
    if backward:
        gating, upward, gate, up, own_gating, own_upward, shared_gate, shared_up = refs[:8]
        lefts = [gating.at[0], gating.at[1], upward.at[0], upward.at[1]]
        refs = refs[8:]
    else:
        hidden, down, down_other, own_hidden, other_hidden, shared, shared_other = refs[:7]
        lefts = [hidden.at[0], hidden.at[1]]
        refs = refs[7:]
    count = len(lefts)
    job_inputs, result, job_outputs = (
        refs[:inputs], refs[inputs], refs[inputs + 1 : inputs + 1 + outputs]
    )
    refs = refs[inputs + 1 + outputs :]
    (
        left_tiles, rights, extra_left, extra_right, part, from_row, from_fast,
        from_fast_late, from_row_late, from_slow,
        left_sems, right_sems, extra_sems, row_sems, fast_sems, fast_late_sems, row_late_sems,
        slow_sems, job_sems, job_total,
    ) = refs
    (slow_at, fast_at, row_at, col_at), (slow, fast, row_count) = positions()
    slow_ids, fast_ids, row_ids, core_ids = peers(True)
    jobs = make_jobs(job_inputs, job_outputs, job_total, core_ids[0], job_sems)
    exp_count = slow * fast
    exp_index = lax.axis_index("exp")
    rows, width = result.shape
    half = rows // 2
    low, high = pl.ds(0, half), pl.ds(half, half)
    group = rows * row_count
    group_rows = pl.ds(pl.multiple_of(exp_index * group, group), group)
    own_half = pl.ds(pl.multiple_of(col_at * width, width), width)

    def slow_of(turn):
        return (slow_at + 1 + turn) % slow

    def order(step):
        return slow_of(step // fast) * fast + (fast_at + 1 + step % fast) % fast

    def loads(step, slot):
        first = pl.multiple_of(order(step) * group, group)
        return [
            pltpu.make_async_copy(
                left.at[:, pl.ds(first, group)], left_tiles.at[slot, number],
                left_sems.at[slot, number],
            )
            for number, left in enumerate(lefts)
        ]

    if backward:
        right_pairs = [(array.at[side], rights.at[2 * number + side])
                       for number, array in enumerate((gate, up)) for side in range(2)]
        extra_pairs = [
            (own_gating.at[group_rows], extra_left.at[0]),
            (own_upward.at[group_rows], extra_left.at[1]),
            (shared_gate, extra_right.at[0]),
            (shared_up, extra_right.at[1]),
        ]
        extra_product = matmul_right
    else:
        split = down.shape[1]
        right_pairs = []
        for side in range(2):
            for source, place in ((down, col_at), (down_other, 1 - col_at)):
                spot = pl.ds(pl.multiple_of(place * split, 16), split)
                right_pairs.append((source.at[side, :, own_half], rights.at[side, spot]))
        extra_pairs = [
            (own_hidden.at[:, group_rows], extra_left.at[0]),
            (other_hidden, extra_left.at[1]),
            (shared.at[:, own_half], extra_right.at[0]),
            (shared_other.at[:, own_half], extra_right.at[1]),
        ]
        extra_product = matmul_left
    prepared = [
        pltpu.make_async_copy(source, target, right_sems.at[number])
        for number, (source, target) in enumerate(right_pairs)
    ]
    extras = [
        pltpu.make_async_copy(source, target, extra_sems.at[number])
        for number, (source, target) in enumerate(extra_pairs)
    ]
    for copy in prepared + loads(0, 0) + extras:
        copy.start()
    enter((slow_ids, fast_ids, row_ids, core_ids))
    for copy in prepared:
        copy.wait()

    def make(step):
        slot = step % 2

        @pl.when(step + 1 < exp_count)
        def _():
            for copy in loads(step + 1, 1 - slot):
                copy.start()

        for copy in loads(step, slot):
            copy.wait()
        index = order(step)
        total = matmul_left(left_tiles[slot, 0], rights[0])
        for number in range(1, count):
            total = total + matmul_left(left_tiles[slot, number], rights[number])
        part[index] = total.astype(jnp.bfloat16).reshape(row_count, rows, width)

        @pl.when(step == exp_count - 1)
        def _():
            for copy in extras:
                copy.wait()
            extra = extra_product(extra_left[0], extra_right[0])
            extra = extra + extra_product(extra_left[1], extra_right[1])
            before = part[index].astype(jnp.float32)
            part[index] = (before + extra.reshape(before.shape)).astype(jnp.bfloat16)

        for number, device in enumerate(row_ids):
            goal = (row_at + number + 1) % row_count
            remote(
                part.at[index, goal, low], from_row.at[number, index], row_sems,
                (number, index), device,
            )
        slow_index = index // fast
        for number, device in enumerate(fast_ids):

            @pl.when(index % fast == (fast_at + number + 1) % fast)
            def _():
                for goal in range(row_count):
                    remote(
                        part.at[index, goal, high], from_fast.at[number, slow_index, goal],
                        fast_sems, (number, slow_index, goal), device,
                    )

    def add_up(index, goal, span, arrivals):
        total = part[index, goal, span].astype(jnp.float32)
        for buffer, sems, spot in arrivals:
            wait_arrived(buffer.at[spot], sems, spot)
            total = total + buffer[spot].astype(jnp.float32)
        return total

    def of_rows(index):
        return [(from_row, row_sems, (number, index)) for number in range(row_count - 1)]

    def of_fasts(slow_index, goal):
        return [
            (from_fast, fast_sems, (number, slow_index, goal)) for number in range(fast - 1)
        ]

    def second(slow_index):
        for number, device in enumerate(fast_ids):
            index = slow_index * fast + (fast_at + number + 1) % fast
            part[index, row_at, low] = add_up(index, row_at, low, of_rows(index)).astype(
                jnp.bfloat16
            )
            remote(
                part.at[index, row_at, low], from_fast_late.at[number, slow_index],
                fast_late_sems, (number, slow_index), device,
            )
        mine = slow_index * fast + fast_at
        for number, device in enumerate(row_ids):
            goal = (row_at + number + 1) % row_count
            part[mine, goal, high] = add_up(
                mine, goal, high, of_fasts(slow_index, goal)
            ).astype(jnp.bfloat16)
            remote(
                part.at[mine, goal, high], from_row_late.at[number, slow_index],
                row_late_sems, (number, slow_index), device,
            )

    def finish(slow_index, span, late):
        mine = slow_index * fast + fast_at
        if late == 0:
            arrivals = of_rows(mine) + [
                (from_fast_late, fast_late_sems, (number, slow_index))
                for number in range(fast - 1)
            ]
        else:
            arrivals = of_fasts(slow_index, row_at) + [
                (from_row_late, row_late_sems, (number, slow_index))
                for number in range(row_count - 1)
            ]
        return add_up(mine, row_at, span, arrivals)

    def third(number):
        slow_index = slow_of(number)
        mine = slow_index * fast + fast_at
        for late, span in enumerate((low, high)):
            part[mine, row_at, span] = finish(slow_index, span, late).astype(jnp.bfloat16)
            remote(
                part.at[mine, row_at, span], from_slow.at[late, number], slow_sems,
                (late, number), slow_ids[number],
            )

    for turn in range(slow + 1):
        if turn < slow:
            pl.loop(turn * fast, turn * fast + fast)(make)
        if turn >= 1:
            second(slow_of(turn - 1))
        if turn >= 2:
            third(turn - 2)
        if jobs:
            jobs.pop(0)()
    for job in jobs:
        job()
    for late, span in enumerate((low, high)):
        total = finish(slow_at, span, late)
        for number in range(slow - 1):
            wait_arrived(from_slow.at[late, number], slow_sems, (late, number))
            total = total + from_slow[late, number].astype(jnp.float32)
        result[span, :] = total

    @pl.loop(0, exp_count)
    def _(index):
        for number in range(row_count - 1):
            sent(from_row.at[number, index], row_sems, (number, index))

    @pl.loop(0, slow)
    def _(slow_index):
        for number in range(fast - 1):
            for goal in range(row_count):
                spot = (number, slow_index, goal)
                sent(from_fast.at[spot], fast_sems, spot)
            sent(from_fast_late.at[number, slow_index], fast_late_sems, (number, slow_index))
        for number in range(row_count - 1):
            sent(from_row_late.at[number, slow_index], row_late_sems, (number, slow_index))

    for number in range(slow - 1):
        for late in range(2):
            sent(from_slow.at[late, number], slow_sems, (late, number))


def no_scatter_jobs(inputs, outputs, total, core, sems):
    return []


def scatter_products(
    operands, backward, collective_id, make_jobs=no_scatter_jobs, job_operands=(), shapes=()
):
    exp_count, row_count = lax.axis_size("exp"), lax.axis_size("row")
    slow = min(4, exp_count)
    fast = exp_count // slow
    _, units, tokens = operands[0].shape
    rows = tokens // exp_count // row_count
    group = rows * row_count
    half = rows // 2
    kind = jnp.bfloat16
    if backward:
        count, (width, shared_units) = 4, operands[6].shape
        extra_shapes = [(2, group, shared_units), (2, width, shared_units)]
    else:
        count, shared_units, width = 2, operands[5].shape[0], operands[1].shape[2] // 2
        extra_shapes = [(2, shared_units, group), (2, shared_units, width)]
    return pl.pallas_call(
        functools.partial(
            scatter_kernel, backward=backward, make_jobs=make_jobs, inputs=len(job_operands),
            outputs=len(shapes),
        ),
        out_shape=[jax.ShapeDtypeStruct((rows, width), jnp.float32), *shapes],
        in_specs=[ANY_SPEC] * (len(operands) + len(job_operands)),
        out_specs=[pl.BlockSpec(memory_space=pltpu.VMEM)] + [ANY_SPEC] * len(shapes),
        scratch_shapes=[
            pltpu.VMEM((2, count, units, group), kind),
            pltpu.VMEM((count, units, width), kind),
            pltpu.VMEM(extra_shapes[0], kind),
            pltpu.VMEM(extra_shapes[1], kind),
            pltpu.VMEM((exp_count, row_count, rows, width), kind),
            pltpu.VMEM((row_count - 1, exp_count, half, width), kind),
            pltpu.VMEM((fast - 1, slow, row_count, half, width), kind),
            pltpu.VMEM((fast - 1, slow, half, width), kind),
            pltpu.VMEM((row_count - 1, slow, half, width), kind),
            pltpu.VMEM((2, slow - 1, half, width), kind),
            pltpu.SemaphoreType.DMA((2, count)),
            pltpu.SemaphoreType.DMA((4,)),
            pltpu.SemaphoreType.DMA((4,)),
            pltpu.SemaphoreType.DMA((2, row_count - 1, exp_count)),
            pltpu.SemaphoreType.DMA((2, fast - 1, slow, row_count)),
            pltpu.SemaphoreType.DMA((2, fast - 1, slow)),
            pltpu.SemaphoreType.DMA((2, row_count - 1, slow)),
            pltpu.SemaphoreType.DMA((2, 2, slow - 1)),
            pltpu.SemaphoreType.DMA((2, 1)),
            pltpu.VMEM(TOTAL if make_jobs is not no_scatter_jobs else (8, 128), jnp.float32),
        ],
        compiler_params=pltpu.CompilerParams(
            collective_id=collective_id, has_side_effects=True, vmem_limit_bytes=VMEM_LIMIT
        ),
        cost_estimate=pl.CostEstimate(
            flops=2 * tokens * units * width * count,
            bytes_accessed=tokens * units * count * 2 + 60 * 1024 * 1024,
            transcendentals=0,
        ),
    )(*operands, *job_operands)


def unit_grads(gating, upward, grad_hidden):
    bend = 0.5 * jnp.tanh(0.5 * gating)
    sigmoid = 0.5 + bend
    silu = gating * sigmoid
    grad_upward = (grad_hidden * silu).astype(jnp.bfloat16)
    grad_gating = (grad_hidden * upward * (sigmoid + silu * (0.5 - bend))).astype(jnp.bfloat16)
    return silu * upward, grad_gating, grad_upward


def units_kernel(
    mixer_rows, tables, all_grad,
    expert_gate, gate_other, expert_up, up_other, expert_down, down_other,
    shared_gate, shared_gate_other, shared_up, shared_up_other, shared_down, shared_down_other,
    all_mixer,
    expert_hidden, expert_gating, expert_upward, shared_hidden, shared_gating, shared_upward,
    mixer_turned,
    gates, ups, downs, shared_gates, shared_ups, shared_downs, inputs, table, tiles, turned_tiles,
    shared_tiles, shared_turned,
    weight_sems, input_sems, local_sems, send_sems, recv_sems, shared_local, shared_send,
    shared_recv, *gather_sems
):
    step = pl.program_id(0)
    steps = pl.num_programs(0)
    (slow_at, fast_at, _, col), (slow, fast, row_count) = positions()
    core = {"col": 1 - col}
    rows, width = mixer_rows.shape
    tile = rows * row_count
    part = tile // 2
    split = expert_down.shape[1]
    shared_split = shared_down.shape[0]
    shared_steps = steps // 2
    halves = [pl.ds(pl.multiple_of(side * width, width), width) for side in (col, 1 - col)]
    targets = [expert_hidden, expert_gating, expert_upward]
    shared_targets = [shared_gating, shared_upward]
    gather = Gather(
        mixer_rows, lambda index: all_mixer.at[0, index], lambda index: all_mixer.at[1, index],
        gather_sems, False,
    )

    def line_of(at):
        place = at % slow
        near = [
            sorted(range(slow), key=lambda line, own=own: (abs(line - own), line))
            for own in range(slow)
        ]
        line = jnp.int32(0)
        for own in range(slow):
            for number in range(slow):
                line = line + jnp.where(
                    (slow_at == own) & (place == number), near[own][number], 0
                ).astype(jnp.int32)
        return line

    def group_of(at):
        fast_off = at // slow
        return line_of(at) * fast + (fast_at + fast - fast_off) % fast

    def weight_copies():
        pairs = [
            (expert_gate.at[col], gates.at[0]),
            (gate_other, gates.at[1]),
            (expert_up.at[col], ups.at[0]),
            (up_other, ups.at[1]),
        ]
        own_rows = pl.ds(pl.multiple_of(col * split, 16), split)
        other_rows = pl.ds(pl.multiple_of((1 - col) * split, 16), split)
        shared_own = pl.ds(pl.multiple_of(col * shared_split, 16), shared_split)
        shared_other = pl.ds(pl.multiple_of((1 - col) * shared_split, 16), shared_split)
        for side in range(2):
            pairs += [
                (expert_down.at[col, :, halves[side]], downs.at[side, own_rows]),
                (down_other.at[col, :, halves[side]], downs.at[side, other_rows]),
            ]
        pairs += [
            (shared_gate, shared_gates.at[0]),
            (shared_gate_other, shared_gates.at[1]),
            (shared_up, shared_ups.at[0]),
            (shared_up_other, shared_ups.at[1]),
        ]
        for side in range(2):
            pairs += [
                (shared_down.at[:, halves[side]], shared_downs.at[side, shared_own]),
                (shared_down_other.at[:, halves[side]], shared_downs.at[side, shared_other]),
            ]
        return [
            pltpu.make_async_copy(src, dst, weight_sems.at[number])
            for number, (src, dst) in enumerate(pairs)
        ]

    def known_copies(at):
        group = group_of(at)
        slot = at % 3
        blocks = pl.ds(group * row_count, row_count)
        span = pl.ds(pl.multiple_of(group * tile, tile), tile)
        return [
            pltpu.make_async_copy(
                all_grad.at[blocks, side], inputs.at[slot, 2 + number],
                input_sems.at[slot, 2 + number],
            )
            for number, side in enumerate((col, 1 - col))
        ] + [pltpu.make_async_copy(tables.at[span], table.at[slot], input_sems.at[slot, 4])]

    def mixer_copies(at):
        slot = at % 3
        blocks = pl.ds(group_of(at) * row_count, row_count)
        return [
            pltpu.make_async_copy(
                all_mixer.at[side, blocks], inputs.at[slot, side], input_sems.at[slot, side]
            )
            for side in range(2)
        ]

    def results(at, slot):
        columns = pl.ds(pl.multiple_of(group_of(at) * tile, tile), tile)
        local, far = [], []
        for number, target in enumerate(targets):
            spot = target.at[col, :, columns]
            local.append(
                pltpu.make_async_copy(tiles.at[slot, number], spot, local_sems.at[slot, number])
            )
            far.append(
                pltpu.make_async_remote_copy(
                    src_ref=tiles.at[slot, number],
                    dst_ref=spot,
                    send_sem=send_sems.at[slot, number],
                    recv_sem=recv_sems.at[number, at],
                    device_id=core,
                    device_id_type=MESH,
                )
            )
        local.append(
            pltpu.make_async_copy(
                turned_tiles.at[slot], mixer_turned.at[:, columns], local_sems.at[slot, 3]
            )
        )
        return local, far

    def shared_span(turn, member, side):
        first = group_of(2 * turn + member) * tile + side * part
        return pl.ds(pl.multiple_of(first, part), part)

    def shared_results(turn, slot):
        own_rows = pl.ds(pl.multiple_of(col * shared_split, 16), shared_split)
        other_rows = pl.ds(pl.multiple_of((1 - col) * shared_split, 16), shared_split)
        local, far = [], []
        for member in range(2):
            span = shared_span(turn, member, col)
            here = pl.ds(member * part, part)
            triples = [
                (shared_tiles.at[slot, number, here], target.at[span],
                 shared_tiles.at[slot, number, here])
                for number, target in enumerate(shared_targets)
            ]
            triples.append(
                (shared_turned.at[slot, own_rows, here], shared_hidden.at[:, span],
                 shared_turned.at[slot, other_rows, here])
            )
            for number, (near, goal, away) in enumerate(triples):
                local.append(
                    pltpu.make_async_copy(near, goal, shared_local.at[slot, member, number])
                )
                far.append(
                    pltpu.make_async_remote_copy(
                        src_ref=away,
                        dst_ref=goal,
                        send_sem=shared_send.at[slot, member, number],
                        recv_sem=shared_recv.at[number, member, turn],
                        device_id=core,
                        device_id_type=MESH,
                    )
                )
        return local, far

    def wait_out(pair):
        local, far = pair
        for copy in local:
            copy.wait()
        for copy in far:
            copy.wait_send()

    def fetch(at):
        gather.ready(line_of(at), at // slow)
        for copy in mixer_copies(at):
            copy.start()

    weights_early = 8

    @pl.when(step == 0)
    def _():
        for copy in weight_copies()[:weights_early] + known_copies(0):
            copy.start()
        enter(peers(True))
        gather.start()
        for copy in weight_copies()[weights_early:]:
            copy.start()
        gather.corner(0)
        gather.hop(1)
        gather.keep().wait()
        fetch(0)
        for copy in weight_copies()[:weights_early]:
            copy.wait()

    slot = step % 2

    @pl.when(step + 1 < steps)
    def _():
        for copy in known_copies(step + 1):
            copy.start()

    @pl.when(step >= 2)
    def _():
        wait_out(results(step - 2, slot))

    for copy in known_copies(step) + mixer_copies(step):
        copy.wait()

    def block(at, number):
        return inputs[at % 3, number].reshape(tile, width)

    mixers = (block(step, 0), block(step, 1))
    grads = (block(step, 2), block(step, 3))
    turned_tiles[slot] = mixers[0].T

    def both(pair, weights, product):
        return product(pair[0], weights[0]) + product(pair[1], weights[1])

    def turned(weights, pair):
        return matmul_right(weights[0], pair[0]) + matmul_right(weights[1], pair[1])

    columns = table[step % 3].T
    own_expert = (lax.axis_index("exp") * expert_down.shape[0] + col).astype(jnp.float32)
    chosen = columns[TABLE["ids"] : TABLE["ids"] + TOP]
    router = columns[TABLE["router"] : TABLE["router"] + TOP]
    scale = jnp.sum(jnp.where(chosen == own_expert, router, 0.0), axis=0, keepdims=True)
    hidden, gating, upward = unit_grads(
        turned(gates, mixers), turned(ups, mixers), turned(downs, grads) * scale
    )
    tiles[slot, 0] = (hidden * scale).astype(jnp.bfloat16)
    tiles[slot, 1] = gating
    tiles[slot, 2] = upward
    local, far = results(step, slot)
    for copy in local + far:
        copy.start()

    @pl.when(step == 0)
    def _():
        gather.hop(2)
        gather.corner(1)
        for copy in weight_copies()[weights_early:]:
            copy.wait()

    @pl.when(step == 1)
    def _():
        gather.hop(3)
        gather.corner(2)

    @pl.when(step == 2)
    def _():
        gather.corner(3)
        gather.last(0)

    for number in range(1, slow):

        @pl.when(step == number + 2)
        def _():
            gather.last(number)

    @pl.when(step + 1 < steps)
    def _():
        fetch(step + 1)

    @pl.when(step % 2 == 1)
    def _():
        turn = step // 2
        turn_slot = turn % 2

        @pl.when(turn >= 2)
        def _():
            wait_out(shared_results(turn - 2, turn_slot))

        first = col * (row_count // 2)

        def pick(number):
            wanted = pl.ds(first, row_count // 2)
            return jnp.concatenate(
                [
                    inputs[at % 3, number, wanted].reshape(part, width)
                    for at in (step - 1, step)
                ],
                axis=0,
            )

        chosen_rows = [pick(number) for number in range(4)]
        hidden, gating, upward = unit_grads(
            both(chosen_rows[:2], shared_gates, matmul),
            both(chosen_rows[:2], shared_ups, matmul),
            both(chosen_rows[2:], shared_downs, matmul_right),
        )
        shared_tiles[turn_slot, 0] = gating
        shared_tiles[turn_slot, 1] = upward
        shared_turned[turn_slot] = hidden.astype(jnp.bfloat16).T
        local, far = shared_results(turn, turn_slot)
        for copy in local + far:
            copy.start()

    @pl.when(step == steps - 1)
    def _():
        for back in range(2):
            at = steps - 1 - back
            wait_out(results(at, at % 2))
            turn = shared_steps - 1 - back
            wait_out(shared_results(turn, turn % 2))

        @pl.loop(0, steps)
        def _(at):
            columns = pl.ds(pl.multiple_of(group_of(at) * tile, tile), tile)
            for number, target in enumerate(targets):
                spot = target.at[1 - col, :, columns]
                pltpu.make_async_copy(spot, spot, recv_sems.at[number, at]).wait()

        @pl.loop(0, shared_steps)
        def _(turn):
            for member in range(2):
                span = shared_span(turn, member, 1 - col)
                spots = [target.at[span] for target in shared_targets]
                spots.append(shared_hidden.at[:, span])
                for number, spot in enumerate(spots):
                    pltpu.make_async_copy(
                        spot, spot, shared_recv.at[number, member, turn]
                    ).wait()

        gather.finish(True)


def run_units(mixer_rows, tables, grad, weights, collective_id):
    rows, width = mixer_rows.shape
    exp_count, row_count = lax.axis_size("exp"), lax.axis_size("row")
    tokens = tables.shape[0]
    tile = rows * row_count
    units = weights[0].shape[1]
    shared_units = weights[6].shape[1]
    kind = jnp.bfloat16
    pair = jax.ShapeDtypeStruct((2, units, tokens), kind)
    shared = jax.ShapeDtypeStruct((tokens, shared_units), kind)
    half = jax.ShapeDtypeStruct((shared_units // 2, tokens), kind)
    steps = exp_count
    dma = pltpu.SemaphoreType.DMA
    mixer, *others = pl.pallas_call(
        units_kernel,
        out_shape=[
            jax.ShapeDtypeStruct((2, exp_count * row_count, rows, width), kind),
            pair, pair, pair, half, shared, shared, jax.ShapeDtypeStruct((width, tokens), kind),
        ],
        grid=(steps,),
        in_specs=[ANY_SPEC] * (len(weights) + 3),
        out_specs=[ANY_SPEC] * 8,
        scratch_shapes=[
            pltpu.VMEM((2, units, width), kind),
            pltpu.VMEM((2, units, width), kind),
            pltpu.VMEM((2, units, width), kind),
            pltpu.VMEM((2, width, shared_units), kind),
            pltpu.VMEM((2, width, shared_units), kind),
            pltpu.VMEM((2, shared_units, width), kind),
            pltpu.VMEM((3, 4, row_count, rows, width), kind),
            pltpu.VMEM((3, tile, 128), jnp.float32),
            pltpu.VMEM((2, 3, units, tile), kind),
            pltpu.VMEM((2, width, tile), kind),
            pltpu.VMEM((2, 2, tile, shared_units), kind),
            pltpu.VMEM((2, shared_units, tile), kind),
            dma((16,)),
            dma((3, 5)),
            dma((2, 4)),
            dma((2, 3)),
            dma((3, steps)),
            dma((2, 2, 3)),
            dma((2, 2, 3)),
            dma((3, 2, steps // 2)),
            *Gather.sems(),
        ],
        compiler_params=pltpu.CompilerParams(
            collective_id=collective_id, has_side_effects=True, vmem_limit_bytes=VMEM_LIMIT
        ),
        cost_estimate=pl.CostEstimate(
            flops=2 * tokens * units * width * 2 * 6,
            bytes_accessed=50 * 1024 * 1024,
            transcendentals=2 * tokens * units,
        ),
    )(mixer_rows, tables, grad, *weights)
    return mixer.reshape(2, tokens, width), *others


def tail_kernel(
    rows, inverse_one, gain, grad_hidden, sums_in, latent_normed, latent_scale, latent_gain,
    keyvalue_weight, query_other, latent_weight,
    grad_query, grad_keyvalue, grad_rope, query_weight,
    attended_turned, stream, attention_turned, compressed_turned,
    input_grad, sums, latent_all, output_weight_grad, keyvalue_weight_grad, query_weight_grad,
    queries, keyvalues, ropes, query_own, latent_out, latent_in, latent_row_in, wide_out, wide_in,
    wide_rows, wide_row_in, latent_block, squares, squares_in,
    running, slow_in, fast_in, row_in, core_in,
    total_scratch,
    local_sems, core_sems, row_sems, slow_sums, fast_sums, row_sums, core_sums, *gather_sems,
    fused
):
    (slow_at, fast_at, row_at, col_at), (slow, fast, row_count) = positions()
    slow_ids, fast_ids, row_ids, core_ids = peers(True)
    core = core_ids[0]
    count, width = rows.shape
    group = row_count * count
    group_rows = pl.ds(pl.multiple_of(lax.axis_index("exp") * group, group), group)
    query_width = query_own.shape[1]
    jobs = []
    if fused:
        jobs = weight_jobs(
            (
                attended_turned, stream, attention_turned, compressed_turned, grad_query,
                grad_keyvalue,
            ),
            (output_weight_grad, keyvalue_weight_grad, query_weight_grad),
            total_scratch,
        )

    def work():
        if jobs:
            jobs.pop(0)()

    own_heads = pl.ds(pl.multiple_of(col_at * query_width, query_width), query_width)
    loads = [
        pltpu.make_async_copy(source, target, local_sems.at[number])
        for number, (source, target) in enumerate(
            (
                (grad_keyvalue.at[group_rows], keyvalues),
                (grad_rope.at[group_rows], ropes),
                (grad_query.at[0, group_rows], queries),
                (query_weight.at[:, own_heads], query_own),
            )
        )
    ]
    for copy in loads:
        copy.start()
    enter((slow_ids, fast_ids, row_ids, core_ids))
    for copy in loads:
        copy.wait()
    compressed = matmul_right(keyvalues[...], keyvalue_weight[...])
    unit = latent_normed[...]
    scaled = compressed * latent_gain[:1]
    inner = jnp.mean(scaled * unit, axis=1, keepdims=True)
    raw = latent_scale[...] * (scaled - unit * inner)
    latent_out[0] = jnp.concatenate([raw, ropes[...]], axis=1).astype(jnp.bfloat16)
    started = [remote(latent_out.at[0], latent_in, core_sems, (0,), core)]
    wide_out[...] = matmul_right(queries[...], query_other[...]).astype(jnp.bfloat16)
    started.append(remote(wide_out, wide_in, core_sems, (1,), core))
    latent_gain_part = jnp.sum(compressed * unit, axis=0, keepdims=True)
    own_wide = matmul_right(queries[...], query_own[...])
    wait_arrived(latent_in, core_sems, (0,))
    latent_out[1] = (
        latent_out[0].astype(jnp.float32) + latent_in[...].astype(jnp.float32)
    ).astype(jnp.bfloat16)
    for number, device in enumerate(row_ids):
        started.append(
            remote(latent_out.at[1], latent_row_in.at[number], row_sems, (0, number), device)
        )
    wait_arrived(wide_in, core_sems, (1,))
    own_wide = own_wide + wide_in[...].astype(jnp.float32)
    wide_rows[...] = own_wide.astype(jnp.bfloat16).reshape(wide_rows.shape)
    for number, device in enumerate(row_ids):
        goal = (row_at + number + 1) % row_count
        started.append(
            remote(wide_rows.at[goal], wide_row_in.at[number], row_sems, (1, number), device)
        )
    work()
    latent = latent_out[1].astype(jnp.float32)
    for number in range(row_count - 1):
        wait_arrived(latent_row_in.at[number], row_sems, (0, number))
        latent = latent + latent_row_in[number].astype(jnp.float32)
    latent_out[2] = latent.astype(jnp.bfloat16)
    part = count // 2
    first = pl.multiple_of(row_at * count, count)
    latent_block[...] = latent_out[2, pl.ds(pl.multiple_of(first + col_at * part, part), part)]
    gather = Gather(
        latent_block, lambda index: latent_all.at[index, col_at],
        lambda index: latent_all.at[index, 1 - col_at], gather_sems, True,
    )
    gather.start()
    steps = gather.steps()
    gradient = matmul(latent_out[2, pl.ds(first, count)], latent_weight[...])
    gradient = gradient + wide_rows[row_at].astype(jnp.float32)
    for number in range(row_count - 1):
        wait_arrived(wide_row_in.at[number], row_sems, (1, number))
        gradient = gradient + wide_row_in[number].astype(jnp.float32)
    scale = inverse_one[:, :1]
    normed = rows[...].astype(jnp.float32) * scale
    scaled = gradient * gain[:1]
    squares[...] = jnp.broadcast_to(
        jnp.sum(scaled * normed, axis=1, keepdims=True), squares.shape
    )
    started.append(remote(squares, squares_in, core_sems, (2,), core))
    steps.pop(0)()
    gain_part = jnp.sum(gradient * normed, axis=0, keepdims=True)
    row = lax.broadcasted_iota(jnp.int32, sums_in.shape, 0)
    padded = jnp.concatenate(
        [latent_gain_part, jnp.zeros((1, width - latent_gain_part.shape[1]), jnp.float32)], axis=1
    )
    total = jnp.where(row == 0, gain_part, jnp.where(row == 2, padded, sums_in[...]))
    wait_arrived(squares_in, core_sems, (2,))
    inner = (squares[...] + squares_in[...])[:, :1] / (2 * width)
    input_grad[...] = grad_hidden[...] + scale * (scaled - normed * inner)
    work()
    stages = (
        (slow_ids, slow_in, slow_sums),
        (fast_ids, fast_in, fast_sums),
        (row_ids, row_in, row_sums),
        (core_ids, core_in, core_sums),
    )
    for stage, (devices, buffer, sems) in enumerate(stages):
        running[stage] = total
        for number, device in enumerate(devices):
            started.append(
                remote(running.at[stage], buffer.at[number], sems, (number,), device)
            )
        steps.pop(0)()
        for number in range(len(devices)):
            wait_arrived(buffer.at[number], sems, (number,))
            arrived = buffer[number]
            total = total + (jnp.where(row == 2, arrived, 0.0) if stage == 3 else arrived)
    sums[...] = total
    for step in steps[: slow - 1]:
        step()
    while jobs:
        work()
    for step in steps[slow - 1 :]:
        step()
    gather.finish()
    for copy in started:
        copy.wait_send()


def weight_jobs(inputs, outputs, total):
    attended, stream, turned, small_turned, query_both, keyvalue = inputs
    return [
        row_job(small_turned, keyvalue, outputs[1], total),
        sided_job(attended, stream, outputs[0], total),
        sided_job(turned, query_both, outputs[2], total),
    ]


def tail(operands, shapes, fused, collective_id):
    exp_count, row_count = lax.axis_size("exp"), lax.axis_size("row")
    slow = min(4, exp_count)
    fast = exp_count // slow
    rows = operands[0]
    count, width = rows.shape
    group = row_count * count
    latent_width = operands[10].shape[0]
    query_width, keyvalue_width = operands[9].shape[1], operands[8].shape[1]
    low, high = jnp.bfloat16, jnp.float32
    vmem = pl.BlockSpec(memory_space=pltpu.VMEM)
    dma = pltpu.SemaphoreType.DMA
    sums = (8, width)
    counts = (slow - 1, fast - 1, row_count - 1, 1)
    return pl.pallas_call(
        functools.partial(tail_kernel, fused=fused),
        out_shape=[
            jax.ShapeDtypeStruct((count, width), high),
            jax.ShapeDtypeStruct(sums, high),
            jax.ShapeDtypeStruct((exp_count * row_count, 2, count // 2, latent_width), low),
            *shapes,
        ],
        in_specs=[vmem] * 11 + [ANY_SPEC] * 8,
        out_specs=[vmem, vmem] + [ANY_SPEC] * 4,
        scratch_shapes=[
            pltpu.VMEM((group, query_width), low),
            pltpu.VMEM((group, keyvalue_width), low),
            pltpu.VMEM((group, DR), high),
            pltpu.VMEM((width, query_width), low),
            pltpu.VMEM((3, group, latent_width), low),
            pltpu.VMEM((group, latent_width), low),
            pltpu.VMEM((row_count - 1, group, latent_width), low),
            pltpu.VMEM((group, width), low),
            pltpu.VMEM((group, width), low),
            pltpu.VMEM((row_count, count, width), low),
            pltpu.VMEM((row_count - 1, count, width), low),
            pltpu.VMEM((count // 2, latent_width), low),
            pltpu.VMEM((count, 128), high),
            pltpu.VMEM((count, 128), high),
            pltpu.VMEM((4, *sums), high),
            *[pltpu.VMEM((number, *sums), high) for number in counts],
            pltpu.VMEM(TOTAL if fused else (8, 128), high),
            dma((4,)),
            dma((2, 3)),
            dma((2, 2, row_count - 1)),
            *[dma((2, number)) for number in counts],
            *Gather.sems(),
        ],
        compiler_params=pltpu.CompilerParams(
            collective_id=collective_id, has_side_effects=True, vmem_limit_bytes=VMEM_LIMIT
        ),
    )(*operands)


def local(
    layer_input,
    attention_gain,
    query_weight,
    latent_weight,
    latent_gain,
    keyvalue_weight,
    output_weight,
    feedforward_gain,
    shared_gate,
    shared_up,
    shared_down,
    expert_gate,
    expert_up,
    expert_down,
    sequence_lengths,
    expert_ids,
    expert_weights,
    output_grad,
):
    exp_index, row_index, col_index = (
        lax.axis_index("exp"),
        lax.axis_index("row"),
        lax.axis_index("col"),
    )
    exp_count = lax.axis_size("exp")
    local_tokens, half_width = layer_input.shape
    full_width = 2 * half_width
    per_device = expert_gate.shape[0]
    group_size = local_tokens * lax.axis_size("row")
    tokens = group_size * exp_count
    group_start = exp_index * group_size

    def part_of(array, side, axis):
        width = array.shape[axis] // 2
        return lax.dynamic_slice_in_dim(array, side * width, width, axis)

    def split_exchange(array, axis):
        return part_of(array, col_index, axis), swap_core(part_of(array, 1 - col_index, axis))

    def own_rows(array):
        return lax.dynamic_slice_in_dim(array, group_start, group_size, 0)

    col = col_index.reshape(1)
    top = expert_ids.shape[1]
    _, places = sequence_layout(sequence_lengths[0], group_size)
    cosine, sine = rope_tables(places)
    first_key = jnp.arange(group_size, dtype=jnp.int32) - places

    def widened(array, width):
        return jnp.pad(array.astype(jnp.float32), ((0, 0), (0, width - array.shape[1])))

    tables = jnp.concatenate(
        [
            widened(expert_ids, 8),
            widened(expert_weights, 8),
            widened(first_key[:, None], 16),
            cosine,
            sine,
            jnp.zeros((group_size, 32), jnp.float32),
        ],
        axis=1,
    )
    latent_turned = latent_weight.T
    gate_turned, up_turned = expert_gate.swapaxes(1, 2), expert_up.swapaxes(1, 2)
    gain_own = jnp.broadcast_to(attention_gain.astype(jnp.float32), (8, half_width))
    latent_gains = jnp.broadcast_to(latent_gain.astype(jnp.float32), (8, R))

    gain_two = feedforward_gain.astype(jnp.float32)
    (
        own_normed, own_scale, inverse_one, hidden_state, normed_two, scale_two, mixer_input,
        tables_all, grad_all, input_all, query_other, latent_other, gain_other,
        gate_other, up_other, down_other, shared_gate_other, shared_up_other, shared_down_other,
    ) = prologue(
        layer_input, gain_own, latent_gains, keyvalue_weight, output_weight,
        gain_two[None], tables, query_weight, latent_turned, output_grad,
        (gate_turned, up_turned, expert_down, shared_gate, shared_up, shared_down), 6,
    )
    scale_two = scale_two[:, :1]
    weights = (
        gain_own, gain_other, query_weight, query_other, latent_turned, latent_other,
        latent_gains, keyvalue_weight,
    )
    tables_all = tables_all.reshape(tokens, -1)
    (
        mixer, both_hidden, both_gating, both_upward, shared_hidden, shared_gating, shared_upward,
        mixer_turned,
    ) = run_units(
        mixer_input,
        tables_all,
        grad_all,
        (
            gate_turned, gate_other, up_turned, up_other, expert_down, down_other,
            shared_gate, shared_gate_other, shared_up, shared_up_other,
            shared_down, shared_down_other,
        ),
        1,
    )
    fused = tokens <= 2048
    low = jnp.bfloat16

    def shape(*sizes, kind=low):
        return jax.ShapeDtypeStruct(sizes, kind)

    units, shared_units = gate_turned.shape[1], shared_gate.shape[1]

    def gate_jobs(inputs, outputs, total, *_):
        gating, upward, rows, rows_turned, own_gating, own_upward = inputs
        return [
            stacked_job(gating, rows, outputs[0], total),
            stacked_job(upward, rows, outputs[1], total),
            row_job(rows_turned, own_gating, outputs[2], total),
            row_job(rows_turned, own_upward, outputs[3], total),
        ]

    gate_operands = (
        both_gating, both_upward, mixer, mixer_turned, shared_gating, shared_upward
    )
    gate_shapes = [shape(per_device, units, half_width)] * 2 + [
        shape(half_width, shared_units)
    ] * 2
    products = (
        both_gating, both_upward, gate_turned, up_turned, shared_gating, shared_upward,
        shared_gate, shared_up,
    )
    if fused:
        mixer_grad, *gate_grads = scatter_products(
            products, True, 2, gate_jobs, gate_operands, gate_shapes
        )
    else:
        (mixer_grad,) = scatter_products(products, True, 2)
        gate_grads = run_jobs(gate_jobs, gate_operands, gate_shapes)

    upstream = output_grad.astype(jnp.float32)
    grad_norm_two, gain_two_grad = norm_backward(mixer_grad, normed_two, scale_two, gain_two)
    grad_hidden = upstream + grad_norm_two

    heads_width = keyvalue_weight.shape[1] // 2
    query_width = query_weight.shape[1] // 2

    def stream_jobs(inputs, outputs, total):
        hidden, own_hidden, grads, values = inputs[:4]
        return [
            *project_jobs(values, inputs[4:12], inputs[12], outputs[2:], 2),
            expert_down_job(hidden, grads, outputs[0], total),
            shared_down_job(own_hidden, grads, outputs[1], total),
        ]

    stream_operands = (
        both_hidden, shared_hidden, grad_all, input_all, *weights, tables_all
    )
    stream_shapes = [
        shape(*expert_down.shape),
        shape(*shared_down.shape),
        shape(tokens, query_width),
        shape(tokens, keyvalue_weight.shape[1]),
        shape(tokens, DR),
        shape(half_width, tokens),
        shape(R, tokens),
    ]
    stream_input = grad_hidden.astype(jnp.bfloat16)
    if fused:
        stream, results = gather_everywhere(
            stream_input, 3, stream_jobs, stream_operands, stream_shapes
        )
    else:
        stream, _ = gather_everywhere(stream_input, 3)
        results = run_jobs(stream_jobs, stream_operands, stream_shapes)
    (
        expert_down_grad, shared_down_grad, query_all, keyvalue_all, rope_key_all,
        attention_turned, compressed_turned,
    ) = results

    other_hidden = swap_core(
        lax.dynamic_slice_in_dim(shared_hidden, group_start, group_size, 1)
    )

    def attention_part(inputs, outputs, total, core, sems):
        arrays, (stream_ref, weight) = inputs[:4], inputs[4:]
        attended_ref, query_both, keyvalue_ref, rope_ref = outputs
        jobs = attention_jobs(
            arrays, stream_ref, weight,
            (attended_ref, query_both.at[0], keyvalue_ref, rope_ref), exp_count, 4,
        )

        def exchange():
            remote(query_both.at[0], query_both.at[1], sems, (0,), core).wait()

        return [*jobs, exchange]

    weight_shapes = [
        shape(*output_weight.shape), shape(*keyvalue_weight.shape), shape(*query_weight.shape)
    ]
    (
        produced, attended_turned, query_grads, grad_keyvalue, grad_rope
    ) = scatter_products(
        (
            both_hidden, expert_down, down_other, shared_hidden, other_hidden,
            shared_down, shared_down_other,
        ),
        False,
        4,
        attention_part,
        (
            tables_all, query_all, keyvalue_all, rope_key_all, stream, output_weight,
        ),
        [
            shape(heads_width, tokens),
            shape(2, tokens, query_width),
            shape(tokens, keyvalue_weight.shape[1]),
            shape(tokens, DR, kind=jnp.float32),
        ],
    )
    layer_result = (hidden_state + produced).astype(jnp.bfloat16)
    sums_in = jnp.pad(gain_two_grad[None], ((1, 6), (0, 0)))
    weight_operands = (attended_turned, stream, attention_turned, compressed_turned)
    input_grad, sums, latent_all, *weight_grads = tail(
        (
            layer_input, inverse_one, gain_own, grad_hidden, sums_in, own_normed, own_scale,
            latent_gains, keyvalue_weight, query_other, latent_turned,
            query_grads, grad_keyvalue, grad_rope, query_weight, *weight_operands,
        ),
        weight_shapes,
        fused,
        5,
    )
    if not fused:
        weight_grads = run_jobs(
            weight_jobs, (*weight_operands, query_grads, grad_keyvalue), weight_shapes
        )
    output_weight_grad, keyvalue_weight_grad, query_weight_grad = weight_grads
    latent_weight_grad = matmul(attention_turned, latent_all.reshape(tokens, -1))
    wide = [
        array.astype(jnp.float32)
        for array in (
            query_weight_grad, keyvalue_weight_grad, output_weight_grad, *gate_grads,
            shared_down_grad, expert_down_grad,
        )
    ]
    return (
        layer_result,
        input_grad,
        sums[0],
        wide[0],
        latent_weight_grad,
        sums[2, : latent_gain.shape[0]],
        wide[1],
        wide[2],
        sums[1],
        wide[5],
        wide[6],
        wide[7],
        wide[3].swapaxes(1, 2),
        wide[4].swapaxes(1, 2),
        wide[8],
    )


def solution(mesh):
    in_specs = (
        P(("exp", "row"), "col"),
        P("col"),
        P("col", "row"),
        P("col", None),
        P(),
        P(None, ("row", "col")),
        P(("row", "col"), None),
        P("col"),
        P("col", "row"),
        P("col", "row"),
        P(("row", "col"), None),
        P("exp", "col", "row"),
        P("exp", "col", "row"),
        P("exp", ("row", "col"), None),
        P("exp", None),
        P("exp", None),
        P("exp", None),
        P(("exp", "row"), "col"),
    )
    out_specs = (
        P(("exp", "row"), "col"),
        P(("exp", "row"), "col"),
        P("col"),
        P("col", "row"),
        P("col", None),
        P(),
        P(None, ("row", "col")),
        P(("row", "col"), None),
        P("col"),
        P("col", "row"),
        P("col", "row"),
        P(("row", "col"), None),
        P("exp", "col", "row"),
        P("exp", "col", "row"),
        P("exp", ("row", "col"), None),
    )
    return jax.shard_map(local, mesh=mesh, in_specs=in_specs, out_specs=out_specs, check_vma=False)
```

```python
import functools

import jax
import jax.numpy as jnp
from jax import lax
from jax.experimental import pallas as pl
from jax.experimental.pallas import tpu as pltpu
from jax.sharding import PartitionSpec as P

DN = 128
DR = 64
DV = 128
R = 512
TOP = 6


EPSILON = 1e-06
ROPE_BASE = 50000.0
NEGATIVE = -1e30


def matmul(former, latter):
    return jnp.dot(former, latter, preferred_element_type=jnp.float32)


def matmul_left(former, latter):
    return lax.dot_general(
        former, latter, (((0,), (0,)), ((), ())), preferred_element_type=jnp.float32
    )


def matmul_right(former, latter):
    return lax.dot_general(
        former, latter, (((1,), (1,)), ((), ())), preferred_element_type=jnp.float32
    )


def sequence_layout(lengths, group_size):
    seq_ends = jnp.cumsum(lengths)
    token_order = jnp.arange(group_size, dtype=jnp.int32)
    segment = jnp.sum((token_order[:, None] >= seq_ends[None, :]).astype(jnp.int32), axis=1)
    seq_starts = seq_ends - lengths
    own_start = jnp.sum(
        jnp.where(
            segment[:, None] == jnp.arange(lengths.shape[0], dtype=jnp.int32)[None, :],
            seq_starts[None, :],
            0,
        ),
        axis=1,
    )
    return (segment, token_order - own_start)


def rope_tables(places):
    inverse_frequency = ROPE_BASE ** (-(jnp.arange(DR // 2, dtype=jnp.float32) * 2.0 / DR))
    angles = places.astype(jnp.float32)[:, None] * inverse_frequency[None, :]
    return (jnp.cos(angles), jnp.sin(angles))


MESH = pl.DeviceIdType.MESH
VMEM_LIMIT = 60 * 1024 * 1024
LOG2_E = 1.4426950408889634


def full_spec(array):
    zeros = (0,) * array.ndim
    return pl.BlockSpec(array.shape, lambda *_: zeros)


ANY_SPEC = pl.BlockSpec(memory_space=pl.ANY)


def swap_core(values):
    return lax.ppermute(values, "col", [(0, 1), (1, 0)])


def half_sums(values):
    return lax.psum(values, "col")


def norm_backward(gradient, normed, inverse_rms, gain_vector):
    full_width = normed.shape[1] * lax.axis_size("col")
    scaled = gradient * gain_vector
    inner_sum = half_sums(jnp.sum(scaled * normed, axis=1)) / full_width
    return (
        inverse_rms * (scaled - normed * inner_sum[:, None]),
        jnp.sum(gradient * normed, axis=0),
    )


TABLE = dict(ids=0, router=8, first=16, cosine=32, sine=64)


def rotary_tables(table):
    cosine = table[:, TABLE["cosine"] : TABLE["cosine"] + DR // 2]
    sine = table[:, TABLE["sine"] : TABLE["sine"] + DR // 2]
    return jnp.concatenate([cosine, cosine], axis=1), jnp.concatenate([-sine, sine], axis=1)


def first_keys(table):
    return table[:, TABLE["first"] : TABLE["first"] + 1].astype(jnp.int32)


def rotary(values, cosine_both, sine_signed):
    half = values.shape[-1] // 2
    swapped = jnp.concatenate([values[:, half:], values[:, :half]], axis=-1)
    return values * cosine_both + swapped * sine_signed


def project_rows(
    rows_own, rows_other, gain_own, gain_other, query_own, query_other, latent_own, latent_other,
    latent_gain, keyvalue_weight, table, query, keyvalue, rope_key
):
    rows_own = rows_own.astype(jnp.float32)
    rows_other = rows_other.astype(jnp.float32)
    total = jnp.sum(rows_own * rows_own, axis=1, keepdims=True)
    total = total + jnp.sum(rows_other * rows_other, axis=1, keepdims=True)
    scale = lax.rsqrt(total / (2 * rows_own.shape[1]) + EPSILON)
    rows_own = (rows_own * scale * gain_own[:1]).astype(jnp.bfloat16)
    rows_other = (rows_other * scale * gain_other[:1]).astype(jnp.bfloat16)
    queries = matmul(rows_own, query_own[...]) + matmul(rows_other, query_other[...])
    cosine, sine = rotary_tables(table)
    for first in range(0, query.shape[1], DN + DR):
        rope = rotary(queries[:, first + DN : first + DN + DR], cosine, sine)
        query[:, first : first + DN + DR] = jnp.concatenate(
            [queries[:, first : first + DN], rope], axis=1
        ).astype(jnp.bfloat16)
    latent = matmul_right(rows_own, latent_own[...]) + matmul_right(rows_other, latent_other[...])
    raw = latent[:, :R]
    latent_scale = lax.rsqrt(jnp.mean(raw * raw, axis=1, keepdims=True) + EPSILON)
    latent_normed = raw * latent_scale
    compressed = (latent_normed * latent_gain[:1]).astype(jnp.bfloat16)
    keyvalue[...] = matmul(compressed, keyvalue_weight[...]).astype(jnp.bfloat16)
    rope_key[...] = rotary(latent[:, R:], cosine, sine).astype(jnp.bfloat16)
    return rows_own, compressed, latent_normed, latent_scale, scale


def softmax_parts(queries, keys, bias):
    scores = matmul_right(queries, keys) * ((DN + DR) ** (-0.5) * LOG2_E) + bias
    exponent = jnp.exp2(scores - jnp.max(scores, axis=1, keepdims=True))
    return exponent * (1.0 / jnp.sum(exponent, axis=1, keepdims=True))


def mask_bias(first_key):
    size = first_key.shape[0]
    row = lax.broadcasted_iota(jnp.int32, (size, size), 0)
    column = lax.broadcasted_iota(jnp.int32, (size, size), 1)
    return jnp.where((column <= row) & (column >= first_key), 0.0, NEGATIVE)


def head_keys(keyvalue, rope_keys, head):
    first = head * (DN + DV)
    keys = jnp.concatenate([keyvalue[:, first : first + DN], rope_keys], axis=1)
    return keys, keyvalue[:, first + DN : first + DN + DV]


def attend_kernel(table, query, keyvalue, rope_key, attended):
    bias = mask_bias(first_keys(table))
    rope_keys = rope_key[...]
    for head in range(query.shape[1] // (DN + DR)):
        first = head * (DN + DR)
        keys, values = head_keys(keyvalue, rope_keys, head)
        weights = softmax_parts(query[:, first : first + DN + DR], keys, bias)
        attended[:, head * DV : (head + 1) * DV] = matmul(
            weights.astype(jnp.bfloat16), values
        ).astype(jnp.bfloat16)


def attention_body(
    table, query, keyvalue, rope_key, stream_own, stream_other,
    output_own, output_other, attended, grad_query, grad_keyvalue, grad_rope
):
    factor = (DN + DR) ** (-0.5)
    bias = mask_bias(first_keys(table))
    cosine, sine = rotary_tables(table)
    rope_keys = rope_key[...]
    size = query.shape[0]
    grad_heads = matmul_right(stream_own[0], output_own[...]) + matmul_right(
        stream_other[0], output_other[...]
    )
    grad_heads = grad_heads.astype(jnp.bfloat16)
    rope_total = jnp.zeros((size, DR), jnp.float32)
    for head in range(query.shape[1] // (DN + DR)):
        first = head * (DN + DR)
        first_kv = head * (DN + DV)
        queries = query[:, first : first + DN + DR]
        keys, values = head_keys(keyvalue, rope_keys, head)
        probabilities = softmax_parts(queries, keys, bias)
        weights = probabilities.astype(jnp.bfloat16)
        result = matmul(weights, values)
        attended[head * DV : (head + 1) * DV, :] = result.astype(jnp.bfloat16).T
        grad_head = grad_heads[:, head * DV : (head + 1) * DV]
        inner = jnp.sum(result * grad_head.astype(jnp.float32), axis=1, keepdims=True)
        grad_scores = (probabilities * (matmul_right(grad_head, values) - inner)).astype(
            jnp.bfloat16
        )
        grad_queries = matmul(grad_scores, keys) * factor
        grad_keys = matmul_left(grad_scores, queries) * factor
        unrotated = rotary(grad_queries[:, DN:], cosine, -sine)
        grad_query[:, first : first + DN + DR] = jnp.concatenate(
            [grad_queries[:, :DN], unrotated], axis=1
        ).astype(jnp.bfloat16)
        grad_keyvalue[:, first_kv : first_kv + DN] = grad_keys[:, :DN].astype(jnp.bfloat16)
        grad_keyvalue[:, first_kv + DN : first_kv + DN + DV] = matmul_left(
            weights, grad_head
        ).astype(jnp.bfloat16)
        rope_total = rope_total + grad_keys[:, DN:]
    grad_rope[...] = rotary(rope_total, cosine, -sine)


def positions():
    exp_count = lax.axis_size("exp")
    slow = min(4, exp_count)
    fast = exp_count // slow
    row_count = lax.axis_size("row")
    exp_index = lax.axis_index("exp")
    place = (exp_index // fast, exp_index % fast, lax.axis_index("row"), lax.axis_index("col"))
    return place, (slow, fast, row_count)


def peers(with_core):
    (slow_at, fast_at, row_at, col_at), (slow, fast, row_count) = positions()
    slow_ids = [
        {"exp": (slow_at + step) % slow * fast + fast_at} for step in range(1, slow)
    ]
    fast_ids = [
        {"exp": slow_at * fast + (fast_at + step) % fast} for step in range(1, fast)
    ]
    row_ids = [{"row": (row_at + step) % row_count} for step in range(1, row_count)]
    core_ids = [{"col": 1 - col_at}] if with_core else []
    return slow_ids, fast_ids, row_ids, core_ids


def enter(groups):
    barrier = pltpu.get_barrier_semaphore()
    count = 0
    for group in groups:
        for device in group:
            pl.semaphore_signal(barrier, inc=1, device_id=device, device_id_type=MESH)
            count += 1
    pl.semaphore_wait(barrier, count)


def remote(src, dst, sems, index, device):
    copy = pltpu.make_async_remote_copy(
        src_ref=src,
        dst_ref=dst,
        send_sem=sems.at[(0, *index)],
        recv_sem=sems.at[(1, *index)],
        device_id=device,
        device_id_type=MESH,
    )
    copy.start()
    return copy


def wait_arrived(dst, sems, index):
    pltpu.make_async_copy(dst, dst, sems.at[(1, *index)]).wait()


def sent(src, sems, index):
    pltpu.make_async_copy(src, src, sems.at[(0, *index)]).wait()


class Gather:
    def __init__(self, source, own, other, sems, by_core):
        self.source, self.own, self.other = source, own, other
        self.far = own if by_core else other
        self.place, self.sizes = positions()
        self.fast_ids, self.row_ids, core_ids = peers(True)[1:]
        self.core = core_ids[0]
        self.half = source.shape[0] // 2
        (
            self.local, self.up, self.down, self.fast, self.row, self.low, self.high,
            self.core_sems, self.core_half,
        ) = sems

    @staticmethod
    def sems():
        exp_count, row_count = lax.axis_size("exp"), lax.axis_size("row")
        slow = min(4, exp_count)
        fast = exp_count // slow
        corner = (fast - 1, row_count - 1, slow)
        return [pltpu.SemaphoreType.DMA] + [
            pltpu.SemaphoreType.DMA((2, *shape))
            for shape in (
                (slow - 1,), (slow - 1,), (fast - 1, slow), (row_count - 1, slow), corner, corner,
                (fast, row_count, slow), (2, *corner),
            )
        ]

    def index(self, line, fast_off, row_off):
        _, fast_at, row_at, _ = self.place
        _, fast, row_count = self.sizes
        fast_index = (fast_at + fast - fast_off) % fast
        return (line * fast + fast_index) * row_count + (row_at + row_count - row_off) % row_count

    def part(self, ref, number):
        return ref.at[pl.ds(number * self.half, self.half)]

    def keep(self):
        mine = self.index(self.place[0], 0, 0)
        return pltpu.make_async_copy(self.source, self.own(mine), self.local)

    def along(self, up, src, index, number):
        slow_at, fast_at = self.place[:2]
        slow, fast, _ = self.sizes

        @pl.when(slow_at < slow - 1 if up else slow_at > 0)
        def _():
            goal = (slow_at + 1 if up else slow_at - 1) * fast + fast_at
            remote(
                src, self.own(index), self.up if up else self.down, (number,), {"exp": goal}
            )

    def spread(self, src, line):
        index = self.index(line, 0, 0)
        for number, device in enumerate(self.fast_ids):
            remote(src, self.own(index), self.fast, (number, line), device)
        for number, device in enumerate(self.row_ids):
            remote(src, self.own(index), self.row, (number, line), device)
        remote(src, self.far(index), self.core_sems, (0, 0, line), self.core)

    def start(self):
        self.keep().start()
        mine = self.index(self.place[0], 0, 0)
        self.along(True, self.source, mine, 0)
        self.along(False, self.source, mine, 0)
        self.spread(self.source, self.place[0])

    def lines(self, number, act):
        slow_at, slow = self.place[0], self.sizes[0]
        if number == 0:
            act(slow_at, None)
            return

        @pl.when(slow_at >= number)
        def _():
            act(slow_at - number, True)

        @pl.when(slow_at + number < slow)
        def _():
            act(slow_at + number, False)

    def hop(self, number):
        def act(line, up):
            block = self.own(self.index(line, 0, 0))
            wait_arrived(block, self.up if up else self.down, (number - 1,))
            if number < self.sizes[0] - 1:
                self.along(up, block, self.index(line, 0, 0), number)
            self.spread(block, line)

        self.lines(number, act)

    def corner(self, number):
        _, fast, row_count = self.sizes

        def act(line, _):
            for fast_off in range(1, fast):
                index = self.index(line, fast_off, 0)
                block = self.own(index)
                wait_arrived(block, self.fast, (fast_off - 1, line))
                for count, device in enumerate(self.row_ids):
                    low = self.part(block, 0)
                    remote(low, low, self.low, (fast_off - 1, count, line), device)
                remote(block, self.far(index), self.core_sems, (fast_off, 0, line), self.core)
            for row_off in range(1, row_count):
                index = self.index(line, 0, row_off)
                block = self.own(index)
                wait_arrived(block, self.row, (row_off - 1, line))
                for count, device in enumerate(self.fast_ids):
                    high = self.part(block, 1)
                    remote(high, high, self.high, (count, row_off - 1, line), device)
                remote(block, self.far(index), self.core_sems, (0, row_off, line), self.core)

        self.lines(number, act)

    def last(self, number):
        _, fast, row_count = self.sizes

        def act(line, _):
            for fast_off in range(1, fast):
                for row_off in range(1, row_count):
                    index = self.index(line, fast_off, row_off)
                    spot = (fast_off - 1, row_off - 1, line)
                    for count, sems in enumerate((self.low, self.high)):
                        half = self.part(self.own(index), count)
                        wait_arrived(half, sems, spot)
                        remote(
                            half, self.part(self.far(index), count), self.core_half,
                            (count, *spot), self.core,
                        )

        self.lines(number, act)

    def ready(self, line, fast_off):
        row_count = self.sizes[2]

        @pl.when(fast_off == 0)
        def _():
            for row_off in range(row_count):
                block = self.other(self.index(line, 0, row_off))
                wait_arrived(block, self.core_sems, (0, row_off, line))

        @pl.when(fast_off > 0)
        def _():
            block = self.other(self.index(line, fast_off, 0))
            wait_arrived(block, self.core_sems, (fast_off, 0, line))
            for row_off in range(1, row_count):
                block = self.other(self.index(line, fast_off, row_off))
                for count in range(2):
                    spot = (count, fast_off - 1, row_off - 1, line)
                    wait_arrived(self.part(block, count), self.core_half, spot)

    def finish(self, all_ready=False):
        slow_at = self.place[0]
        slow, fast, row_count = self.sizes
        whole = self.own(self.index(slow_at, 0, 0))
        half = self.part(whole, 0)

        @pl.loop(0, slow)
        def _(line):
            for fast_off in range(fast):
                for row_off in range(row_count):
                    block = self.other(self.index(line, fast_off, row_off))
                    if fast_off and row_off:
                        spot = (fast_off - 1, row_off - 1, line)
                        for count in range(2):
                            if not all_ready:
                                wait_arrived(
                                    self.part(block, count), self.core_half, (count, *spot)
                                )
                            sent(half, self.core_half, (count, *spot))
                        sent(half, self.low, spot)
                        sent(half, self.high, spot)
                    else:
                        if not all_ready:
                            wait_arrived(block, self.core_sems, (fast_off, row_off, line))
                        sent(whole, self.core_sems, (fast_off, row_off, line))
            for count in range(fast - 1):
                sent(whole, self.fast, (count, line))
            for count in range(row_count - 1):
                sent(whole, self.row, (count, line))

        for number in range(slow - 1):

            @pl.when((slow_at >= number) & (slow_at < slow - 1))
            def _():
                sent(whole, self.up, (number,))

            @pl.when((slow_at + number < slow) & (slow_at > 0))
            def _():
                sent(whole, self.down, (number,))

        if not all_ready:
            self.keep().wait()

    def steps(self):
        slow = self.sizes[0]
        return (
            [functools.partial(self.hop, number) for number in range(1, slow)]
            + [functools.partial(self.corner, number) for number in range(slow)]
            + [functools.partial(self.last, number) for number in range(slow)]
        )


def prologue_kernel(
    rows, gain, latent_gain, keyvalue_weight, output_weight, table,
    gain_two, tables, query_weight, latent_weight, upstream,
    gate, up, down, shared_gate, shared_up, shared_down,
    latent_normed, latent_scale, inverse_one, hidden, normed, inverse, mixer,
    tables_all, grad_all, query_far, latent_far, gain_far,
    gate_far, up_far, down_far, shared_gate_far, shared_up_far, shared_down_far,
    rows_own, rows_other, query_own, query_other, latent_own, latent_other, gain_other,
    query, keyvalue, rope_key, attended, scales, given, from_core, rows_out, from_rows,
    squares, squares_in,
    local_sems, row_sems, core_rows, slow_sems, fast_sems, core_sems, mix_core, mix_rows,
    weight_sems, *gather_sems
):
    (slow_at, fast_at, row_at, col_at), (slow, fast, row_count) = positions()
    slow_ids, fast_ids, row_ids, core_ids = peers(True)
    core = core_ids[0]
    count, width = rows.shape
    mine = slow_at * fast + fast_at
    query_width = query_own.shape[1]
    own_heads = pl.ds(pl.multiple_of(col_at * query_width, query_width), query_width)
    given_heads = pl.ds(pl.multiple_of((1 - col_at) * query_width, query_width), query_width)
    gather = Gather(
        upstream, lambda index: grad_all.at[index, col_at],
        lambda index: grad_all.at[index, 1 - col_at], gather_sems, True,
    )
    loads = [
        pltpu.make_async_copy(query_weight.at[:, own_heads], query_own, local_sems.at[0]),
        pltpu.make_async_copy(latent_weight, latent_own, local_sems.at[1]),
        pltpu.make_async_copy(tables, tables_all.at[mine], local_sems.at[2]),
    ]
    for copy in loads:
        copy.start()
    rows_own[row_at] = rows[...]
    enter((slow_ids, fast_ids, row_ids, core_ids))
    started = [
        remote(rows, rows_own.at[row_at], row_sems, (number,), device)
        for number, device in enumerate(row_ids)
    ]
    started.append(remote(rows, rows_other.at[row_at], core_rows, (0,), core))
    started.append(remote(gain, gain_other, core_sems, (0,), core))
    started.append(remote(query_weight.at[:, given_heads], query_other, core_sems, (1,), core))
    started.append(remote(latent_weight, latent_other, core_sems, (2,), core))
    for number, device in enumerate(slow_ids):
        started.append(remote(tables, tables_all.at[mine], slow_sems, (number,), device))
    for number, device in enumerate(fast_ids):
        started.append(remote(tables, tables_all.at[mine], fast_sems, (number, 0), device))
    gather.start()
    steps = gather.steps()
    for offset in range(1, row_count):
        index = (row_at + row_count - offset) % row_count
        wait_arrived(rows_own.at[index], row_sems, (offset - 1,))
        started.append(
            remote(rows_own.at[index], rows_other.at[index], core_rows, (offset,), core)
        )
    for offset in range(row_count):
        index = (row_at + row_count - offset) % row_count
        wait_arrived(rows_other.at[index], core_rows, (offset,))
    steps.pop(0)()
    for number, target in enumerate((gain_other, query_other, latent_other)):
        wait_arrived(target, core_sems, (number,))
    exchanged = [
        (gate.at[1 - col_at], gate_far), (up.at[1 - col_at], up_far), (down, down_far),
        (shared_gate, shared_gate_far), (shared_up, shared_up_far), (shared_down, shared_down_far),
    ]
    for number, (source, target) in enumerate(exchanged):
        started.append(remote(source, target, weight_sems, (number,), core))
    for copy in loads:
        copy.wait()
    steps.pop(0)()
    keeps = [
        pltpu.make_async_copy(source, target, local_sems.at[number])
        for number, (source, target) in enumerate(
            ((query_other, query_far), (latent_other, latent_far), (gain_other, gain_far))
        )
    ]
    for copy in keeps:
        copy.start()
    _, _, latent_unit, latent_rms, scale = project_rows(
        rows_own[...].reshape(row_count * count, width),
        rows_other[...].reshape(row_count * count, width),
        gain, gain_other, query_own, query_other, latent_own, latent_other, latent_gain,
        keyvalue_weight, table, query, keyvalue, rope_key,
    )
    latent_normed[...] = latent_unit
    latent_scale[...] = latent_rms
    scales[...] = jnp.broadcast_to(scale, scales.shape)
    inverse_one[...] = scales[pl.ds(pl.multiple_of(row_at * count, count), count), :]
    steps.pop(0)()
    attend_kernel(table, query, keyvalue, rope_key, attended)
    steps.pop(0)()
    for offset in range(1, slow):
        index = (slow_at + slow - offset) % slow * fast + fast_at
        wait_arrived(tables_all.at[index], slow_sems, (offset - 1,))
        for number, device in enumerate(fast_ids):
            started.append(
                remote(
                    tables_all.at[index], tables_all.at[index], fast_sems, (number, offset), device
                )
            )

    own_half = pl.ds(pl.multiple_of(col_at * width, width), width)
    other_half = pl.ds(pl.multiple_of((1 - col_at) * width, width), width)
    given[...] = matmul(attended[...], output_weight[:, other_half]).astype(jnp.bfloat16)
    started.append(remote(given, from_core, mix_core, (0,), core))
    total = matmul(attended[...], output_weight[:, own_half])
    wait_arrived(from_core, mix_core, (0,))
    total = total + from_core[...].astype(jnp.float32)
    rows_out[...] = total.astype(jnp.bfloat16).reshape(rows_out.shape)
    for number, device in enumerate(row_ids):
        goal = (row_at + number + 1) % row_count
        started.append(remote(rows_out.at[goal], from_rows.at[number], mix_rows, (number,), device))
    steps.pop(0)()
    state = rows[...].astype(jnp.float32) + rows_out[row_at].astype(jnp.float32)
    for number in range(row_count - 1):
        wait_arrived(from_rows.at[number], mix_rows, (number,))
        state = state + from_rows[number].astype(jnp.float32)
    hidden[...] = state
    own_squares = jnp.sum(state * state, axis=1, keepdims=True)
    squares[...] = jnp.broadcast_to(own_squares, squares.shape)
    started.append(remote(squares, squares_in, mix_core, (1,), core))
    steps.pop(0)()
    wait_arrived(squares_in, mix_core, (1,))
    rms = lax.rsqrt((squares[...] + squares_in[...]) / (2 * width) + EPSILON)
    inverse[...] = rms
    unit = state * rms[:, :1]
    normed[...] = unit
    mixer[...] = (unit * gain_two[...]).astype(jnp.bfloat16)
    for step in steps:
        step()
    for offset in range(slow):
        for number in range(1, fast):
            index = (slow_at + slow - offset) % slow * fast + (fast_at + fast - number) % fast
            wait_arrived(tables_all.at[index], fast_sems, (number - 1, offset))
    gather.finish()
    for number, (_, target) in enumerate(exchanged):
        wait_arrived(target, weight_sems, (number,))
    for copy in started:
        copy.wait_send()
    for copy in keeps:
        copy.wait()


def prologue(
    rows, gain, latent_gain, keyvalue_weight, output_weight, gain_two, tables,
    query_weight, latent_weight, upstream, others, collective_id
):
    exp_count, row_count = lax.axis_size("exp"), lax.axis_size("row")
    slow = min(4, exp_count)
    fast = exp_count // slow
    count, width = rows.shape
    group = row_count * count
    query_width = query_weight.shape[1] // 2
    keyvalue_width = keyvalue_weight.shape[1]
    latent_width = latent_weight.shape[0]
    low = jnp.bfloat16
    high = jnp.float32
    vmem = pl.BlockSpec(memory_space=pltpu.VMEM)
    wide = jax.ShapeDtypeStruct((count, width), high)
    narrow = jax.ShapeDtypeStruct((count, 128), high)
    dma = pltpu.SemaphoreType.DMA
    return pl.pallas_call(
        prologue_kernel,
        out_shape=[
            jax.ShapeDtypeStruct((group, R), high),
            jax.ShapeDtypeStruct((group, 1), high),
            narrow, wide, wide, narrow,
            jax.ShapeDtypeStruct((count, width), low),
            jax.ShapeDtypeStruct((exp_count, *tables.shape), high),
            jax.ShapeDtypeStruct((exp_count * row_count, 2, count, width), low),
            jax.ShapeDtypeStruct((width, query_width), low),
            jax.ShapeDtypeStruct(latent_weight.shape, low),
            jax.ShapeDtypeStruct(gain.shape, high),
            *[
                jax.ShapeDtypeStruct(array.shape[number < 2 :], low)
                for number, array in enumerate(others)
            ],
        ],
        in_specs=[vmem] * 7 + [ANY_SPEC] * 10,
        out_specs=[vmem] * 7 + [ANY_SPEC] * 11,
        scratch_shapes=[
            pltpu.VMEM((row_count, count, width), low),
            pltpu.VMEM((row_count, count, width), low),
            pltpu.VMEM((width, query_width), low),
            pltpu.VMEM((width, query_width), low),
            pltpu.VMEM((latent_width, width), low),
            pltpu.VMEM((latent_width, width), low),
            pltpu.VMEM(gain.shape, high),
            pltpu.VMEM((group, query_width), low),
            pltpu.VMEM((group, keyvalue_width), low),
            pltpu.VMEM((group, DR), low),
            pltpu.VMEM((group, keyvalue_width // 2), low),
            pltpu.VMEM((group, 128), high),
            pltpu.VMEM((group, width), low),
            pltpu.VMEM((group, width), low),
            pltpu.VMEM((row_count, count, width), low),
            pltpu.VMEM((row_count - 1, count, width), low),
            pltpu.VMEM((count, 128), high),
            pltpu.VMEM((count, 128), high),
            dma((3,)),
            dma((2, row_count - 1)),
            dma((2, row_count)),
            dma((2, slow - 1)),
            dma((2, fast - 1, slow)),
            dma((2, 3)),
            dma((2, 2)),
            dma((2, row_count - 1)),
            dma((2, 6)),
            *Gather.sems(),
        ],
        compiler_params=pltpu.CompilerParams(
            collective_id=collective_id, has_side_effects=True, vmem_limit_bytes=VMEM_LIMIT
        ),
    )(
        rows, gain, latent_gain, keyvalue_weight, output_weight, tables, gain_two, tables,
        query_weight, latent_weight, upstream, *others,
    )


def pipeline(body, grid, inputs, outputs):
    pltpu.emit_pipeline(
        body,
        grid=grid,
        in_specs=[pl.BlockSpec(block, place) for _, block, place in inputs],
        out_specs=[pl.BlockSpec(block, place) for _, block, place in outputs],
    )(*[ref for ref, _, _ in inputs], *[ref for ref, _, _ in outputs])


def product_body(total, axis, steps):
    def body(left, right, result):
        step = pl.program_id(axis)
        product = matmul(
            left[...].reshape(-1, left.shape[-1]), right[...].reshape(-1, right.shape[-1])
        )
        spot = total.at[pl.ds(0, product.shape[0]), pl.ds(0, product.shape[1])]

        @pl.when(step == 0)
        def _():
            spot[...] = product

        @pl.when((step > 0) & (step < steps - 1))
        def _():
            spot[...] += product

        @pl.when(step == steps - 1)
        def _():
            result[...] = (spot[...] + product).reshape(result.shape).astype(result.dtype)

    return body


DEPTH = 1024


def stacked_job(left, right, result, total):
    parts, units, tokens = left.shape
    width = right.shape[2]
    steps = tokens // DEPTH

    def run():
        pipeline(
            product_body(total, 1, steps),
            (parts, steps),
            [
                (left, (1, units, DEPTH), lambda part, step: (part, 0, step)),
                (right, (1, DEPTH, width), lambda part, step: (0, step, 0)),
            ],
            [(result, (1, units, width), lambda part, step: (part, 0, 0))],
        )

    return run


def row_job(left, right, result, total):
    features, tokens = left.shape
    units = right.shape[1]
    steps = tokens // DEPTH

    def run():
        pipeline(
            product_body(total, 0, steps),
            (steps,),
            [
                (left, (features, DEPTH), lambda step: (0, step)),
                (right, (DEPTH, units), lambda step: (step, 0)),
            ],
            [(result, (features, units), lambda step: (0, 0))],
        )

    return run


def expert_down_job(left, right, result, total):
    parts, units, tokens = left.shape
    _, _, rows, width = right.shape
    steps = tokens // DEPTH
    col = lax.axis_index("col")

    def run():
        pipeline(
            product_body(total, 1, steps),
            (2, steps),
            [
                (left, (parts, units // 2, DEPTH), lambda side, step: (0, col, step)),
                (right, (DEPTH // rows, 1, rows, width), lambda side, step: (step, side, 0, 0)),
            ],
            [(result, (parts, units // 2, width), lambda side, step: (0, 0, side))],
        )

    return run


def shared_down_job(left, right, result, total):
    units, tokens = left.shape
    _, _, rows, width = right.shape
    steps = tokens // DEPTH

    def run():
        pipeline(
            product_body(total, 1, steps),
            (2, steps),
            [
                (left, (units, DEPTH), lambda side, step: (0, step)),
                (right, (DEPTH // rows, 1, rows, width), lambda side, step: (step, side, 0, 0)),
            ],
            [(result, (units, width), lambda side, step: (0, side))],
        )

    return run


def sided_job(left, right, result, total):
    units, tokens = left.shape
    width = right.shape[2]
    steps = tokens // DEPTH
    col = lax.axis_index("col")

    def run():
        pipeline(
            product_body(total, 1, steps),
            (2, steps),
            [
                (left, (units, DEPTH), lambda side, step: (0, step)),
                (right, (1, DEPTH, width), lambda side, step: (side, step, 0)),
            ],
            [(result, (units, width), lambda side, step: (0, (col + side) % 2))],
        )

    return run


def project_body(own, other, *rest):
    rows, width = own.shape[0] * own.shape[2], own.shape[3]
    normed, compressed, _, _, _ = project_rows(
        own[...].reshape(rows, width), other[...].reshape(rows, width), *rest[:-2]
    )
    rest[-2][...] = normed.T
    rest[-1][...] = compressed.T


def project_jobs(values, weights, tables, results, parts):
    blocks, _, rows, width = values.shape
    tile_blocks = 256 // rows
    steps = blocks // tile_blocks // parts
    col = lax.axis_index("col")
    query_width = weights[3].shape[1]

    def job(part):
        def at(step):
            return part * steps + step

        def table(array):
            return (array, (256, array.shape[1]), lambda step: (at(step), 0))

        def whole(array):
            return (array, array.shape, lambda step: (0, 0))

        def run():
            inputs = [
                (values, (tile_blocks, 1, rows, width), lambda step: (at(step), col, 0, 0)),
                (values, (tile_blocks, 1, rows, width), lambda step: (at(step), 1 - col, 0, 0)),
            ]
            weight_inputs = [whole(array) for array in weights]
            weight_inputs[2] = (weights[2], (width, query_width), lambda step: (0, col))
            inputs += weight_inputs + [table(tables)]
            outputs = [table(array) for array in results[:3]]
            outputs += [
                (array, (array.shape[0], 256), lambda step: (0, at(step))) for array in results[3:]
            ]
            pipeline(project_body, (steps,), inputs, outputs)

        return run

    return [job(part) for part in range(parts)]


def attention_jobs(arrays, stream, output_weight, results, groups, parts):
    size = arrays[0].shape[0] // groups
    width = stream.shape[2]
    col = lax.axis_index("col")
    steps = groups // parts

    def job(part):
        def at(step):
            return part * steps + step

        def table(array):
            return (array, (size, array.shape[1]), lambda step: (at(step), 0))

        def run():
            inputs = [table(array) for array in arrays]
            inputs += [
                (stream, (1, size, width), lambda step: (0, at(step), 0)),
                (stream, (1, size, width), lambda step: (1, at(step), 0)),
                (output_weight, (output_weight.shape[0], width), lambda step: (0, col)),
                (output_weight, (output_weight.shape[0], width), lambda step: (0, 1 - col)),
            ]
            outputs = [
                (results[0], (results[0].shape[0], size), lambda step: (0, at(step)))
            ] + [table(array) for array in results[1:]]
            pipeline(attention_body, (steps,), inputs, outputs)

        return run

    return [job(part) for part in range(parts)]


TOTAL = (1024, 1408)


def jobs_kernel(*refs, make_jobs, inputs):
    for job in make_jobs(refs[:inputs], refs[inputs:-1], refs[-1]):
        job()


def run_jobs(make_jobs, operands, shapes):
    return pl.pallas_call(
        functools.partial(jobs_kernel, make_jobs=make_jobs, inputs=len(operands)),
        out_shape=shapes,
        in_specs=[ANY_SPEC] * len(operands),
        out_specs=[ANY_SPEC] * len(shapes),
        scratch_shapes=[pltpu.VMEM(TOTAL, jnp.float32)],
        compiler_params=pltpu.CompilerParams(vmem_limit_bytes=VMEM_LIMIT),
    )(*operands)


def no_jobs(inputs, outputs, total):
    return []


def gather_kernel(*refs, make_jobs, inputs, sems):
    source, job_inputs, target = refs[0], refs[1 : 1 + inputs], refs[1 + inputs]
    total, gather_sems = refs[-sems - 1], refs[-sems:]
    jobs = make_jobs(job_inputs, refs[2 + inputs : -sems - 1], total)
    gather = Gather(
        source, lambda index: target.at[0, index], lambda index: target.at[1, index], gather_sems,
        False,
    )

    def work():
        if jobs:
            jobs.pop(0)()

    enter(peers(True))
    gather.start()
    steps = gather.steps()
    slow = gather.sizes[0]
    for number, step in enumerate(steps):
        if number in (0, slow - 2, slow + 1, 2 * slow):
            work()
        step()
    while jobs:
        work()
    gather.finish()


def gather_everywhere(values, collective_id, make_jobs=no_jobs, operands=(), shapes=()):
    exp_count, row_count = lax.axis_size("exp"), lax.axis_size("row")
    slow = min(4, exp_count)
    fast = exp_count // slow
    rows, width = values.shape
    blocks = exp_count * row_count
    result = jax.ShapeDtypeStruct((2, blocks, rows, width), values.dtype)
    sems = Gather.sems()
    gathered, *others = pl.pallas_call(
        functools.partial(
            gather_kernel, make_jobs=make_jobs, inputs=len(operands), sems=len(sems)
        ),
        out_shape=[result, *shapes],
        in_specs=[ANY_SPEC] * (1 + len(operands)),
        out_specs=[ANY_SPEC] * (1 + len(shapes)),
        scratch_shapes=[pltpu.VMEM(TOTAL, jnp.float32), *sems],
        compiler_params=pltpu.CompilerParams(
            collective_id=collective_id, has_side_effects=True, vmem_limit_bytes=VMEM_LIMIT
        ),
        cost_estimate=pl.CostEstimate(
            flops=0, bytes_accessed=4 * blocks * rows * width * 4, transcendentals=0
        ),
    )(values, *operands)
    return gathered.reshape(2, blocks * rows, width), others


def scatter_kernel(*refs, backward, make_jobs, inputs, outputs):
    if backward:
        gating, upward, gate, up, own_gating, own_upward, shared_gate, shared_up = refs[:8]
        lefts = [gating.at[0], gating.at[1], upward.at[0], upward.at[1]]
        refs = refs[8:]
    else:
        hidden, down, down_other, own_hidden, other_hidden, shared, shared_other = refs[:7]
        lefts = [hidden.at[0], hidden.at[1]]
        refs = refs[7:]
    count = len(lefts)
    job_inputs, result, job_outputs = (
        refs[:inputs], refs[inputs], refs[inputs + 1 : inputs + 1 + outputs]
    )
    refs = refs[inputs + 1 + outputs :]
    (
        left_tiles, rights, extra_left, extra_right, part, from_row, from_fast,
        from_fast_late, from_row_late, from_slow,
        left_sems, right_sems, extra_sems, row_sems, fast_sems, fast_late_sems, row_late_sems,
        slow_sems, job_sems, job_total,
    ) = refs
    (slow_at, fast_at, row_at, col_at), (slow, fast, row_count) = positions()
    slow_ids, fast_ids, row_ids, core_ids = peers(True)
    jobs = make_jobs(job_inputs, job_outputs, job_total, core_ids[0], job_sems)
    exp_count = slow * fast
    exp_index = lax.axis_index("exp")
    rows, width = result.shape
    half = rows // 2
    low, high = pl.ds(0, half), pl.ds(half, half)
    group = rows * row_count
    group_rows = pl.ds(pl.multiple_of(exp_index * group, group), group)
    own_half = pl.ds(pl.multiple_of(col_at * width, width), width)

    def slow_of(turn):
        return (slow_at + 1 + turn) % slow

    def order(step):
        return slow_of(step // fast) * fast + (fast_at + 1 + step % fast) % fast

    def loads(step, slot):
        first = pl.multiple_of(order(step) * group, group)
        return [
            pltpu.make_async_copy(
                left.at[:, pl.ds(first, group)], left_tiles.at[slot, number],
                left_sems.at[slot, number],
            )
            for number, left in enumerate(lefts)
        ]

    if backward:
        right_pairs = [(array.at[side], rights.at[2 * number + side])
                       for number, array in enumerate((gate, up)) for side in range(2)]
        extra_pairs = [
            (own_gating.at[group_rows], extra_left.at[0]),
            (own_upward.at[group_rows], extra_left.at[1]),
            (shared_gate, extra_right.at[0]),
            (shared_up, extra_right.at[1]),
        ]
        extra_product = matmul_right
    else:
        split = down.shape[1]
        right_pairs = []
        for side in range(2):
            for source, place in ((down, col_at), (down_other, 1 - col_at)):
                spot = pl.ds(pl.multiple_of(place * split, 16), split)
                right_pairs.append((source.at[side, :, own_half], rights.at[side, spot]))
        extra_pairs = [
            (own_hidden.at[:, group_rows], extra_left.at[0]),
            (other_hidden, extra_left.at[1]),
            (shared.at[:, own_half], extra_right.at[0]),
            (shared_other.at[:, own_half], extra_right.at[1]),
        ]
        extra_product = matmul_left
    prepared = [
        pltpu.make_async_copy(source, target, right_sems.at[number])
        for number, (source, target) in enumerate(right_pairs)
    ]
    extras = [
        pltpu.make_async_copy(source, target, extra_sems.at[number])
        for number, (source, target) in enumerate(extra_pairs)
    ]
    for copy in prepared + loads(0, 0) + extras:
        copy.start()
    enter((slow_ids, fast_ids, row_ids, core_ids))
    for copy in prepared:
        copy.wait()

    def make(step):
        slot = step % 2

        @pl.when(step + 1 < exp_count)
        def _():
            for copy in loads(step + 1, 1 - slot):
                copy.start()

        for copy in loads(step, slot):
            copy.wait()
        index = order(step)
        total = matmul_left(left_tiles[slot, 0], rights[0])
        for number in range(1, count):
            total = total + matmul_left(left_tiles[slot, number], rights[number])
        part[index] = total.astype(jnp.bfloat16).reshape(row_count, rows, width)

        @pl.when(step == exp_count - 1)
        def _():
            for copy in extras:
                copy.wait()
            extra = extra_product(extra_left[0], extra_right[0])
            extra = extra + extra_product(extra_left[1], extra_right[1])
            before = part[index].astype(jnp.float32)
            part[index] = (before + extra.reshape(before.shape)).astype(jnp.bfloat16)

        for number, device in enumerate(row_ids):
            goal = (row_at + number + 1) % row_count
            remote(
                part.at[index, goal, low], from_row.at[number, index], row_sems,
                (number, index), device,
            )
        slow_index = index // fast
        for number, device in enumerate(fast_ids):

            @pl.when(index % fast == (fast_at + number + 1) % fast)
            def _():
                for goal in range(row_count):
                    remote(
                        part.at[index, goal, high], from_fast.at[number, slow_index, goal],
                        fast_sems, (number, slow_index, goal), device,
                    )

    def add_up(index, goal, span, arrivals):
        total = part[index, goal, span].astype(jnp.float32)
        for buffer, sems, spot in arrivals:
            wait_arrived(buffer.at[spot], sems, spot)
            total = total + buffer[spot].astype(jnp.float32)
        return total

    def of_rows(index):
        return [(from_row, row_sems, (number, index)) for number in range(row_count - 1)]

    def of_fasts(slow_index, goal):
        return [
            (from_fast, fast_sems, (number, slow_index, goal)) for number in range(fast - 1)
        ]

    def second(slow_index):
        for number, device in enumerate(fast_ids):
            index = slow_index * fast + (fast_at + number + 1) % fast
            part[index, row_at, low] = add_up(index, row_at, low, of_rows(index)).astype(
                jnp.bfloat16
            )
            remote(
                part.at[index, row_at, low], from_fast_late.at[number, slow_index],
                fast_late_sems, (number, slow_index), device,
            )
        mine = slow_index * fast + fast_at
        for number, device in enumerate(row_ids):
            goal = (row_at + number + 1) % row_count
            part[mine, goal, high] = add_up(
                mine, goal, high, of_fasts(slow_index, goal)
            ).astype(jnp.bfloat16)
            remote(
                part.at[mine, goal, high], from_row_late.at[number, slow_index],
                row_late_sems, (number, slow_index), device,
            )

    def finish(slow_index, span, late):
        mine = slow_index * fast + fast_at
        if late == 0:
            arrivals = of_rows(mine) + [
                (from_fast_late, fast_late_sems, (number, slow_index))
                for number in range(fast - 1)
            ]
        else:
            arrivals = of_fasts(slow_index, row_at) + [
                (from_row_late, row_late_sems, (number, slow_index))
                for number in range(row_count - 1)
            ]
        return add_up(mine, row_at, span, arrivals)

    def third(number):
        slow_index = slow_of(number)
        mine = slow_index * fast + fast_at
        for late, span in enumerate((low, high)):
            part[mine, row_at, span] = finish(slow_index, span, late).astype(jnp.bfloat16)
            remote(
                part.at[mine, row_at, span], from_slow.at[late, number], slow_sems,
                (late, number), slow_ids[number],
            )

    for turn in range(slow + 1):
        if turn < slow:
            pl.loop(turn * fast, turn * fast + fast)(make)
        if turn >= 1:
            second(slow_of(turn - 1))
        if turn >= 2:
            third(turn - 2)
        if jobs:
            jobs.pop(0)()
    for job in jobs:
        job()
    for late, span in enumerate((low, high)):
        total = finish(slow_at, span, late)
        for number in range(slow - 1):
            wait_arrived(from_slow.at[late, number], slow_sems, (late, number))
            total = total + from_slow[late, number].astype(jnp.float32)
        result[span, :] = total

    @pl.loop(0, exp_count)
    def _(index):
        for number in range(row_count - 1):
            sent(from_row.at[number, index], row_sems, (number, index))

    @pl.loop(0, slow)
    def _(slow_index):
        for number in range(fast - 1):
            for goal in range(row_count):
                spot = (number, slow_index, goal)
                sent(from_fast.at[spot], fast_sems, spot)
            sent(from_fast_late.at[number, slow_index], fast_late_sems, (number, slow_index))
        for number in range(row_count - 1):
            sent(from_row_late.at[number, slow_index], row_late_sems, (number, slow_index))

    for number in range(slow - 1):
        for late in range(2):
            sent(from_slow.at[late, number], slow_sems, (late, number))


def no_scatter_jobs(inputs, outputs, total, core, sems):
    return []


def scatter_products(
    operands, backward, collective_id, make_jobs=no_scatter_jobs, job_operands=(), shapes=()
):
    exp_count, row_count = lax.axis_size("exp"), lax.axis_size("row")
    slow = min(4, exp_count)
    fast = exp_count // slow
    _, units, tokens = operands[0].shape
    rows = tokens // exp_count // row_count
    group = rows * row_count
    half = rows // 2
    kind = jnp.bfloat16
    if backward:
        count, (width, shared_units) = 4, operands[6].shape
        extra_shapes = [(2, group, shared_units), (2, width, shared_units)]
    else:
        count, shared_units, width = 2, operands[5].shape[0], operands[1].shape[2] // 2
        extra_shapes = [(2, shared_units, group), (2, shared_units, width)]
    return pl.pallas_call(
        functools.partial(
            scatter_kernel, backward=backward, make_jobs=make_jobs, inputs=len(job_operands),
            outputs=len(shapes),
        ),
        out_shape=[jax.ShapeDtypeStruct((rows, width), jnp.float32), *shapes],
        in_specs=[ANY_SPEC] * (len(operands) + len(job_operands)),
        out_specs=[pl.BlockSpec(memory_space=pltpu.VMEM)] + [ANY_SPEC] * len(shapes),
        scratch_shapes=[
            pltpu.VMEM((2, count, units, group), kind),
            pltpu.VMEM((count, units, width), kind),
            pltpu.VMEM(extra_shapes[0], kind),
            pltpu.VMEM(extra_shapes[1], kind),
            pltpu.VMEM((exp_count, row_count, rows, width), kind),
            pltpu.VMEM((row_count - 1, exp_count, half, width), kind),
            pltpu.VMEM((fast - 1, slow, row_count, half, width), kind),
            pltpu.VMEM((fast - 1, slow, half, width), kind),
            pltpu.VMEM((row_count - 1, slow, half, width), kind),
            pltpu.VMEM((2, slow - 1, half, width), kind),
            pltpu.SemaphoreType.DMA((2, count)),
            pltpu.SemaphoreType.DMA((4,)),
            pltpu.SemaphoreType.DMA((4,)),
            pltpu.SemaphoreType.DMA((2, row_count - 1, exp_count)),
            pltpu.SemaphoreType.DMA((2, fast - 1, slow, row_count)),
            pltpu.SemaphoreType.DMA((2, fast - 1, slow)),
            pltpu.SemaphoreType.DMA((2, row_count - 1, slow)),
            pltpu.SemaphoreType.DMA((2, 2, slow - 1)),
            pltpu.SemaphoreType.DMA((2, 1)),
            pltpu.VMEM(TOTAL if make_jobs is not no_scatter_jobs else (8, 128), jnp.float32),
        ],
        compiler_params=pltpu.CompilerParams(
            collective_id=collective_id, has_side_effects=True, vmem_limit_bytes=VMEM_LIMIT
        ),
        cost_estimate=pl.CostEstimate(
            flops=2 * tokens * units * width * count,
            bytes_accessed=tokens * units * count * 2 + 60 * 1024 * 1024,
            transcendentals=0,
        ),
    )(*operands, *job_operands)


def unit_grads(gating, upward, grad_hidden):
    bend = 0.5 * jnp.tanh(0.5 * gating)
    sigmoid = 0.5 + bend
    silu = gating * sigmoid
    grad_upward = (grad_hidden * silu).astype(jnp.bfloat16)
    grad_gating = (grad_hidden * upward * (sigmoid + silu * (0.5 - bend))).astype(jnp.bfloat16)
    return silu * upward, grad_gating, grad_upward


def units_kernel(
    mixer_rows, tables, all_grad, layer_rows,
    expert_gate, gate_other, expert_up, up_other, expert_down, down_other,
    shared_gate, shared_gate_other, shared_up, shared_up_other, shared_down, shared_down_other,
    all_mixer, all_rows,
    expert_hidden, expert_gating, expert_upward, shared_hidden, shared_gating, shared_upward,
    mixer_turned,
    gates, ups, downs, shared_gates, shared_ups, shared_downs, inputs, table, tiles, turned_tiles,
    shared_tiles, shared_turned,
    weight_sems, input_sems, local_sems, send_sems, recv_sems, shared_local, shared_send,
    shared_recv, *gather_sems
):
    step = pl.program_id(0)
    steps = pl.num_programs(0)
    (slow_at, fast_at, _, col), (slow, fast, row_count) = positions()
    core = {"col": 1 - col}
    rows, width = mixer_rows.shape
    tile = rows * row_count
    part = tile // 2
    split = expert_down.shape[1]
    shared_split = shared_down.shape[0]
    shared_steps = steps // 2
    halves = [pl.ds(pl.multiple_of(side * width, width), width) for side in (col, 1 - col)]
    targets = [expert_hidden, expert_gating, expert_upward]
    shared_targets = [shared_gating, shared_upward]
    gather = Gather(
        mixer_rows, lambda index: all_mixer.at[0, index], lambda index: all_mixer.at[1, index],
        gather_sems[: len(gather_sems) // 2], False,
    )
    late = Gather(
        layer_rows, lambda index: all_rows.at[index, col],
        lambda index: all_rows.at[index, 1 - col], gather_sems[len(gather_sems) // 2 :], True,
    )

    def line_of(at):
        place = at % slow
        near = [
            sorted(range(slow), key=lambda line, own=own: (abs(line - own), line))
            for own in range(slow)
        ]
        line = jnp.int32(0)
        for own in range(slow):
            for number in range(slow):
                line = line + jnp.where(
                    (slow_at == own) & (place == number), near[own][number], 0
                ).astype(jnp.int32)
        return line

    def group_of(at):
        fast_off = at // slow
        return line_of(at) * fast + (fast_at + fast - fast_off) % fast

    def weight_copies():
        pairs = [
            (expert_gate.at[col], gates.at[0]),
            (gate_other, gates.at[1]),
            (expert_up.at[col], ups.at[0]),
            (up_other, ups.at[1]),
        ]
        own_rows = pl.ds(pl.multiple_of(col * split, 16), split)
        other_rows = pl.ds(pl.multiple_of((1 - col) * split, 16), split)
        shared_own = pl.ds(pl.multiple_of(col * shared_split, 16), shared_split)
        shared_other = pl.ds(pl.multiple_of((1 - col) * shared_split, 16), shared_split)
        for side in range(2):
            pairs += [
                (expert_down.at[col, :, halves[side]], downs.at[side, own_rows]),
                (down_other.at[col, :, halves[side]], downs.at[side, other_rows]),
            ]
        pairs += [
            (shared_gate, shared_gates.at[0]),
            (shared_gate_other, shared_gates.at[1]),
            (shared_up, shared_ups.at[0]),
            (shared_up_other, shared_ups.at[1]),
        ]
        for side in range(2):
            pairs += [
                (shared_down.at[:, halves[side]], shared_downs.at[side, shared_own]),
                (shared_down_other.at[:, halves[side]], shared_downs.at[side, shared_other]),
            ]
        return [
            pltpu.make_async_copy(src, dst, weight_sems.at[number])
            for number, (src, dst) in enumerate(pairs)
        ]

    def known_copies(at):
        group = group_of(at)
        slot = at % 3
        blocks = pl.ds(group * row_count, row_count)
        span = pl.ds(pl.multiple_of(group * tile, tile), tile)
        return [
            pltpu.make_async_copy(
                all_grad.at[blocks, side], inputs.at[slot, 2 + number],
                input_sems.at[slot, 2 + number],
            )
            for number, side in enumerate((col, 1 - col))
        ] + [pltpu.make_async_copy(tables.at[span], table.at[slot], input_sems.at[slot, 4])]

    def mixer_copies(at):
        slot = at % 3
        blocks = pl.ds(group_of(at) * row_count, row_count)
        return [
            pltpu.make_async_copy(
                all_mixer.at[side, blocks], inputs.at[slot, side], input_sems.at[slot, side]
            )
            for side in range(2)
        ]

    def results(at, slot):
        columns = pl.ds(pl.multiple_of(group_of(at) * tile, tile), tile)
        local, far = [], []
        for number, target in enumerate(targets):
            spot = target.at[col, :, columns]
            local.append(
                pltpu.make_async_copy(tiles.at[slot, number], spot, local_sems.at[slot, number])
            )
            far.append(
                pltpu.make_async_remote_copy(
                    src_ref=tiles.at[slot, number],
                    dst_ref=spot,
                    send_sem=send_sems.at[slot, number],
                    recv_sem=recv_sems.at[number, at],
                    device_id=core,
                    device_id_type=MESH,
                )
            )
        local.append(
            pltpu.make_async_copy(
                turned_tiles.at[slot], mixer_turned.at[:, columns], local_sems.at[slot, 3]
            )
        )
        return local, far

    def shared_span(turn, member, side):
        first = group_of(2 * turn + member) * tile + side * part
        return pl.ds(pl.multiple_of(first, part), part)

    def shared_results(turn, slot):
        own_rows = pl.ds(pl.multiple_of(col * shared_split, 16), shared_split)
        other_rows = pl.ds(pl.multiple_of((1 - col) * shared_split, 16), shared_split)
        local, far = [], []
        for member in range(2):
            span = shared_span(turn, member, col)
            here = pl.ds(member * part, part)
            triples = [
                (shared_tiles.at[slot, number, here], target.at[span],
                 shared_tiles.at[slot, number, here])
                for number, target in enumerate(shared_targets)
            ]
            triples.append(
                (shared_turned.at[slot, own_rows, here], shared_hidden.at[:, span],
                 shared_turned.at[slot, other_rows, here])
            )
            for number, (near, goal, away) in enumerate(triples):
                local.append(
                    pltpu.make_async_copy(near, goal, shared_local.at[slot, member, number])
                )
                far.append(
                    pltpu.make_async_remote_copy(
                        src_ref=away,
                        dst_ref=goal,
                        send_sem=shared_send.at[slot, member, number],
                        recv_sem=shared_recv.at[number, member, turn],
                        device_id=core,
                        device_id_type=MESH,
                    )
                )
        return local, far

    def wait_out(pair):
        local, far = pair
        for copy in local:
            copy.wait()
        for copy in far:
            copy.wait_send()

    def fetch(at):
        gather.ready(line_of(at), at // slow)
        for copy in mixer_copies(at):
            copy.start()

    weights_early = 8

    @pl.when(step == 0)
    def _():
        for copy in weight_copies()[:weights_early] + known_copies(0):
            copy.start()
        enter(peers(True))
        gather.start()
        for copy in weight_copies()[weights_early:]:
            copy.start()
        gather.corner(0)
        gather.hop(1)
        gather.keep().wait()
        fetch(0)
        for copy in weight_copies()[:weights_early]:
            copy.wait()

    slot = step % 2

    @pl.when(step + 1 < steps)
    def _():
        for copy in known_copies(step + 1):
            copy.start()

    @pl.when(step >= 2)
    def _():
        wait_out(results(step - 2, slot))

    for copy in known_copies(step) + mixer_copies(step):
        copy.wait()

    def block(at, number):
        return inputs[at % 3, number].reshape(tile, width)

    mixers = (block(step, 0), block(step, 1))
    grads = (block(step, 2), block(step, 3))
    turned_tiles[slot] = mixers[0].T

    def both(pair, weights, product):
        return product(pair[0], weights[0]) + product(pair[1], weights[1])

    def turned(weights, pair):
        return matmul_right(weights[0], pair[0]) + matmul_right(weights[1], pair[1])

    columns = table[step % 3].T
    own_expert = (lax.axis_index("exp") * expert_down.shape[0] + col).astype(jnp.float32)
    chosen = columns[TABLE["ids"] : TABLE["ids"] + TOP]
    router = columns[TABLE["router"] : TABLE["router"] + TOP]
    scale = jnp.sum(jnp.where(chosen == own_expert, router, 0.0), axis=0, keepdims=True)
    hidden, gating, upward = unit_grads(
        turned(gates, mixers), turned(ups, mixers), turned(downs, grads) * scale
    )
    tiles[slot, 0] = (hidden * scale).astype(jnp.bfloat16)
    tiles[slot, 1] = gating
    tiles[slot, 2] = upward
    local, far = results(step, slot)
    for copy in local + far:
        copy.start()

    def acts(*number_and_acts):
        for number, chosen in number_and_acts:

            @pl.when(step == number)
            def _():
                for act, *arguments in chosen:
                    act(*arguments)

    def wait_weights():
        for copy in weight_copies()[weights_early:]:
            copy.wait()

    acts(
        (0, [(gather.hop, 2), (gather.corner, 1), (gather.hop, 3), (wait_weights,)]),
        (1, [(gather.corner, 2), (gather.last, 0)]),
        (2, [(gather.corner, 3), (gather.last, 1), (late.start,)]),
        (3, [(gather.last, 2), (late.hop, 1)]),
        (4, [(gather.last, 3), (late.hop, 2)]),
        (5, [(late.hop, 3), (late.corner, 0)]),
        (6, [(late.corner, 1), (late.corner, 2), (late.last, 0)]),
        (7, [(late.corner, 3), (late.last, 1)]),
    )

    @pl.when(step + 1 < steps)
    def _():
        fetch(step + 1)

    @pl.when(step % 2 == 1)
    def _():
        turn = step // 2
        turn_slot = turn % 2

        @pl.when(turn >= 2)
        def _():
            wait_out(shared_results(turn - 2, turn_slot))

        first = col * (row_count // 2)

        def pick(number):
            wanted = pl.ds(first, row_count // 2)
            return jnp.concatenate(
                [
                    inputs[at % 3, number, wanted].reshape(part, width)
                    for at in (step - 1, step)
                ],
                axis=0,
            )

        chosen_rows = [pick(number) for number in range(4)]
        hidden, gating, upward = unit_grads(
            both(chosen_rows[:2], shared_gates, matmul),
            both(chosen_rows[:2], shared_ups, matmul),
            both(chosen_rows[2:], shared_downs, matmul_right),
        )
        shared_tiles[turn_slot, 0] = gating
        shared_tiles[turn_slot, 1] = upward
        shared_turned[turn_slot] = hidden.astype(jnp.bfloat16).T
        local, far = shared_results(turn, turn_slot)
        for copy in local + far:
            copy.start()

    @pl.when(step == steps - 1)
    def _():
        for back in range(2):
            at = steps - 1 - back
            wait_out(results(at, at % 2))
            turn = shared_steps - 1 - back
            wait_out(shared_results(turn, turn % 2))

        @pl.loop(0, steps)
        def _(at):
            columns = pl.ds(pl.multiple_of(group_of(at) * tile, tile), tile)
            for number, target in enumerate(targets):
                spot = target.at[1 - col, :, columns]
                pltpu.make_async_copy(spot, spot, recv_sems.at[number, at]).wait()

        @pl.loop(0, shared_steps)
        def _(turn):
            for member in range(2):
                span = shared_span(turn, member, 1 - col)
                spots = [target.at[span] for target in shared_targets]
                spots.append(shared_hidden.at[:, span])
                for number, spot in enumerate(spots):
                    pltpu.make_async_copy(
                        spot, spot, shared_recv.at[number, member, turn]
                    ).wait()

        gather.finish(True)
        late.last(2)
        late.last(3)
        late.finish()


def run_units(mixer_rows, tables, grad, layer_rows, weights, collective_id):
    rows, width = mixer_rows.shape
    exp_count, row_count = lax.axis_size("exp"), lax.axis_size("row")
    tokens = tables.shape[0]
    tile = rows * row_count
    units = weights[0].shape[1]
    shared_units = weights[6].shape[1]
    kind = jnp.bfloat16
    pair = jax.ShapeDtypeStruct((2, units, tokens), kind)
    shared = jax.ShapeDtypeStruct((tokens, shared_units), kind)
    half = jax.ShapeDtypeStruct((shared_units // 2, tokens), kind)
    steps = exp_count
    dma = pltpu.SemaphoreType.DMA
    mixer, *others = pl.pallas_call(
        units_kernel,
        out_shape=[
            jax.ShapeDtypeStruct((2, exp_count * row_count, rows, width), kind),
            jax.ShapeDtypeStruct(grad.shape, kind),
            pair, pair, pair, half, shared, shared, jax.ShapeDtypeStruct((width, tokens), kind),
        ],
        grid=(steps,),
        in_specs=[ANY_SPEC] * (len(weights) + 4),
        out_specs=[ANY_SPEC] * 9,
        scratch_shapes=[
            pltpu.VMEM((2, units, width), kind),
            pltpu.VMEM((2, units, width), kind),
            pltpu.VMEM((2, units, width), kind),
            pltpu.VMEM((2, width, shared_units), kind),
            pltpu.VMEM((2, width, shared_units), kind),
            pltpu.VMEM((2, shared_units, width), kind),
            pltpu.VMEM((3, 4, row_count, rows, width), kind),
            pltpu.VMEM((3, tile, 128), jnp.float32),
            pltpu.VMEM((2, 3, units, tile), kind),
            pltpu.VMEM((2, width, tile), kind),
            pltpu.VMEM((2, 2, tile, shared_units), kind),
            pltpu.VMEM((2, shared_units, tile), kind),
            dma((16,)),
            dma((3, 5)),
            dma((2, 4)),
            dma((2, 3)),
            dma((3, steps)),
            dma((2, 2, 3)),
            dma((2, 2, 3)),
            dma((3, 2, steps // 2)),
            *Gather.sems(),
            *Gather.sems(),
        ],
        compiler_params=pltpu.CompilerParams(
            collective_id=collective_id, has_side_effects=True, vmem_limit_bytes=VMEM_LIMIT
        ),
        cost_estimate=pl.CostEstimate(
            flops=2 * tokens * units * width * 2 * 6,
            bytes_accessed=50 * 1024 * 1024,
            transcendentals=2 * tokens * units,
        ),
    )(mixer_rows, tables, grad, layer_rows, *weights)
    return mixer.reshape(2, tokens, width), *others


def tail_kernel(
    rows, inverse_one, gain, grad_hidden, sums_in, latent_normed, latent_scale, latent_gain,
    keyvalue_weight, query_other, latent_weight,
    grad_query, grad_keyvalue, grad_rope, query_weight,
    attended_turned, stream, attention_turned, compressed_turned,
    input_grad, sums, latent_all, output_weight_grad, keyvalue_weight_grad, query_weight_grad,
    queries, keyvalues, ropes, query_own, latent_out, latent_in, latent_row_in, wide_out, wide_in,
    wide_rows, wide_row_in, latent_block, squares, squares_in,
    running, slow_in, fast_in, row_in, core_in,
    total_scratch,
    local_sems, core_sems, row_sems, slow_sums, fast_sums, row_sums, core_sums, *gather_sems,
    fused
):
    (slow_at, fast_at, row_at, col_at), (slow, fast, row_count) = positions()
    slow_ids, fast_ids, row_ids, core_ids = peers(True)
    core = core_ids[0]
    count, width = rows.shape
    group = row_count * count
    group_rows = pl.ds(pl.multiple_of(lax.axis_index("exp") * group, group), group)
    query_width = query_own.shape[1]
    jobs = []
    if fused:
        jobs = weight_jobs(
            (
                attended_turned, stream, attention_turned, compressed_turned, grad_query,
                grad_keyvalue,
            ),
            (output_weight_grad, keyvalue_weight_grad, query_weight_grad),
            total_scratch,
        )

    def work():
        if jobs:
            jobs.pop(0)()

    own_heads = pl.ds(pl.multiple_of(col_at * query_width, query_width), query_width)
    loads = [
        pltpu.make_async_copy(source, target, local_sems.at[number])
        for number, (source, target) in enumerate(
            (
                (grad_keyvalue.at[group_rows], keyvalues),
                (grad_rope.at[group_rows], ropes),
                (grad_query.at[0, group_rows], queries),
                (query_weight.at[:, own_heads], query_own),
            )
        )
    ]
    for copy in loads:
        copy.start()
    enter((slow_ids, fast_ids, row_ids, core_ids))
    for copy in loads:
        copy.wait()
    compressed = matmul_right(keyvalues[...], keyvalue_weight[...])
    unit = latent_normed[...]
    scaled = compressed * latent_gain[:1]
    inner = jnp.mean(scaled * unit, axis=1, keepdims=True)
    raw = latent_scale[...] * (scaled - unit * inner)
    latent_out[0] = jnp.concatenate([raw, ropes[...]], axis=1).astype(jnp.bfloat16)
    started = [remote(latent_out.at[0], latent_in, core_sems, (0,), core)]
    wide_out[...] = matmul_right(queries[...], query_other[...]).astype(jnp.bfloat16)
    started.append(remote(wide_out, wide_in, core_sems, (1,), core))
    latent_gain_part = jnp.sum(compressed * unit, axis=0, keepdims=True)
    own_wide = matmul_right(queries[...], query_own[...])
    wait_arrived(latent_in, core_sems, (0,))
    latent_out[1] = (
        latent_out[0].astype(jnp.float32) + latent_in[...].astype(jnp.float32)
    ).astype(jnp.bfloat16)
    for number, device in enumerate(row_ids):
        started.append(
            remote(latent_out.at[1], latent_row_in.at[number], row_sems, (0, number), device)
        )
    wait_arrived(wide_in, core_sems, (1,))
    own_wide = own_wide + wide_in[...].astype(jnp.float32)
    wide_rows[...] = own_wide.astype(jnp.bfloat16).reshape(wide_rows.shape)
    for number, device in enumerate(row_ids):
        goal = (row_at + number + 1) % row_count
        started.append(
            remote(wide_rows.at[goal], wide_row_in.at[number], row_sems, (1, number), device)
        )
    work()
    latent = latent_out[1].astype(jnp.float32)
    for number in range(row_count - 1):
        wait_arrived(latent_row_in.at[number], row_sems, (0, number))
        latent = latent + latent_row_in[number].astype(jnp.float32)
    latent_out[2] = latent.astype(jnp.bfloat16)
    part = count // 2
    first = pl.multiple_of(row_at * count, count)
    latent_block[...] = latent_out[2, pl.ds(pl.multiple_of(first + col_at * part, part), part)]
    gather = Gather(
        latent_block, lambda index: latent_all.at[index, col_at],
        lambda index: latent_all.at[index, 1 - col_at], gather_sems, True,
    )
    gather.start()
    steps = gather.steps()
    gradient = matmul(latent_out[2, pl.ds(first, count)], latent_weight[...])
    gradient = gradient + wide_rows[row_at].astype(jnp.float32)
    for number in range(row_count - 1):
        wait_arrived(wide_row_in.at[number], row_sems, (1, number))
        gradient = gradient + wide_row_in[number].astype(jnp.float32)
    scale = inverse_one[:, :1]
    normed = rows[...].astype(jnp.float32) * scale
    scaled = gradient * gain[:1]
    squares[...] = jnp.broadcast_to(
        jnp.sum(scaled * normed, axis=1, keepdims=True), squares.shape
    )
    started.append(remote(squares, squares_in, core_sems, (2,), core))
    steps.pop(0)()
    gain_part = jnp.sum(gradient * normed, axis=0, keepdims=True)
    row = lax.broadcasted_iota(jnp.int32, sums_in.shape, 0)
    padded = jnp.concatenate(
        [latent_gain_part, jnp.zeros((1, width - latent_gain_part.shape[1]), jnp.float32)], axis=1
    )
    total = jnp.where(row == 0, gain_part, jnp.where(row == 2, padded, sums_in[...]))
    wait_arrived(squares_in, core_sems, (2,))
    inner = (squares[...] + squares_in[...])[:, :1] / (2 * width)
    input_grad[...] = grad_hidden[...] + scale * (scaled - normed * inner)
    work()
    stages = (
        (slow_ids, slow_in, slow_sums),
        (fast_ids, fast_in, fast_sums),
        (row_ids, row_in, row_sums),
        (core_ids, core_in, core_sums),
    )
    for stage, (devices, buffer, sems) in enumerate(stages):
        running[stage] = total
        for number, device in enumerate(devices):
            started.append(
                remote(running.at[stage], buffer.at[number], sems, (number,), device)
            )
        steps.pop(0)()
        for number in range(len(devices)):
            wait_arrived(buffer.at[number], sems, (number,))
            arrived = buffer[number]
            total = total + (jnp.where(row == 2, arrived, 0.0) if stage == 3 else arrived)
    sums[...] = total
    for step in steps[: slow - 1]:
        step()
    while jobs:
        work()
    for step in steps[slow - 1 :]:
        step()
    gather.finish()
    for copy in started:
        copy.wait_send()


def weight_jobs(inputs, outputs, total):
    attended, stream, turned, small_turned, query_both, keyvalue = inputs
    return [
        row_job(small_turned, keyvalue, outputs[1], total),
        sided_job(attended, stream, outputs[0], total),
        sided_job(turned, query_both, outputs[2], total),
    ]


def tail(operands, shapes, fused, collective_id):
    exp_count, row_count = lax.axis_size("exp"), lax.axis_size("row")
    slow = min(4, exp_count)
    fast = exp_count // slow
    rows = operands[0]
    count, width = rows.shape
    group = row_count * count
    latent_width = operands[10].shape[0]
    query_width, keyvalue_width = operands[9].shape[1], operands[8].shape[1]
    low, high = jnp.bfloat16, jnp.float32
    vmem = pl.BlockSpec(memory_space=pltpu.VMEM)
    dma = pltpu.SemaphoreType.DMA
    sums = (8, width)
    counts = (slow - 1, fast - 1, row_count - 1, 1)
    return pl.pallas_call(
        functools.partial(tail_kernel, fused=fused),
        out_shape=[
            jax.ShapeDtypeStruct((count, width), high),
            jax.ShapeDtypeStruct(sums, high),
            jax.ShapeDtypeStruct((exp_count * row_count, 2, count // 2, latent_width), low),
            *shapes,
        ],
        in_specs=[vmem] * 11 + [ANY_SPEC] * 8,
        out_specs=[vmem, vmem] + [ANY_SPEC] * 4,
        scratch_shapes=[
            pltpu.VMEM((group, query_width), low),
            pltpu.VMEM((group, keyvalue_width), low),
            pltpu.VMEM((group, DR), high),
            pltpu.VMEM((width, query_width), low),
            pltpu.VMEM((3, group, latent_width), low),
            pltpu.VMEM((group, latent_width), low),
            pltpu.VMEM((row_count - 1, group, latent_width), low),
            pltpu.VMEM((group, width), low),
            pltpu.VMEM((group, width), low),
            pltpu.VMEM((row_count, count, width), low),
            pltpu.VMEM((row_count - 1, count, width), low),
            pltpu.VMEM((count // 2, latent_width), low),
            pltpu.VMEM((count, 128), high),
            pltpu.VMEM((count, 128), high),
            pltpu.VMEM((4, *sums), high),
            *[pltpu.VMEM((number, *sums), high) for number in counts],
            pltpu.VMEM(TOTAL if fused else (8, 128), high),
            dma((4,)),
            dma((2, 3)),
            dma((2, 2, row_count - 1)),
            *[dma((2, number)) for number in counts],
            *Gather.sems(),
        ],
        compiler_params=pltpu.CompilerParams(
            collective_id=collective_id, has_side_effects=True, vmem_limit_bytes=VMEM_LIMIT
        ),
    )(*operands)


def local(
    layer_input,
    attention_gain,
    query_weight,
    latent_weight,
    latent_gain,
    keyvalue_weight,
    output_weight,
    feedforward_gain,
    shared_gate,
    shared_up,
    shared_down,
    expert_gate,
    expert_up,
    expert_down,
    sequence_lengths,
    expert_ids,
    expert_weights,
    output_grad,
):
    exp_index, row_index, col_index = (
        lax.axis_index("exp"),
        lax.axis_index("row"),
        lax.axis_index("col"),
    )
    exp_count = lax.axis_size("exp")
    local_tokens, half_width = layer_input.shape
    full_width = 2 * half_width
    per_device = expert_gate.shape[0]
    group_size = local_tokens * lax.axis_size("row")
    tokens = group_size * exp_count
    group_start = exp_index * group_size

    def part_of(array, side, axis):
        width = array.shape[axis] // 2
        return lax.dynamic_slice_in_dim(array, side * width, width, axis)

    def split_exchange(array, axis):
        return part_of(array, col_index, axis), swap_core(part_of(array, 1 - col_index, axis))

    def own_rows(array):
        return lax.dynamic_slice_in_dim(array, group_start, group_size, 0)

    col = col_index.reshape(1)
    top = expert_ids.shape[1]
    _, places = sequence_layout(sequence_lengths[0], group_size)
    cosine, sine = rope_tables(places)
    first_key = jnp.arange(group_size, dtype=jnp.int32) - places

    def widened(array, width):
        return jnp.pad(array.astype(jnp.float32), ((0, 0), (0, width - array.shape[1])))

    tables = jnp.concatenate(
        [
            widened(expert_ids, 8),
            widened(expert_weights, 8),
            widened(first_key[:, None], 16),
            cosine,
            sine,
            jnp.zeros((group_size, 32), jnp.float32),
        ],
        axis=1,
    )
    latent_turned = latent_weight.T
    gate_turned, up_turned = expert_gate.swapaxes(1, 2), expert_up.swapaxes(1, 2)
    gain_own = jnp.broadcast_to(attention_gain.astype(jnp.float32), (8, half_width))
    latent_gains = jnp.broadcast_to(latent_gain.astype(jnp.float32), (8, R))

    gain_two = feedforward_gain.astype(jnp.float32)
    (
        own_normed, own_scale, inverse_one, hidden_state, normed_two, scale_two, mixer_input,
        tables_all, grad_all, query_other, latent_other, gain_other,
        gate_other, up_other, down_other, shared_gate_other, shared_up_other, shared_down_other,
    ) = prologue(
        layer_input, gain_own, latent_gains, keyvalue_weight, output_weight,
        gain_two[None], tables, query_weight, latent_turned, output_grad,
        (gate_turned, up_turned, expert_down, shared_gate, shared_up, shared_down), 6,
    )
    scale_two = scale_two[:, :1]
    weights = (
        gain_own, gain_other, query_weight, query_other, latent_turned, latent_other,
        latent_gains, keyvalue_weight,
    )
    tables_all = tables_all.reshape(tokens, -1)
    (
        mixer, input_all, both_hidden, both_gating, both_upward, shared_hidden, shared_gating,
        shared_upward, mixer_turned,
    ) = run_units(
        mixer_input,
        tables_all,
        grad_all,
        layer_input,
        (
            gate_turned, gate_other, up_turned, up_other, expert_down, down_other,
            shared_gate, shared_gate_other, shared_up, shared_up_other,
            shared_down, shared_down_other,
        ),
        1,
    )
    fused = tokens <= 2048
    low = jnp.bfloat16

    def shape(*sizes, kind=low):
        return jax.ShapeDtypeStruct(sizes, kind)

    units, shared_units = gate_turned.shape[1], shared_gate.shape[1]

    def gate_jobs(inputs, outputs, total, *_):
        gating, upward, rows, rows_turned, own_gating, own_upward = inputs
        return [
            stacked_job(gating, rows, outputs[0], total),
            stacked_job(upward, rows, outputs[1], total),
            row_job(rows_turned, own_gating, outputs[2], total),
            row_job(rows_turned, own_upward, outputs[3], total),
        ]

    gate_operands = (
        both_gating, both_upward, mixer, mixer_turned, shared_gating, shared_upward
    )
    gate_shapes = [shape(per_device, units, half_width)] * 2 + [
        shape(half_width, shared_units)
    ] * 2
    products = (
        both_gating, both_upward, gate_turned, up_turned, shared_gating, shared_upward,
        shared_gate, shared_up,
    )
    if fused:
        mixer_grad, *gate_grads = scatter_products(
            products, True, 2, gate_jobs, gate_operands, gate_shapes
        )
    else:
        (mixer_grad,) = scatter_products(products, True, 2)
        gate_grads = run_jobs(gate_jobs, gate_operands, gate_shapes)

    upstream = output_grad.astype(jnp.float32)
    grad_norm_two, gain_two_grad = norm_backward(mixer_grad, normed_two, scale_two, gain_two)
    grad_hidden = upstream + grad_norm_two

    heads_width = keyvalue_weight.shape[1] // 2
    query_width = query_weight.shape[1] // 2

    def stream_jobs(inputs, outputs, total):
        hidden, own_hidden, grads, values = inputs[:4]
        return [
            expert_down_job(hidden, grads, outputs[0], total),
            shared_down_job(own_hidden, grads, outputs[1], total),
            *project_jobs(values, inputs[4:12], inputs[12], outputs[2:], 2),
        ]

    stream_operands = (
        both_hidden, shared_hidden, grad_all, input_all, *weights, tables_all
    )
    stream_shapes = [
        shape(*expert_down.shape),
        shape(*shared_down.shape),
        shape(tokens, query_width),
        shape(tokens, keyvalue_weight.shape[1]),
        shape(tokens, DR),
        shape(half_width, tokens),
        shape(R, tokens),
    ]
    stream_input = grad_hidden.astype(jnp.bfloat16)
    if fused:
        stream, results = gather_everywhere(
            stream_input, 3, stream_jobs, stream_operands, stream_shapes
        )
    else:
        stream, _ = gather_everywhere(stream_input, 3)
        results = run_jobs(stream_jobs, stream_operands, stream_shapes)
    (
        expert_down_grad, shared_down_grad, query_all, keyvalue_all, rope_key_all,
        attention_turned, compressed_turned,
    ) = results

    other_hidden = swap_core(
        lax.dynamic_slice_in_dim(shared_hidden, group_start, group_size, 1)
    )

    def attention_part(inputs, outputs, total, core, sems):
        arrays, (stream_ref, weight) = inputs[:4], inputs[4:]
        attended_ref, query_both, keyvalue_ref, rope_ref = outputs
        jobs = attention_jobs(
            arrays, stream_ref, weight,
            (attended_ref, query_both.at[0], keyvalue_ref, rope_ref), exp_count, 4,
        )

        def exchange():
            remote(query_both.at[0], query_both.at[1], sems, (0,), core).wait()

        return [*jobs, exchange]

    weight_shapes = [
        shape(*output_weight.shape), shape(*keyvalue_weight.shape), shape(*query_weight.shape)
    ]
    (
        produced, attended_turned, query_grads, grad_keyvalue, grad_rope
    ) = scatter_products(
        (
            both_hidden, expert_down, down_other, shared_hidden, other_hidden,
            shared_down, shared_down_other,
        ),
        False,
        4,
        attention_part,
        (
            tables_all, query_all, keyvalue_all, rope_key_all, stream, output_weight,
        ),
        [
            shape(heads_width, tokens),
            shape(2, tokens, query_width),
            shape(tokens, keyvalue_weight.shape[1]),
            shape(tokens, DR, kind=jnp.float32),
        ],
    )
    layer_result = (hidden_state + produced).astype(jnp.bfloat16)
    sums_in = jnp.pad(gain_two_grad[None], ((1, 6), (0, 0)))
    weight_operands = (attended_turned, stream, attention_turned, compressed_turned)
    input_grad, sums, latent_all, *weight_grads = tail(
        (
            layer_input, inverse_one, gain_own, grad_hidden, sums_in, own_normed, own_scale,
            latent_gains, keyvalue_weight, query_other, latent_turned,
            query_grads, grad_keyvalue, grad_rope, query_weight, *weight_operands,
        ),
        weight_shapes,
        fused,
        5,
    )
    if not fused:
        weight_grads = run_jobs(
            weight_jobs, (*weight_operands, query_grads, grad_keyvalue), weight_shapes
        )
    output_weight_grad, keyvalue_weight_grad, query_weight_grad = weight_grads
    latent_weight_grad = matmul(attention_turned, latent_all.reshape(tokens, -1))
    wide = [
        array.astype(jnp.float32)
        for array in (
            query_weight_grad, keyvalue_weight_grad, output_weight_grad, *gate_grads,
            shared_down_grad, expert_down_grad,
        )
    ]
    return (
        layer_result,
        input_grad,
        sums[0],
        wide[0],
        latent_weight_grad,
        sums[2, : latent_gain.shape[0]],
        wide[1],
        wide[2],
        sums[1],
        wide[5],
        wide[6],
        wide[7],
        wide[3].swapaxes(1, 2),
        wide[4].swapaxes(1, 2),
        wide[8],
    )


def solution(mesh):
    in_specs = (
        P(("exp", "row"), "col"),
        P("col"),
        P("col", "row"),
        P("col", None),
        P(),
        P(None, ("row", "col")),
        P(("row", "col"), None),
        P("col"),
        P("col", "row"),
        P("col", "row"),
        P(("row", "col"), None),
        P("exp", "col", "row"),
        P("exp", "col", "row"),
        P("exp", ("row", "col"), None),
        P("exp", None),
        P("exp", None),
        P("exp", None),
        P(("exp", "row"), "col"),
    )
    out_specs = (
        P(("exp", "row"), "col"),
        P(("exp", "row"), "col"),
        P("col"),
        P("col", "row"),
        P("col", None),
        P(),
        P(None, ("row", "col")),
        P(("row", "col"), None),
        P("col"),
        P("col", "row"),
        P("col", "row"),
        P(("row", "col"), None),
        P("exp", "col", "row"),
        P("exp", "col", "row"),
        P("exp", ("row", "col"), None),
    )
    return jax.shard_map(local, mesh=mesh, in_specs=in_specs, out_specs=out_specs, check_vma=False)
```

```python
import functools

import jax
import jax.numpy as jnp
from jax import lax
from jax.experimental import pallas as pl
from jax.experimental.pallas import tpu as pltpu
from jax.sharding import PartitionSpec as P

DN = 128
DR = 64
DV = 128
R = 512
TOP = 6


EPSILON = 1e-06
ROPE_BASE = 50000.0
NEGATIVE = -1e30


def matmul(former, latter):
    return jnp.dot(former, latter, preferred_element_type=jnp.float32)


def matmul_left(former, latter):
    return lax.dot_general(
        former, latter, (((0,), (0,)), ((), ())), preferred_element_type=jnp.float32
    )


def matmul_right(former, latter):
    return lax.dot_general(
        former, latter, (((1,), (1,)), ((), ())), preferred_element_type=jnp.float32
    )


def sequence_layout(lengths, group_size):
    seq_ends = jnp.cumsum(lengths)
    token_order = jnp.arange(group_size, dtype=jnp.int32)
    segment = jnp.sum((token_order[:, None] >= seq_ends[None, :]).astype(jnp.int32), axis=1)
    seq_starts = seq_ends - lengths
    own_start = jnp.sum(
        jnp.where(
            segment[:, None] == jnp.arange(lengths.shape[0], dtype=jnp.int32)[None, :],
            seq_starts[None, :],
            0,
        ),
        axis=1,
    )
    return (segment, token_order - own_start)


def rope_tables(places):
    inverse_frequency = ROPE_BASE ** (-(jnp.arange(DR // 2, dtype=jnp.float32) * 2.0 / DR))
    angles = places.astype(jnp.float32)[:, None] * inverse_frequency[None, :]
    return (jnp.cos(angles), jnp.sin(angles))


MESH = pl.DeviceIdType.MESH
VMEM_LIMIT = 60 * 1024 * 1024
LOG2_E = 1.4426950408889634


def full_spec(array):
    zeros = (0,) * array.ndim
    return pl.BlockSpec(array.shape, lambda *_: zeros)


ANY_SPEC = pl.BlockSpec(memory_space=pl.ANY)


def swap_core(values):
    return lax.ppermute(values, "col", [(0, 1), (1, 0)])


def half_sums(values):
    return lax.psum(values, "col")


def norm_backward(gradient, normed, inverse_rms, gain_vector):
    full_width = normed.shape[1] * lax.axis_size("col")
    scaled = gradient * gain_vector
    inner_sum = half_sums(jnp.sum(scaled * normed, axis=1)) / full_width
    return (
        inverse_rms * (scaled - normed * inner_sum[:, None]),
        jnp.sum(gradient * normed, axis=0),
    )


TABLE = dict(ids=0, router=8, first=16, cosine=32, sine=64)


def rotary_tables(table):
    cosine = table[:, TABLE["cosine"] : TABLE["cosine"] + DR // 2]
    sine = table[:, TABLE["sine"] : TABLE["sine"] + DR // 2]
    return jnp.concatenate([cosine, cosine], axis=1), jnp.concatenate([-sine, sine], axis=1)


def first_keys(table):
    return table[:, TABLE["first"] : TABLE["first"] + 1].astype(jnp.int32)


def rotary(values, cosine_both, sine_signed):
    half = values.shape[-1] // 2
    swapped = jnp.concatenate([values[:, half:], values[:, :half]], axis=-1)
    return values * cosine_both + swapped * sine_signed


def project_rows(
    rows_own, rows_other, gain_own, gain_other, query_own, query_other, latent_own, latent_other,
    latent_gain, keyvalue_weight, table, query, keyvalue, rope_key
):
    rows_own = rows_own.astype(jnp.float32)
    rows_other = rows_other.astype(jnp.float32)
    total = jnp.sum(rows_own * rows_own, axis=1, keepdims=True)
    total = total + jnp.sum(rows_other * rows_other, axis=1, keepdims=True)
    scale = lax.rsqrt(total / (2 * rows_own.shape[1]) + EPSILON)
    rows_own = (rows_own * scale * gain_own[:1]).astype(jnp.bfloat16)
    rows_other = (rows_other * scale * gain_other[:1]).astype(jnp.bfloat16)
    queries = matmul(rows_own, query_own[...]) + matmul(rows_other, query_other[...])
    cosine, sine = rotary_tables(table)
    for first in range(0, query.shape[1], DN + DR):
        rope = rotary(queries[:, first + DN : first + DN + DR], cosine, sine)
        query[:, first : first + DN + DR] = jnp.concatenate(
            [queries[:, first : first + DN], rope], axis=1
        ).astype(jnp.bfloat16)
    latent = matmul_right(rows_own, latent_own[...]) + matmul_right(rows_other, latent_other[...])
    raw = latent[:, :R]
    latent_scale = lax.rsqrt(jnp.mean(raw * raw, axis=1, keepdims=True) + EPSILON)
    latent_normed = raw * latent_scale
    compressed = (latent_normed * latent_gain[:1]).astype(jnp.bfloat16)
    keyvalue[...] = matmul(compressed, keyvalue_weight[...]).astype(jnp.bfloat16)
    rope_key[...] = rotary(latent[:, R:], cosine, sine).astype(jnp.bfloat16)
    return rows_own, compressed, latent_normed, latent_scale, scale


def softmax_parts(queries, keys, bias):
    scores = matmul_right(queries, keys) * ((DN + DR) ** (-0.5) * LOG2_E) + bias
    exponent = jnp.exp2(scores - jnp.max(scores, axis=1, keepdims=True))
    return exponent * (1.0 / jnp.sum(exponent, axis=1, keepdims=True))


def mask_bias(first_key):
    size = first_key.shape[0]
    row = lax.broadcasted_iota(jnp.int32, (size, size), 0)
    column = lax.broadcasted_iota(jnp.int32, (size, size), 1)
    return jnp.where((column <= row) & (column >= first_key), 0.0, NEGATIVE)


def head_keys(keyvalue, rope_keys, head):
    first = head * (DN + DV)
    keys = jnp.concatenate([keyvalue[:, first : first + DN], rope_keys], axis=1)
    return keys, keyvalue[:, first + DN : first + DN + DV]


def attend_kernel(table, query, keyvalue, rope_key, attended):
    bias = mask_bias(first_keys(table))
    rope_keys = rope_key[...]
    for head in range(query.shape[1] // (DN + DR)):
        first = head * (DN + DR)
        keys, values = head_keys(keyvalue, rope_keys, head)
        weights = softmax_parts(query[:, first : first + DN + DR], keys, bias)
        attended[:, head * DV : (head + 1) * DV] = matmul(
            weights.astype(jnp.bfloat16), values
        ).astype(jnp.bfloat16)


def attention_body(
    table, query, keyvalue, rope_key, stream_own, stream_other,
    output_own, output_other, attended, grad_query, grad_keyvalue, grad_rope
):
    factor = (DN + DR) ** (-0.5)
    bias = mask_bias(first_keys(table))
    cosine, sine = rotary_tables(table)
    rope_keys = rope_key[...]
    size = query.shape[0]
    grad_heads = matmul_right(stream_own[0], output_own[...]) + matmul_right(
        stream_other[0], output_other[...]
    )
    grad_heads = grad_heads.astype(jnp.bfloat16)
    rope_total = jnp.zeros((size, DR), jnp.float32)
    for head in range(query.shape[1] // (DN + DR)):
        first = head * (DN + DR)
        first_kv = head * (DN + DV)
        queries = query[:, first : first + DN + DR]
        keys, values = head_keys(keyvalue, rope_keys, head)
        probabilities = softmax_parts(queries, keys, bias)
        weights = probabilities.astype(jnp.bfloat16)
        result = matmul(weights, values)
        attended[head * DV : (head + 1) * DV, :] = result.astype(jnp.bfloat16).T
        grad_head = grad_heads[:, head * DV : (head + 1) * DV]
        inner = jnp.sum(result * grad_head.astype(jnp.float32), axis=1, keepdims=True)
        grad_scores = (probabilities * (matmul_right(grad_head, values) - inner)).astype(
            jnp.bfloat16
        )
        grad_queries = matmul(grad_scores, keys) * factor
        grad_keys = matmul_left(grad_scores, queries) * factor
        unrotated = rotary(grad_queries[:, DN:], cosine, -sine)
        grad_query[:, first : first + DN + DR] = jnp.concatenate(
            [grad_queries[:, :DN], unrotated], axis=1
        ).astype(jnp.bfloat16)
        grad_keyvalue[:, first_kv : first_kv + DN] = grad_keys[:, :DN].astype(jnp.bfloat16)
        grad_keyvalue[:, first_kv + DN : first_kv + DN + DV] = matmul_left(
            weights, grad_head
        ).astype(jnp.bfloat16)
        rope_total = rope_total + grad_keys[:, DN:]
    grad_rope[...] = rotary(rope_total, cosine, -sine)


def positions():
    exp_count = lax.axis_size("exp")
    slow = min(4, exp_count)
    fast = exp_count // slow
    row_count = lax.axis_size("row")
    exp_index = lax.axis_index("exp")
    place = (exp_index // fast, exp_index % fast, lax.axis_index("row"), lax.axis_index("col"))
    return place, (slow, fast, row_count)


def peers(with_core):
    (slow_at, fast_at, row_at, col_at), (slow, fast, row_count) = positions()
    slow_ids = [
        {"exp": (slow_at + step) % slow * fast + fast_at} for step in range(1, slow)
    ]
    fast_ids = [
        {"exp": slow_at * fast + (fast_at + step) % fast} for step in range(1, fast)
    ]
    row_ids = [{"row": (row_at + step) % row_count} for step in range(1, row_count)]
    core_ids = [{"col": 1 - col_at}] if with_core else []
    return slow_ids, fast_ids, row_ids, core_ids


def enter(groups):
    barrier = pltpu.get_barrier_semaphore()
    count = 0
    for group in groups:
        for device in group:
            pl.semaphore_signal(barrier, inc=1, device_id=device, device_id_type=MESH)
            count += 1
    pl.semaphore_wait(barrier, count)


def remote(src, dst, sems, index, device):
    copy = pltpu.make_async_remote_copy(
        src_ref=src,
        dst_ref=dst,
        send_sem=sems.at[(0, *index)],
        recv_sem=sems.at[(1, *index)],
        device_id=device,
        device_id_type=MESH,
    )
    copy.start()
    return copy


def wait_arrived(dst, sems, index):
    pltpu.make_async_copy(dst, dst, sems.at[(1, *index)]).wait()


def sent(src, sems, index):
    pltpu.make_async_copy(src, src, sems.at[(0, *index)]).wait()


class Gather:
    def __init__(self, source, own, other, sems, by_core):
        self.source, self.own, self.other = source, own, other
        self.far = own if by_core else other
        self.place, self.sizes = positions()
        self.fast_ids, self.row_ids, core_ids = peers(True)[1:]
        self.core = core_ids[0]
        self.half = source.shape[0] // 2
        (
            self.local, self.up, self.down, self.fast, self.row, self.low, self.high,
            self.core_sems, self.core_half,
        ) = sems

    @staticmethod
    def sems():
        exp_count, row_count = lax.axis_size("exp"), lax.axis_size("row")
        slow = min(4, exp_count)
        fast = exp_count // slow
        corner = (fast - 1, row_count - 1, slow)
        return [pltpu.SemaphoreType.DMA] + [
            pltpu.SemaphoreType.DMA((2, *shape))
            for shape in (
                (slow - 1,), (slow - 1,), (fast - 1, slow), (row_count - 1, slow), corner, corner,
                (fast, row_count, slow), (2, *corner),
            )
        ]

    def index(self, line, fast_off, row_off):
        _, fast_at, row_at, _ = self.place
        _, fast, row_count = self.sizes
        fast_index = (fast_at + fast - fast_off) % fast
        return (line * fast + fast_index) * row_count + (row_at + row_count - row_off) % row_count

    def part(self, ref, number):
        return ref.at[pl.ds(number * self.half, self.half)]

    def keep(self):
        mine = self.index(self.place[0], 0, 0)
        return pltpu.make_async_copy(self.source, self.own(mine), self.local)

    def along(self, up, src, index, number):
        slow_at, fast_at = self.place[:2]
        slow, fast, _ = self.sizes

        @pl.when(slow_at < slow - 1 if up else slow_at > 0)
        def _():
            goal = (slow_at + 1 if up else slow_at - 1) * fast + fast_at
            remote(
                src, self.own(index), self.up if up else self.down, (number,), {"exp": goal}
            )

    def spread(self, src, line):
        index = self.index(line, 0, 0)
        for number, device in enumerate(self.fast_ids):
            remote(src, self.own(index), self.fast, (number, line), device)
        for number, device in enumerate(self.row_ids):
            remote(src, self.own(index), self.row, (number, line), device)
        remote(src, self.far(index), self.core_sems, (0, 0, line), self.core)

    def start(self):
        self.keep().start()
        mine = self.index(self.place[0], 0, 0)
        self.along(True, self.source, mine, 0)
        self.along(False, self.source, mine, 0)
        self.spread(self.source, self.place[0])

    def lines(self, number, act):
        slow_at, slow = self.place[0], self.sizes[0]
        if number == 0:
            act(slow_at, None)
            return

        @pl.when(slow_at >= number)
        def _():
            act(slow_at - number, True)

        @pl.when(slow_at + number < slow)
        def _():
            act(slow_at + number, False)

    def hop(self, number):
        def act(line, up):
            block = self.own(self.index(line, 0, 0))
            wait_arrived(block, self.up if up else self.down, (number - 1,))
            if number < self.sizes[0] - 1:
                self.along(up, block, self.index(line, 0, 0), number)
            self.spread(block, line)

        self.lines(number, act)

    def corner(self, number):
        _, fast, row_count = self.sizes

        def act(line, _):
            for fast_off in range(1, fast):
                index = self.index(line, fast_off, 0)
                block = self.own(index)
                wait_arrived(block, self.fast, (fast_off - 1, line))
                for count, device in enumerate(self.row_ids):
                    low = self.part(block, 0)
                    remote(low, low, self.low, (fast_off - 1, count, line), device)
                remote(block, self.far(index), self.core_sems, (fast_off, 0, line), self.core)
            for row_off in range(1, row_count):
                index = self.index(line, 0, row_off)
                block = self.own(index)
                wait_arrived(block, self.row, (row_off - 1, line))
                for count, device in enumerate(self.fast_ids):
                    high = self.part(block, 1)
                    remote(high, high, self.high, (count, row_off - 1, line), device)
                remote(block, self.far(index), self.core_sems, (0, row_off, line), self.core)

        self.lines(number, act)

    def last(self, number):
        _, fast, row_count = self.sizes

        def act(line, _):
            for fast_off in range(1, fast):
                for row_off in range(1, row_count):
                    index = self.index(line, fast_off, row_off)
                    spot = (fast_off - 1, row_off - 1, line)
                    for count, sems in enumerate((self.low, self.high)):
                        half = self.part(self.own(index), count)
                        wait_arrived(half, sems, spot)
                        remote(
                            half, self.part(self.far(index), count), self.core_half,
                            (count, *spot), self.core,
                        )

        self.lines(number, act)

    def ready(self, line, fast_off):
        row_count = self.sizes[2]

        @pl.when(fast_off == 0)
        def _():
            for row_off in range(row_count):
                block = self.other(self.index(line, 0, row_off))
                wait_arrived(block, self.core_sems, (0, row_off, line))

        @pl.when(fast_off > 0)
        def _():
            block = self.other(self.index(line, fast_off, 0))
            wait_arrived(block, self.core_sems, (fast_off, 0, line))
            for row_off in range(1, row_count):
                block = self.other(self.index(line, fast_off, row_off))
                for count in range(2):
                    spot = (count, fast_off - 1, row_off - 1, line)
                    wait_arrived(self.part(block, count), self.core_half, spot)

    def finish(self, all_ready=False):
        slow_at = self.place[0]
        slow, fast, row_count = self.sizes
        whole = self.own(self.index(slow_at, 0, 0))
        half = self.part(whole, 0)

        @pl.loop(0, slow)
        def _(line):
            for fast_off in range(fast):
                for row_off in range(row_count):
                    block = self.other(self.index(line, fast_off, row_off))
                    if fast_off and row_off:
                        spot = (fast_off - 1, row_off - 1, line)
                        for count in range(2):
                            if not all_ready:
                                wait_arrived(
                                    self.part(block, count), self.core_half, (count, *spot)
                                )
                            sent(half, self.core_half, (count, *spot))
                        sent(half, self.low, spot)
                        sent(half, self.high, spot)
                    else:
                        if not all_ready:
                            wait_arrived(block, self.core_sems, (fast_off, row_off, line))
                        sent(whole, self.core_sems, (fast_off, row_off, line))
            for count in range(fast - 1):
                sent(whole, self.fast, (count, line))
            for count in range(row_count - 1):
                sent(whole, self.row, (count, line))

        for number in range(slow - 1):

            @pl.when((slow_at >= number) & (slow_at < slow - 1))
            def _():
                sent(whole, self.up, (number,))

            @pl.when((slow_at + number < slow) & (slow_at > 0))
            def _():
                sent(whole, self.down, (number,))

        if not all_ready:
            self.keep().wait()

    def steps(self):
        slow = self.sizes[0]
        return (
            [functools.partial(self.hop, number) for number in range(1, slow)]
            + [functools.partial(self.corner, number) for number in range(slow)]
            + [functools.partial(self.last, number) for number in range(slow)]
        )


def prologue_kernel(
    rows, gain, latent_gain, keyvalue_weight, output_weight, table,
    gain_two, tables, query_weight, latent_weight, upstream,
    gate, up, down, shared_gate, shared_up, shared_down,
    latent_normed, latent_scale, inverse_one, hidden, normed, inverse, mixer,
    tables_all, grad_all, query_far, latent_far, gain_far,
    gate_far, up_far, down_far, shared_gate_far, shared_up_far, shared_down_far,
    rows_own, rows_other, query_own, query_other, latent_own, latent_other, gain_other,
    query, keyvalue, rope_key, attended, scales, given, from_core, rows_out, from_rows,
    squares, squares_in,
    local_sems, row_sems, core_rows, slow_sems, fast_sems, core_sems, mix_core, mix_rows,
    weight_sems, *gather_sems
):
    (slow_at, fast_at, row_at, col_at), (slow, fast, row_count) = positions()
    slow_ids, fast_ids, row_ids, core_ids = peers(True)
    core = core_ids[0]
    count, width = rows.shape
    mine = slow_at * fast + fast_at
    query_width = query_own.shape[1]
    own_heads = pl.ds(pl.multiple_of(col_at * query_width, query_width), query_width)
    given_heads = pl.ds(pl.multiple_of((1 - col_at) * query_width, query_width), query_width)
    gather = Gather(
        upstream, lambda index: grad_all.at[index, col_at],
        lambda index: grad_all.at[index, 1 - col_at], gather_sems, True,
    )
    loads = [
        pltpu.make_async_copy(query_weight.at[:, own_heads], query_own, local_sems.at[0]),
        pltpu.make_async_copy(latent_weight, latent_own, local_sems.at[1]),
        pltpu.make_async_copy(tables, tables_all.at[mine], local_sems.at[2]),
    ]
    for copy in loads:
        copy.start()
    rows_own[row_at] = rows[...]
    enter((slow_ids, fast_ids, row_ids, core_ids))
    started = [
        remote(rows, rows_own.at[row_at], row_sems, (number,), device)
        for number, device in enumerate(row_ids)
    ]
    started.append(remote(rows, rows_other.at[row_at], core_rows, (0,), core))
    started.append(remote(gain, gain_other, core_sems, (0,), core))
    started.append(remote(query_weight.at[:, given_heads], query_other, core_sems, (1,), core))
    started.append(remote(latent_weight, latent_other, core_sems, (2,), core))
    for number, device in enumerate(slow_ids):
        started.append(remote(tables, tables_all.at[mine], slow_sems, (number,), device))
    for number, device in enumerate(fast_ids):
        started.append(remote(tables, tables_all.at[mine], fast_sems, (number, 0), device))
    gather.start()
    steps = gather.steps()
    for offset in range(1, row_count):
        index = (row_at + row_count - offset) % row_count
        wait_arrived(rows_own.at[index], row_sems, (offset - 1,))
        started.append(
            remote(rows_own.at[index], rows_other.at[index], core_rows, (offset,), core)
        )
    for offset in range(row_count):
        index = (row_at + row_count - offset) % row_count
        wait_arrived(rows_other.at[index], core_rows, (offset,))
    steps.pop(0)()
    for number, target in enumerate((gain_other, query_other, latent_other)):
        wait_arrived(target, core_sems, (number,))
    exchanged = [
        (gate.at[1 - col_at], gate_far), (up.at[1 - col_at], up_far), (down, down_far),
        (shared_gate, shared_gate_far), (shared_up, shared_up_far), (shared_down, shared_down_far),
    ]
    for number, (source, target) in enumerate(exchanged):
        started.append(remote(source, target, weight_sems, (number,), core))
    for copy in loads:
        copy.wait()
    for _ in range(slow - 2):
        steps.pop(0)()
    keeps = [
        pltpu.make_async_copy(source, target, local_sems.at[number])
        for number, (source, target) in enumerate(
            ((query_other, query_far), (latent_other, latent_far), (gain_other, gain_far))
        )
    ]
    for copy in keeps:
        copy.start()
    _, _, latent_unit, latent_rms, scale = project_rows(
        rows_own[...].reshape(row_count * count, width),
        rows_other[...].reshape(row_count * count, width),
        gain, gain_other, query_own, query_other, latent_own, latent_other, latent_gain,
        keyvalue_weight, table, query, keyvalue, rope_key,
    )
    latent_normed[...] = latent_unit
    latent_scale[...] = latent_rms
    scales[...] = jnp.broadcast_to(scale, scales.shape)
    inverse_one[...] = scales[pl.ds(pl.multiple_of(row_at * count, count), count), :]
    steps.pop(0)()
    attend_kernel(table, query, keyvalue, rope_key, attended)
    steps.pop(0)()
    for offset in range(1, slow):
        index = (slow_at + slow - offset) % slow * fast + fast_at
        wait_arrived(tables_all.at[index], slow_sems, (offset - 1,))
        for number, device in enumerate(fast_ids):
            started.append(
                remote(
                    tables_all.at[index], tables_all.at[index], fast_sems, (number, offset), device
                )
            )

    own_half = pl.ds(pl.multiple_of(col_at * width, width), width)
    other_half = pl.ds(pl.multiple_of((1 - col_at) * width, width), width)
    given[...] = matmul(attended[...], output_weight[:, other_half]).astype(jnp.bfloat16)
    started.append(remote(given, from_core, mix_core, (0,), core))
    total = matmul(attended[...], output_weight[:, own_half])
    wait_arrived(from_core, mix_core, (0,))
    total = total + from_core[...].astype(jnp.float32)
    rows_out[...] = total.astype(jnp.bfloat16).reshape(rows_out.shape)
    for number, device in enumerate(row_ids):
        goal = (row_at + number + 1) % row_count
        started.append(remote(rows_out.at[goal], from_rows.at[number], mix_rows, (number,), device))
    steps.pop(0)()
    state = rows[...].astype(jnp.float32) + rows_out[row_at].astype(jnp.float32)
    for number in range(row_count - 1):
        wait_arrived(from_rows.at[number], mix_rows, (number,))
        state = state + from_rows[number].astype(jnp.float32)
    hidden[...] = state
    own_squares = jnp.sum(state * state, axis=1, keepdims=True)
    squares[...] = jnp.broadcast_to(own_squares, squares.shape)
    started.append(remote(squares, squares_in, mix_core, (1,), core))
    steps.pop(0)()
    wait_arrived(squares_in, mix_core, (1,))
    rms = lax.rsqrt((squares[...] + squares_in[...]) / (2 * width) + EPSILON)
    inverse[...] = rms
    unit = state * rms[:, :1]
    normed[...] = unit
    mixer[...] = (unit * gain_two[...]).astype(jnp.bfloat16)
    for step in steps:
        step()
    for offset in range(slow):
        for number in range(1, fast):
            index = (slow_at + slow - offset) % slow * fast + (fast_at + fast - number) % fast
            wait_arrived(tables_all.at[index], fast_sems, (number - 1, offset))
    gather.finish()
    for number, (_, target) in enumerate(exchanged):
        wait_arrived(target, weight_sems, (number,))
    for copy in started:
        copy.wait_send()
    for copy in keeps:
        copy.wait()


def prologue(
    rows, gain, latent_gain, keyvalue_weight, output_weight, gain_two, tables,
    query_weight, latent_weight, upstream, others, collective_id
):
    exp_count, row_count = lax.axis_size("exp"), lax.axis_size("row")
    slow = min(4, exp_count)
    fast = exp_count // slow
    count, width = rows.shape
    group = row_count * count
    query_width = query_weight.shape[1] // 2
    keyvalue_width = keyvalue_weight.shape[1]
    latent_width = latent_weight.shape[0]
    low = jnp.bfloat16
    high = jnp.float32
    vmem = pl.BlockSpec(memory_space=pltpu.VMEM)
    wide = jax.ShapeDtypeStruct((count, width), high)
    narrow = jax.ShapeDtypeStruct((count, 128), high)
    dma = pltpu.SemaphoreType.DMA
    return pl.pallas_call(
        prologue_kernel,
        out_shape=[
            jax.ShapeDtypeStruct((group, R), high),
            jax.ShapeDtypeStruct((group, 1), high),
            narrow, wide, wide, narrow,
            jax.ShapeDtypeStruct((count, width), low),
            jax.ShapeDtypeStruct((exp_count, *tables.shape), high),
            jax.ShapeDtypeStruct((exp_count * row_count, 2, count, width), low),
            jax.ShapeDtypeStruct((width, query_width), low),
            jax.ShapeDtypeStruct(latent_weight.shape, low),
            jax.ShapeDtypeStruct(gain.shape, high),
            *[
                jax.ShapeDtypeStruct(array.shape[number < 2 :], low)
                for number, array in enumerate(others)
            ],
        ],
        in_specs=[vmem] * 7 + [ANY_SPEC] * 10,
        out_specs=[vmem] * 7 + [ANY_SPEC] * 11,
        scratch_shapes=[
            pltpu.VMEM((row_count, count, width), low),
            pltpu.VMEM((row_count, count, width), low),
            pltpu.VMEM((width, query_width), low),
            pltpu.VMEM((width, query_width), low),
            pltpu.VMEM((latent_width, width), low),
            pltpu.VMEM((latent_width, width), low),
            pltpu.VMEM(gain.shape, high),
            pltpu.VMEM((group, query_width), low),
            pltpu.VMEM((group, keyvalue_width), low),
            pltpu.VMEM((group, DR), low),
            pltpu.VMEM((group, keyvalue_width // 2), low),
            pltpu.VMEM((group, 128), high),
            pltpu.VMEM((group, width), low),
            pltpu.VMEM((group, width), low),
            pltpu.VMEM((row_count, count, width), low),
            pltpu.VMEM((row_count - 1, count, width), low),
            pltpu.VMEM((count, 128), high),
            pltpu.VMEM((count, 128), high),
            dma((3,)),
            dma((2, row_count - 1)),
            dma((2, row_count)),
            dma((2, slow - 1)),
            dma((2, fast - 1, slow)),
            dma((2, 3)),
            dma((2, 2)),
            dma((2, row_count - 1)),
            dma((2, 6)),
            *Gather.sems(),
        ],
        compiler_params=pltpu.CompilerParams(
            collective_id=collective_id, has_side_effects=True, vmem_limit_bytes=VMEM_LIMIT
        ),
    )(
        rows, gain, latent_gain, keyvalue_weight, output_weight, tables, gain_two, tables,
        query_weight, latent_weight, upstream, *others,
    )


def pipeline(body, grid, inputs, outputs):
    pltpu.emit_pipeline(
        body,
        grid=grid,
        in_specs=[pl.BlockSpec(block, place) for _, block, place in inputs],
        out_specs=[pl.BlockSpec(block, place) for _, block, place in outputs],
    )(*[ref for ref, _, _ in inputs], *[ref for ref, _, _ in outputs])


def product_body(total, axis, steps):
    def body(left, right, result):
        step = pl.program_id(axis)
        product = matmul(
            left[...].reshape(-1, left.shape[-1]), right[...].reshape(-1, right.shape[-1])
        )
        spot = total.at[pl.ds(0, product.shape[0]), pl.ds(0, product.shape[1])]

        @pl.when(step == 0)
        def _():
            spot[...] = product

        @pl.when((step > 0) & (step < steps - 1))
        def _():
            spot[...] += product

        @pl.when(step == steps - 1)
        def _():
            result[...] = (spot[...] + product).reshape(result.shape).astype(result.dtype)

    return body


DEPTH = 1024


def stacked_job(left, right, result, total):
    parts, units, tokens = left.shape
    width = right.shape[2]
    steps = tokens // DEPTH

    def run():
        pipeline(
            product_body(total, 1, steps),
            (parts, steps),
            [
                (left, (1, units, DEPTH), lambda part, step: (part, 0, step)),
                (right, (1, DEPTH, width), lambda part, step: (0, step, 0)),
            ],
            [(result, (1, units, width), lambda part, step: (part, 0, 0))],
        )

    return run


def row_job(left, right, result, total):
    features, tokens = left.shape
    units = right.shape[1]
    steps = tokens // DEPTH

    def run():
        pipeline(
            product_body(total, 0, steps),
            (steps,),
            [
                (left, (features, DEPTH), lambda step: (0, step)),
                (right, (DEPTH, units), lambda step: (step, 0)),
            ],
            [(result, (features, units), lambda step: (0, 0))],
        )

    return run


def expert_down_job(left, right, result, total):
    parts, units, tokens = left.shape
    _, _, rows, width = right.shape
    steps = tokens // DEPTH
    col = lax.axis_index("col")

    def run():
        pipeline(
            product_body(total, 1, steps),
            (2, steps),
            [
                (left, (parts, units // 2, DEPTH), lambda side, step: (0, col, step)),
                (right, (DEPTH // rows, 1, rows, width), lambda side, step: (step, side, 0, 0)),
            ],
            [(result, (parts, units // 2, width), lambda side, step: (0, 0, side))],
        )

    return run


def shared_down_job(left, right, result, total):
    units, tokens = left.shape
    _, _, rows, width = right.shape
    steps = tokens // DEPTH

    def run():
        pipeline(
            product_body(total, 1, steps),
            (2, steps),
            [
                (left, (units, DEPTH), lambda side, step: (0, step)),
                (right, (DEPTH // rows, 1, rows, width), lambda side, step: (step, side, 0, 0)),
            ],
            [(result, (units, width), lambda side, step: (0, side))],
        )

    return run


def sided_job(left, right, result, total):
    units, tokens = left.shape
    width = right.shape[2]
    steps = tokens // DEPTH
    col = lax.axis_index("col")

    def run():
        pipeline(
            product_body(total, 1, steps),
            (2, steps),
            [
                (left, (units, DEPTH), lambda side, step: (0, step)),
                (right, (1, DEPTH, width), lambda side, step: (side, step, 0)),
            ],
            [(result, (units, width), lambda side, step: (0, (col + side) % 2))],
        )

    return run


def project_body(own, other, *rest):
    rows, width = own.shape[0] * own.shape[2], own.shape[3]
    normed, compressed, _, _, _ = project_rows(
        own[...].reshape(rows, width), other[...].reshape(rows, width), *rest[:-2]
    )
    rest[-2][...] = normed.T
    rest[-1][...] = compressed.T


def project_jobs(values, weights, tables, results, parts):
    blocks, _, rows, width = values.shape
    tile_blocks = 256 // rows
    steps = blocks // tile_blocks // parts
    col = lax.axis_index("col")
    query_width = weights[3].shape[1]

    def job(part):
        def at(step):
            return part * steps + step

        def table(array):
            return (array, (256, array.shape[1]), lambda step: (at(step), 0))

        def whole(array):
            return (array, array.shape, lambda step: (0, 0))

        def run():
            inputs = [
                (values, (tile_blocks, 1, rows, width), lambda step: (at(step), col, 0, 0)),
                (values, (tile_blocks, 1, rows, width), lambda step: (at(step), 1 - col, 0, 0)),
            ]
            weight_inputs = [whole(array) for array in weights]
            weight_inputs[2] = (weights[2], (width, query_width), lambda step: (0, col))
            inputs += weight_inputs + [table(tables)]
            outputs = [table(array) for array in results[:3]]
            outputs += [
                (array, (array.shape[0], 256), lambda step: (0, at(step))) for array in results[3:]
            ]
            pipeline(project_body, (steps,), inputs, outputs)

        return run

    return [job(part) for part in range(parts)]


def attention_jobs(arrays, stream, output_weight, results, groups, parts):
    size = arrays[0].shape[0] // groups
    width = stream.shape[2]
    col = lax.axis_index("col")
    steps = groups // parts

    def job(part):
        def at(step):
            return part * steps + step

        def table(array):
            return (array, (size, array.shape[1]), lambda step: (at(step), 0))

        def run():
            inputs = [table(array) for array in arrays]
            inputs += [
                (stream, (1, size, width), lambda step: (0, at(step), 0)),
                (stream, (1, size, width), lambda step: (1, at(step), 0)),
                (output_weight, (output_weight.shape[0], width), lambda step: (0, col)),
                (output_weight, (output_weight.shape[0], width), lambda step: (0, 1 - col)),
            ]
            outputs = [
                (results[0], (results[0].shape[0], size), lambda step: (0, at(step)))
            ] + [table(array) for array in results[1:]]
            pipeline(attention_body, (steps,), inputs, outputs)

        return run

    return [job(part) for part in range(parts)]


TOTAL = (1024, 1408)


def jobs_kernel(*refs, make_jobs, inputs):
    for job in make_jobs(refs[:inputs], refs[inputs:-1], refs[-1]):
        job()


def run_jobs(make_jobs, operands, shapes):
    return pl.pallas_call(
        functools.partial(jobs_kernel, make_jobs=make_jobs, inputs=len(operands)),
        out_shape=shapes,
        in_specs=[ANY_SPEC] * len(operands),
        out_specs=[ANY_SPEC] * len(shapes),
        scratch_shapes=[pltpu.VMEM(TOTAL, jnp.float32)],
        compiler_params=pltpu.CompilerParams(vmem_limit_bytes=VMEM_LIMIT),
    )(*operands)


def no_jobs(inputs, outputs, total):
    return []


def gather_kernel(*refs, make_jobs, inputs, sems):
    source, job_inputs, target = refs[0], refs[1 : 1 + inputs], refs[1 + inputs]
    total, gather_sems = refs[-sems - 1], refs[-sems:]
    jobs = make_jobs(job_inputs, refs[2 + inputs : -sems - 1], total)
    gather = Gather(
        source, lambda index: target.at[0, index], lambda index: target.at[1, index], gather_sems,
        False,
    )

    def work():
        if jobs:
            jobs.pop(0)()

    enter(peers(True))
    gather.start()
    steps = gather.steps()
    slow = gather.sizes[0]
    for number, step in enumerate(steps):
        if number in (0, slow - 2, slow + 1, 2 * slow):
            work()
        step()
    while jobs:
        work()
    gather.finish()


def gather_everywhere(values, collective_id, make_jobs=no_jobs, operands=(), shapes=()):
    exp_count, row_count = lax.axis_size("exp"), lax.axis_size("row")
    slow = min(4, exp_count)
    fast = exp_count // slow
    rows, width = values.shape
    blocks = exp_count * row_count
    result = jax.ShapeDtypeStruct((2, blocks, rows, width), values.dtype)
    sems = Gather.sems()
    gathered, *others = pl.pallas_call(
        functools.partial(
            gather_kernel, make_jobs=make_jobs, inputs=len(operands), sems=len(sems)
        ),
        out_shape=[result, *shapes],
        in_specs=[ANY_SPEC] * (1 + len(operands)),
        out_specs=[ANY_SPEC] * (1 + len(shapes)),
        scratch_shapes=[pltpu.VMEM(TOTAL, jnp.float32), *sems],
        compiler_params=pltpu.CompilerParams(
            collective_id=collective_id, has_side_effects=True, vmem_limit_bytes=VMEM_LIMIT
        ),
        cost_estimate=pl.CostEstimate(
            flops=0, bytes_accessed=4 * blocks * rows * width * 4, transcendentals=0
        ),
    )(values, *operands)
    return gathered.reshape(2, blocks * rows, width), others


def scatter_kernel(*refs, backward, make_jobs, inputs, outputs):
    if backward:
        gating, upward, gate, up, own_gating, own_upward, shared_gate, shared_up = refs[:8]
        lefts = [gating.at[0], gating.at[1], upward.at[0], upward.at[1]]
        refs = refs[8:]
    else:
        hidden, down, down_other, own_hidden, other_hidden, shared, shared_other = refs[:7]
        lefts = [hidden.at[0], hidden.at[1]]
        refs = refs[7:]
    count = len(lefts)
    job_inputs, result, job_outputs = (
        refs[:inputs], refs[inputs], refs[inputs + 1 : inputs + 1 + outputs]
    )
    refs = refs[inputs + 1 + outputs :]
    (
        left_tiles, rights, extra_left, extra_right, part, from_row, from_fast,
        from_fast_late, from_row_late, from_slow,
        left_sems, right_sems, extra_sems, row_sems, fast_sems, fast_late_sems, row_late_sems,
        slow_sems, job_sems, job_total,
    ) = refs
    (slow_at, fast_at, row_at, col_at), (slow, fast, row_count) = positions()
    slow_ids, fast_ids, row_ids, core_ids = peers(True)
    jobs = make_jobs(job_inputs, job_outputs, job_total, core_ids[0], job_sems)
    exp_count = slow * fast
    exp_index = lax.axis_index("exp")
    rows, width = result.shape
    half = rows // 2
    low, high = pl.ds(0, half), pl.ds(half, half)
    group = rows * row_count
    group_rows = pl.ds(pl.multiple_of(exp_index * group, group), group)
    own_half = pl.ds(pl.multiple_of(col_at * width, width), width)

    def slow_of(turn):
        return (slow_at + 1 + turn) % slow

    def order(step):
        return slow_of(step // fast) * fast + (fast_at + 1 + step % fast) % fast

    def loads(step, slot):
        first = pl.multiple_of(order(step) * group, group)
        return [
            pltpu.make_async_copy(
                left.at[:, pl.ds(first, group)], left_tiles.at[slot, number],
                left_sems.at[slot, number],
            )
            for number, left in enumerate(lefts)
        ]

    if backward:
        right_pairs = [(array.at[side], rights.at[2 * number + side])
                       for number, array in enumerate((gate, up)) for side in range(2)]
        extra_pairs = [
            (own_gating.at[group_rows], extra_left.at[0]),
            (own_upward.at[group_rows], extra_left.at[1]),
            (shared_gate, extra_right.at[0]),
            (shared_up, extra_right.at[1]),
        ]
        extra_product = matmul_right
    else:
        split = down.shape[1]
        right_pairs = []
        for side in range(2):
            for source, place in ((down, col_at), (down_other, 1 - col_at)):
                spot = pl.ds(pl.multiple_of(place * split, 16), split)
                right_pairs.append((source.at[side, :, own_half], rights.at[side, spot]))
        extra_pairs = [
            (own_hidden.at[:, group_rows], extra_left.at[0]),
            (other_hidden, extra_left.at[1]),
            (shared.at[:, own_half], extra_right.at[0]),
            (shared_other.at[:, own_half], extra_right.at[1]),
        ]
        extra_product = matmul_left
    prepared = [
        pltpu.make_async_copy(source, target, right_sems.at[number])
        for number, (source, target) in enumerate(right_pairs)
    ]
    extras = [
        pltpu.make_async_copy(source, target, extra_sems.at[number])
        for number, (source, target) in enumerate(extra_pairs)
    ]
    for copy in prepared + loads(0, 0) + extras:
        copy.start()
    enter((slow_ids, fast_ids, row_ids, core_ids))
    for copy in prepared:
        copy.wait()

    def make(step):
        slot = step % 2

        @pl.when(step + 1 < exp_count)
        def _():
            for copy in loads(step + 1, 1 - slot):
                copy.start()

        for copy in loads(step, slot):
            copy.wait()
        index = order(step)
        total = matmul_left(left_tiles[slot, 0], rights[0])
        for number in range(1, count):
            total = total + matmul_left(left_tiles[slot, number], rights[number])
        part[index] = total.astype(jnp.bfloat16).reshape(row_count, rows, width)

        @pl.when(step == exp_count - 1)
        def _():
            for copy in extras:
                copy.wait()
            extra = extra_product(extra_left[0], extra_right[0])
            extra = extra + extra_product(extra_left[1], extra_right[1])
            before = part[index].astype(jnp.float32)
            part[index] = (before + extra.reshape(before.shape)).astype(jnp.bfloat16)

        for number, device in enumerate(row_ids):
            goal = (row_at + number + 1) % row_count
            remote(
                part.at[index, goal, low], from_row.at[number, index], row_sems,
                (number, index), device,
            )
        slow_index = index // fast
        for number, device in enumerate(fast_ids):

            @pl.when(index % fast == (fast_at + number + 1) % fast)
            def _():
                for goal in range(row_count):
                    remote(
                        part.at[index, goal, high], from_fast.at[number, slow_index, goal],
                        fast_sems, (number, slow_index, goal), device,
                    )

    def add_up(index, goal, span, arrivals):
        total = part[index, goal, span].astype(jnp.float32)
        for buffer, sems, spot in arrivals:
            wait_arrived(buffer.at[spot], sems, spot)
            total = total + buffer[spot].astype(jnp.float32)
        return total

    def of_rows(index):
        return [(from_row, row_sems, (number, index)) for number in range(row_count - 1)]

    def of_fasts(slow_index, goal):
        return [
            (from_fast, fast_sems, (number, slow_index, goal)) for number in range(fast - 1)
        ]

    def second(slow_index):
        for number, device in enumerate(fast_ids):
            index = slow_index * fast + (fast_at + number + 1) % fast
            part[index, row_at, low] = add_up(index, row_at, low, of_rows(index)).astype(
                jnp.bfloat16
            )
            remote(
                part.at[index, row_at, low], from_fast_late.at[number, slow_index],
                fast_late_sems, (number, slow_index), device,
            )
        mine = slow_index * fast + fast_at
        for number, device in enumerate(row_ids):
            goal = (row_at + number + 1) % row_count
            part[mine, goal, high] = add_up(
                mine, goal, high, of_fasts(slow_index, goal)
            ).astype(jnp.bfloat16)
            remote(
                part.at[mine, goal, high], from_row_late.at[number, slow_index],
                row_late_sems, (number, slow_index), device,
            )

    def finish(slow_index, span, late):
        mine = slow_index * fast + fast_at
        if late == 0:
            arrivals = of_rows(mine) + [
                (from_fast_late, fast_late_sems, (number, slow_index))
                for number in range(fast - 1)
            ]
        else:
            arrivals = of_fasts(slow_index, row_at) + [
                (from_row_late, row_late_sems, (number, slow_index))
                for number in range(row_count - 1)
            ]
        return add_up(mine, row_at, span, arrivals)

    def third(number):
        slow_index = slow_of(number)
        mine = slow_index * fast + fast_at
        for late, span in enumerate((low, high)):
            part[mine, row_at, span] = finish(slow_index, span, late).astype(jnp.bfloat16)
            remote(
                part.at[mine, row_at, span], from_slow.at[late, number], slow_sems,
                (late, number), slow_ids[number],
            )

    for turn in range(slow + 1):
        if turn < slow:
            pl.loop(turn * fast, turn * fast + fast)(make)
        if turn >= 1:
            second(slow_of(turn - 1))
        if turn >= 2:
            third(turn - 2)
        if jobs:
            jobs.pop(0)()
    for job in jobs:
        job()
    for late, span in enumerate((low, high)):
        total = finish(slow_at, span, late)
        for number in range(slow - 1):
            wait_arrived(from_slow.at[late, number], slow_sems, (late, number))
            total = total + from_slow[late, number].astype(jnp.float32)
        result[span, :] = total

    @pl.loop(0, exp_count)
    def _(index):
        for number in range(row_count - 1):
            sent(from_row.at[number, index], row_sems, (number, index))

    @pl.loop(0, slow)
    def _(slow_index):
        for number in range(fast - 1):
            for goal in range(row_count):
                spot = (number, slow_index, goal)
                sent(from_fast.at[spot], fast_sems, spot)
            sent(from_fast_late.at[number, slow_index], fast_late_sems, (number, slow_index))
        for number in range(row_count - 1):
            sent(from_row_late.at[number, slow_index], row_late_sems, (number, slow_index))

    for number in range(slow - 1):
        for late in range(2):
            sent(from_slow.at[late, number], slow_sems, (late, number))


def no_scatter_jobs(inputs, outputs, total, core, sems):
    return []


def scatter_products(
    operands, backward, collective_id, make_jobs=no_scatter_jobs, job_operands=(), shapes=()
):
    exp_count, row_count = lax.axis_size("exp"), lax.axis_size("row")
    slow = min(4, exp_count)
    fast = exp_count // slow
    _, units, tokens = operands[0].shape
    rows = tokens // exp_count // row_count
    group = rows * row_count
    half = rows // 2
    kind = jnp.bfloat16
    if backward:
        count, (width, shared_units) = 4, operands[6].shape
        extra_shapes = [(2, group, shared_units), (2, width, shared_units)]
    else:
        count, shared_units, width = 2, operands[5].shape[0], operands[1].shape[2] // 2
        extra_shapes = [(2, shared_units, group), (2, shared_units, width)]
    return pl.pallas_call(
        functools.partial(
            scatter_kernel, backward=backward, make_jobs=make_jobs, inputs=len(job_operands),
            outputs=len(shapes),
        ),
        out_shape=[jax.ShapeDtypeStruct((rows, width), jnp.float32), *shapes],
        in_specs=[ANY_SPEC] * (len(operands) + len(job_operands)),
        out_specs=[pl.BlockSpec(memory_space=pltpu.VMEM)] + [ANY_SPEC] * len(shapes),
        scratch_shapes=[
            pltpu.VMEM((2, count, units, group), kind),
            pltpu.VMEM((count, units, width), kind),
            pltpu.VMEM(extra_shapes[0], kind),
            pltpu.VMEM(extra_shapes[1], kind),
            pltpu.VMEM((exp_count, row_count, rows, width), kind),
            pltpu.VMEM((row_count - 1, exp_count, half, width), kind),
            pltpu.VMEM((fast - 1, slow, row_count, half, width), kind),
            pltpu.VMEM((fast - 1, slow, half, width), kind),
            pltpu.VMEM((row_count - 1, slow, half, width), kind),
            pltpu.VMEM((2, slow - 1, half, width), kind),
            pltpu.SemaphoreType.DMA((2, count)),
            pltpu.SemaphoreType.DMA((4,)),
            pltpu.SemaphoreType.DMA((4,)),
            pltpu.SemaphoreType.DMA((2, row_count - 1, exp_count)),
            pltpu.SemaphoreType.DMA((2, fast - 1, slow, row_count)),
            pltpu.SemaphoreType.DMA((2, fast - 1, slow)),
            pltpu.SemaphoreType.DMA((2, row_count - 1, slow)),
            pltpu.SemaphoreType.DMA((2, 2, slow - 1)),
            pltpu.SemaphoreType.DMA((2, 1)),
            pltpu.VMEM(TOTAL if make_jobs is not no_scatter_jobs else (8, 128), jnp.float32),
        ],
        compiler_params=pltpu.CompilerParams(
            collective_id=collective_id, has_side_effects=True, vmem_limit_bytes=VMEM_LIMIT
        ),
        cost_estimate=pl.CostEstimate(
            flops=2 * tokens * units * width * count,
            bytes_accessed=tokens * units * count * 2 + 60 * 1024 * 1024,
            transcendentals=0,
        ),
    )(*operands, *job_operands)


def unit_grads(gating, upward, grad_hidden):
    bend = 0.5 * jnp.tanh(0.5 * gating)
    sigmoid = 0.5 + bend
    silu = gating * sigmoid
    grad_upward = (grad_hidden * silu).astype(jnp.bfloat16)
    grad_gating = (grad_hidden * upward * (sigmoid + silu * (0.5 - bend))).astype(jnp.bfloat16)
    return silu * upward, grad_gating, grad_upward


def units_kernel(
    mixer_rows, tables, all_grad, layer_rows,
    expert_gate, gate_other, expert_up, up_other, expert_down, down_other,
    shared_gate, shared_gate_other, shared_up, shared_up_other, shared_down, shared_down_other,
    all_mixer, all_rows,
    expert_hidden, expert_gating, expert_upward, shared_hidden, shared_gating, shared_upward,
    mixer_turned,
    gates, ups, downs, shared_gates, shared_ups, shared_downs, inputs, table, tiles, turned_tiles,
    shared_tiles, shared_turned,
    weight_sems, input_sems, local_sems, send_sems, recv_sems, shared_local, shared_send,
    shared_recv, *gather_sems
):
    step = pl.program_id(0)
    steps = pl.num_programs(0)
    (slow_at, fast_at, _, col), (slow, fast, row_count) = positions()
    core = {"col": 1 - col}
    rows, width = mixer_rows.shape
    tile = rows * row_count
    part = tile // 2
    split = expert_down.shape[1]
    shared_split = shared_down.shape[0]
    shared_steps = steps // 2
    halves = [pl.ds(pl.multiple_of(side * width, width), width) for side in (col, 1 - col)]
    targets = [expert_hidden, expert_gating, expert_upward]
    shared_targets = [shared_gating, shared_upward]
    gather = Gather(
        mixer_rows, lambda index: all_mixer.at[0, index], lambda index: all_mixer.at[1, index],
        gather_sems[: len(gather_sems) // 2], False,
    )
    late = Gather(
        layer_rows, lambda index: all_rows.at[index, col],
        lambda index: all_rows.at[index, 1 - col], gather_sems[len(gather_sems) // 2 :], True,
    )

    def line_of(at):
        place = at % slow
        near = [
            sorted(range(slow), key=lambda line, own=own: (abs(line - own), line))
            for own in range(slow)
        ]
        line = jnp.int32(0)
        for own in range(slow):
            for number in range(slow):
                line = line + jnp.where(
                    (slow_at == own) & (place == number), near[own][number], 0
                ).astype(jnp.int32)
        return line

    def group_of(at):
        fast_off = at // slow
        return line_of(at) * fast + (fast_at + fast - fast_off) % fast

    def weight_copies():
        pairs = [
            (expert_gate.at[col], gates.at[0]),
            (gate_other, gates.at[1]),
            (expert_up.at[col], ups.at[0]),
            (up_other, ups.at[1]),
        ]
        own_rows = pl.ds(pl.multiple_of(col * split, 16), split)
        other_rows = pl.ds(pl.multiple_of((1 - col) * split, 16), split)
        shared_own = pl.ds(pl.multiple_of(col * shared_split, 16), shared_split)
        shared_other = pl.ds(pl.multiple_of((1 - col) * shared_split, 16), shared_split)
        for side in range(2):
            pairs += [
                (expert_down.at[col, :, halves[side]], downs.at[side, own_rows]),
                (down_other.at[col, :, halves[side]], downs.at[side, other_rows]),
            ]
        pairs += [
            (shared_gate, shared_gates.at[0]),
            (shared_gate_other, shared_gates.at[1]),
            (shared_up, shared_ups.at[0]),
            (shared_up_other, shared_ups.at[1]),
        ]
        for side in range(2):
            pairs += [
                (shared_down.at[:, halves[side]], shared_downs.at[side, shared_own]),
                (shared_down_other.at[:, halves[side]], shared_downs.at[side, shared_other]),
            ]
        return [
            pltpu.make_async_copy(src, dst, weight_sems.at[number])
            for number, (src, dst) in enumerate(pairs)
        ]

    def known_copies(at):
        group = group_of(at)
        slot = at % 3
        blocks = pl.ds(group * row_count, row_count)
        span = pl.ds(pl.multiple_of(group * tile, tile), tile)
        return [
            pltpu.make_async_copy(
                all_grad.at[blocks, side], inputs.at[slot, 2 + number],
                input_sems.at[slot, 2 + number],
            )
            for number, side in enumerate((col, 1 - col))
        ] + [pltpu.make_async_copy(tables.at[span], table.at[slot], input_sems.at[slot, 4])]

    def mixer_copies(at):
        slot = at % 3
        blocks = pl.ds(group_of(at) * row_count, row_count)
        return [
            pltpu.make_async_copy(
                all_mixer.at[side, blocks], inputs.at[slot, side], input_sems.at[slot, side]
            )
            for side in range(2)
        ]

    def results(at, slot):
        columns = pl.ds(pl.multiple_of(group_of(at) * tile, tile), tile)
        local, far = [], []
        for number, target in enumerate(targets):
            spot = target.at[col, :, columns]
            local.append(
                pltpu.make_async_copy(tiles.at[slot, number], spot, local_sems.at[slot, number])
            )
            far.append(
                pltpu.make_async_remote_copy(
                    src_ref=tiles.at[slot, number],
                    dst_ref=spot,
                    send_sem=send_sems.at[slot, number],
                    recv_sem=recv_sems.at[number, at],
                    device_id=core,
                    device_id_type=MESH,
                )
            )
        local.append(
            pltpu.make_async_copy(
                turned_tiles.at[slot], mixer_turned.at[:, columns], local_sems.at[slot, 3]
            )
        )
        return local, far

    def shared_span(turn, member, side):
        first = group_of(2 * turn + member) * tile + side * part
        return pl.ds(pl.multiple_of(first, part), part)

    def shared_results(turn, slot):
        own_rows = pl.ds(pl.multiple_of(col * shared_split, 16), shared_split)
        other_rows = pl.ds(pl.multiple_of((1 - col) * shared_split, 16), shared_split)
        local, far = [], []
        for member in range(2):
            span = shared_span(turn, member, col)
            here = pl.ds(member * part, part)
            triples = [
                (shared_tiles.at[slot, number, here], target.at[span],
                 shared_tiles.at[slot, number, here])
                for number, target in enumerate(shared_targets)
            ]
            triples.append(
                (shared_turned.at[slot, own_rows, here], shared_hidden.at[:, span],
                 shared_turned.at[slot, other_rows, here])
            )
            for number, (near, goal, away) in enumerate(triples):
                local.append(
                    pltpu.make_async_copy(near, goal, shared_local.at[slot, member, number])
                )
                far.append(
                    pltpu.make_async_remote_copy(
                        src_ref=away,
                        dst_ref=goal,
                        send_sem=shared_send.at[slot, member, number],
                        recv_sem=shared_recv.at[number, member, turn],
                        device_id=core,
                        device_id_type=MESH,
                    )
                )
        return local, far

    def wait_out(pair):
        local, far = pair
        for copy in local:
            copy.wait()
        for copy in far:
            copy.wait_send()

    def fetch(at):
        gather.ready(line_of(at), at // slow)
        for copy in mixer_copies(at):
            copy.start()

    weights_early = 8

    @pl.when(step == 0)
    def _():
        for copy in weight_copies()[:weights_early] + known_copies(0):
            copy.start()
        enter(peers(True))
        gather.start()
        for copy in weight_copies()[weights_early:]:
            copy.start()
        gather.corner(0)
        gather.hop(1)
        gather.keep().wait()
        fetch(0)
        for copy in weight_copies()[:weights_early]:
            copy.wait()

    slot = step % 2

    @pl.when(step + 1 < steps)
    def _():
        for copy in known_copies(step + 1):
            copy.start()

    @pl.when(step >= 2)
    def _():
        wait_out(results(step - 2, slot))

    for copy in known_copies(step) + mixer_copies(step):
        copy.wait()

    def block(at, number):
        return inputs[at % 3, number].reshape(tile, width)

    mixers = (block(step, 0), block(step, 1))
    grads = (block(step, 2), block(step, 3))
    turned_tiles[slot] = mixers[0].T

    def both(pair, weights, product):
        return product(pair[0], weights[0]) + product(pair[1], weights[1])

    def turned(weights, pair):
        return matmul_right(weights[0], pair[0]) + matmul_right(weights[1], pair[1])

    columns = table[step % 3].T
    own_expert = (lax.axis_index("exp") * expert_down.shape[0] + col).astype(jnp.float32)
    chosen = columns[TABLE["ids"] : TABLE["ids"] + TOP]
    router = columns[TABLE["router"] : TABLE["router"] + TOP]
    scale = jnp.sum(jnp.where(chosen == own_expert, router, 0.0), axis=0, keepdims=True)
    hidden, gating, upward = unit_grads(
        turned(gates, mixers), turned(ups, mixers), turned(downs, grads) * scale
    )
    tiles[slot, 0] = (hidden * scale).astype(jnp.bfloat16)
    tiles[slot, 1] = gating
    tiles[slot, 2] = upward
    local, far = results(step, slot)
    for copy in local + far:
        copy.start()

    def acts(*number_and_acts):
        for number, chosen in number_and_acts:

            @pl.when(step == number)
            def _():
                for act, *arguments in chosen:
                    act(*arguments)

    def wait_weights():
        for copy in weight_copies()[weights_early:]:
            copy.wait()

    acts(
        (0, [(gather.hop, 2), (gather.corner, 1), (gather.hop, 3), (wait_weights,)]),
        (1, [(gather.corner, 2), (gather.last, 0), (late.start,)]),
        (2, [(gather.corner, 3), (gather.last, 1), (late.hop, 1)]),
        (3, [(gather.last, 2), (late.hop, 2)]),
        (4, [(gather.last, 3), (late.hop, 3), (late.corner, 0)]),
        (5, [(late.corner, 1), (late.corner, 2)]),
        (6, [(late.corner, 3), (late.last, 0), (late.last, 1)]),
        (7, [(late.last, 2), (late.last, 3)]),
    )

    @pl.when(step + 1 < steps)
    def _():
        fetch(step + 1)

    @pl.when(step % 2 == 1)
    def _():
        turn = step // 2
        turn_slot = turn % 2

        @pl.when(turn >= 2)
        def _():
            wait_out(shared_results(turn - 2, turn_slot))

        first = col * (row_count // 2)

        def pick(number):
            wanted = pl.ds(first, row_count // 2)
            return jnp.concatenate(
                [
                    inputs[at % 3, number, wanted].reshape(part, width)
                    for at in (step - 1, step)
                ],
                axis=0,
            )

        chosen_rows = [pick(number) for number in range(4)]
        hidden, gating, upward = unit_grads(
            both(chosen_rows[:2], shared_gates, matmul),
            both(chosen_rows[:2], shared_ups, matmul),
            both(chosen_rows[2:], shared_downs, matmul_right),
        )
        shared_tiles[turn_slot, 0] = gating
        shared_tiles[turn_slot, 1] = upward
        shared_turned[turn_slot] = hidden.astype(jnp.bfloat16).T
        local, far = shared_results(turn, turn_slot)
        for copy in local + far:
            copy.start()

    @pl.when(step == steps - 1)
    def _():
        for back in range(2):
            at = steps - 1 - back
            wait_out(results(at, at % 2))
            turn = shared_steps - 1 - back
            wait_out(shared_results(turn, turn % 2))

        @pl.loop(0, steps)
        def _(at):
            columns = pl.ds(pl.multiple_of(group_of(at) * tile, tile), tile)
            for number, target in enumerate(targets):
                spot = target.at[1 - col, :, columns]
                pltpu.make_async_copy(spot, spot, recv_sems.at[number, at]).wait()

        @pl.loop(0, shared_steps)
        def _(turn):
            for member in range(2):
                span = shared_span(turn, member, 1 - col)
                spots = [target.at[span] for target in shared_targets]
                spots.append(shared_hidden.at[:, span])
                for number, spot in enumerate(spots):
                    pltpu.make_async_copy(
                        spot, spot, shared_recv.at[number, member, turn]
                    ).wait()

        gather.finish(True)
        late.finish()


def run_units(mixer_rows, tables, grad, layer_rows, weights, collective_id):
    rows, width = mixer_rows.shape
    exp_count, row_count = lax.axis_size("exp"), lax.axis_size("row")
    tokens = tables.shape[0]
    tile = rows * row_count
    units = weights[0].shape[1]
    shared_units = weights[6].shape[1]
    kind = jnp.bfloat16
    pair = jax.ShapeDtypeStruct((2, units, tokens), kind)
    shared = jax.ShapeDtypeStruct((tokens, shared_units), kind)
    half = jax.ShapeDtypeStruct((shared_units // 2, tokens), kind)
    steps = exp_count
    dma = pltpu.SemaphoreType.DMA
    mixer, *others = pl.pallas_call(
        units_kernel,
        out_shape=[
            jax.ShapeDtypeStruct((2, exp_count * row_count, rows, width), kind),
            jax.ShapeDtypeStruct(grad.shape, kind),
            pair, pair, pair, half, shared, shared, jax.ShapeDtypeStruct((width, tokens), kind),
        ],
        grid=(steps,),
        in_specs=[ANY_SPEC] * (len(weights) + 4),
        out_specs=[ANY_SPEC] * 9,
        scratch_shapes=[
            pltpu.VMEM((2, units, width), kind),
            pltpu.VMEM((2, units, width), kind),
            pltpu.VMEM((2, units, width), kind),
            pltpu.VMEM((2, width, shared_units), kind),
            pltpu.VMEM((2, width, shared_units), kind),
            pltpu.VMEM((2, shared_units, width), kind),
            pltpu.VMEM((3, 4, row_count, rows, width), kind),
            pltpu.VMEM((3, tile, 128), jnp.float32),
            pltpu.VMEM((2, 3, units, tile), kind),
            pltpu.VMEM((2, width, tile), kind),
            pltpu.VMEM((2, 2, tile, shared_units), kind),
            pltpu.VMEM((2, shared_units, tile), kind),
            dma((16,)),
            dma((3, 5)),
            dma((2, 4)),
            dma((2, 3)),
            dma((3, steps)),
            dma((2, 2, 3)),
            dma((2, 2, 3)),
            dma((3, 2, steps // 2)),
            *Gather.sems(),
            *Gather.sems(),
        ],
        compiler_params=pltpu.CompilerParams(
            collective_id=collective_id, has_side_effects=True, vmem_limit_bytes=VMEM_LIMIT
        ),
        cost_estimate=pl.CostEstimate(
            flops=2 * tokens * units * width * 2 * 6,
            bytes_accessed=50 * 1024 * 1024,
            transcendentals=2 * tokens * units,
        ),
    )(mixer_rows, tables, grad, layer_rows, *weights)
    return mixer.reshape(2, tokens, width), *others


def tail_kernel(
    rows, inverse_one, gain, grad_hidden, sums_in, latent_normed, latent_scale, latent_gain,
    keyvalue_weight, query_other, latent_weight,
    grad_query, grad_keyvalue, grad_rope, query_weight,
    attended_turned, stream, attention_turned, compressed_turned,
    input_grad, sums, latent_all, output_weight_grad, keyvalue_weight_grad, query_weight_grad,
    queries, keyvalues, ropes, query_own, latent_out, latent_in, latent_row_in, wide_out, wide_in,
    wide_rows, wide_row_in, latent_block, squares, squares_in,
    running, slow_in, fast_in, row_in, core_in,
    total_scratch,
    local_sems, core_sems, row_sems, slow_sums, fast_sums, row_sums, core_sums, *gather_sems,
    fused
):
    (slow_at, fast_at, row_at, col_at), (slow, fast, row_count) = positions()
    slow_ids, fast_ids, row_ids, core_ids = peers(True)
    core = core_ids[0]
    count, width = rows.shape
    group = row_count * count
    group_rows = pl.ds(pl.multiple_of(lax.axis_index("exp") * group, group), group)
    query_width = query_own.shape[1]
    jobs = []
    if fused:
        jobs = weight_jobs(
            (
                attended_turned, stream, attention_turned, compressed_turned, grad_query,
                grad_keyvalue,
            ),
            (output_weight_grad, keyvalue_weight_grad, query_weight_grad),
            total_scratch,
        )

    def work():
        if jobs:
            jobs.pop(0)()

    own_heads = pl.ds(pl.multiple_of(col_at * query_width, query_width), query_width)
    loads = [
        pltpu.make_async_copy(source, target, local_sems.at[number])
        for number, (source, target) in enumerate(
            (
                (grad_keyvalue.at[group_rows], keyvalues),
                (grad_rope.at[group_rows], ropes),
                (grad_query.at[0, group_rows], queries),
                (query_weight.at[:, own_heads], query_own),
            )
        )
    ]
    for copy in loads:
        copy.start()
    enter((slow_ids, fast_ids, row_ids, core_ids))
    for copy in loads:
        copy.wait()
    compressed = matmul_right(keyvalues[...], keyvalue_weight[...])
    unit = latent_normed[...]
    scaled = compressed * latent_gain[:1]
    inner = jnp.mean(scaled * unit, axis=1, keepdims=True)
    raw = latent_scale[...] * (scaled - unit * inner)
    latent_out[0] = jnp.concatenate([raw, ropes[...]], axis=1).astype(jnp.bfloat16)
    started = [remote(latent_out.at[0], latent_in, core_sems, (0,), core)]
    wide_out[...] = matmul_right(queries[...], query_other[...]).astype(jnp.bfloat16)
    started.append(remote(wide_out, wide_in, core_sems, (1,), core))
    latent_gain_part = jnp.sum(compressed * unit, axis=0, keepdims=True)
    own_wide = matmul_right(queries[...], query_own[...])
    wait_arrived(latent_in, core_sems, (0,))
    latent_out[1] = (
        latent_out[0].astype(jnp.float32) + latent_in[...].astype(jnp.float32)
    ).astype(jnp.bfloat16)
    for number, device in enumerate(row_ids):
        started.append(
            remote(latent_out.at[1], latent_row_in.at[number], row_sems, (0, number), device)
        )
    wait_arrived(wide_in, core_sems, (1,))
    own_wide = own_wide + wide_in[...].astype(jnp.float32)
    wide_rows[...] = own_wide.astype(jnp.bfloat16).reshape(wide_rows.shape)
    for number, device in enumerate(row_ids):
        goal = (row_at + number + 1) % row_count
        started.append(
            remote(wide_rows.at[goal], wide_row_in.at[number], row_sems, (1, number), device)
        )
    work()
    latent = latent_out[1].astype(jnp.float32)
    for number in range(row_count - 1):
        wait_arrived(latent_row_in.at[number], row_sems, (0, number))
        latent = latent + latent_row_in[number].astype(jnp.float32)
    latent_out[2] = latent.astype(jnp.bfloat16)
    part = count // 2
    first = pl.multiple_of(row_at * count, count)
    latent_block[...] = latent_out[2, pl.ds(pl.multiple_of(first + col_at * part, part), part)]
    gather = Gather(
        latent_block, lambda index: latent_all.at[index, col_at],
        lambda index: latent_all.at[index, 1 - col_at], gather_sems, True,
    )
    gather.start()
    steps = gather.steps()
    gradient = matmul(latent_out[2, pl.ds(first, count)], latent_weight[...])
    gradient = gradient + wide_rows[row_at].astype(jnp.float32)
    for number in range(row_count - 1):
        wait_arrived(wide_row_in.at[number], row_sems, (1, number))
        gradient = gradient + wide_row_in[number].astype(jnp.float32)
    scale = inverse_one[:, :1]
    normed = rows[...].astype(jnp.float32) * scale
    scaled = gradient * gain[:1]
    squares[...] = jnp.broadcast_to(
        jnp.sum(scaled * normed, axis=1, keepdims=True), squares.shape
    )
    started.append(remote(squares, squares_in, core_sems, (2,), core))
    steps.pop(0)()
    gain_part = jnp.sum(gradient * normed, axis=0, keepdims=True)
    row = lax.broadcasted_iota(jnp.int32, sums_in.shape, 0)
    padded = jnp.concatenate(
        [latent_gain_part, jnp.zeros((1, width - latent_gain_part.shape[1]), jnp.float32)], axis=1
    )
    total = jnp.where(row == 0, gain_part, jnp.where(row == 2, padded, sums_in[...]))
    wait_arrived(squares_in, core_sems, (2,))
    inner = (squares[...] + squares_in[...])[:, :1] / (2 * width)
    input_grad[...] = grad_hidden[...] + scale * (scaled - normed * inner)
    work()
    stages = (
        (slow_ids, slow_in, slow_sums),
        (fast_ids, fast_in, fast_sums),
        (row_ids, row_in, row_sums),
        (core_ids, core_in, core_sums),
    )
    for stage, (devices, buffer, sems) in enumerate(stages):
        running[stage] = total
        for number, device in enumerate(devices):
            started.append(
                remote(running.at[stage], buffer.at[number], sems, (number,), device)
            )
        steps.pop(0)()
        for number in range(len(devices)):
            wait_arrived(buffer.at[number], sems, (number,))
            arrived = buffer[number]
            total = total + (jnp.where(row == 2, arrived, 0.0) if stage == 3 else arrived)
    sums[...] = total
    for step in steps[: slow - 1]:
        step()
    while jobs:
        work()
    for step in steps[slow - 1 :]:
        step()
    gather.finish()
    for copy in started:
        copy.wait_send()


def weight_jobs(inputs, outputs, total):
    attended, stream, turned, small_turned, query_both, keyvalue = inputs
    return [
        row_job(small_turned, keyvalue, outputs[1], total),
        sided_job(attended, stream, outputs[0], total),
        sided_job(turned, query_both, outputs[2], total),
    ]


def tail(operands, shapes, fused, collective_id):
    exp_count, row_count = lax.axis_size("exp"), lax.axis_size("row")
    slow = min(4, exp_count)
    fast = exp_count // slow
    rows = operands[0]
    count, width = rows.shape
    group = row_count * count
    latent_width = operands[10].shape[0]
    query_width, keyvalue_width = operands[9].shape[1], operands[8].shape[1]
    low, high = jnp.bfloat16, jnp.float32
    vmem = pl.BlockSpec(memory_space=pltpu.VMEM)
    dma = pltpu.SemaphoreType.DMA
    sums = (8, width)
    counts = (slow - 1, fast - 1, row_count - 1, 1)
    return pl.pallas_call(
        functools.partial(tail_kernel, fused=fused),
        out_shape=[
            jax.ShapeDtypeStruct((count, width), high),
            jax.ShapeDtypeStruct(sums, high),
            jax.ShapeDtypeStruct((exp_count * row_count, 2, count // 2, latent_width), low),
            *shapes,
        ],
        in_specs=[vmem] * 11 + [ANY_SPEC] * 8,
        out_specs=[vmem, vmem] + [ANY_SPEC] * 4,
        scratch_shapes=[
            pltpu.VMEM((group, query_width), low),
            pltpu.VMEM((group, keyvalue_width), low),
            pltpu.VMEM((group, DR), high),
            pltpu.VMEM((width, query_width), low),
            pltpu.VMEM((3, group, latent_width), low),
            pltpu.VMEM((group, latent_width), low),
            pltpu.VMEM((row_count - 1, group, latent_width), low),
            pltpu.VMEM((group, width), low),
            pltpu.VMEM((group, width), low),
            pltpu.VMEM((row_count, count, width), low),
            pltpu.VMEM((row_count - 1, count, width), low),
            pltpu.VMEM((count // 2, latent_width), low),
            pltpu.VMEM((count, 128), high),
            pltpu.VMEM((count, 128), high),
            pltpu.VMEM((4, *sums), high),
            *[pltpu.VMEM((number, *sums), high) for number in counts],
            pltpu.VMEM(TOTAL if fused else (8, 128), high),
            dma((4,)),
            dma((2, 3)),
            dma((2, 2, row_count - 1)),
            *[dma((2, number)) for number in counts],
            *Gather.sems(),
        ],
        compiler_params=pltpu.CompilerParams(
            collective_id=collective_id, has_side_effects=True, vmem_limit_bytes=VMEM_LIMIT
        ),
    )(*operands)


def local(
    layer_input,
    attention_gain,
    query_weight,
    latent_weight,
    latent_gain,
    keyvalue_weight,
    output_weight,
    feedforward_gain,
    shared_gate,
    shared_up,
    shared_down,
    expert_gate,
    expert_up,
    expert_down,
    sequence_lengths,
    expert_ids,
    expert_weights,
    output_grad,
):
    exp_index, row_index, col_index = (
        lax.axis_index("exp"),
        lax.axis_index("row"),
        lax.axis_index("col"),
    )
    exp_count = lax.axis_size("exp")
    local_tokens, half_width = layer_input.shape
    full_width = 2 * half_width
    per_device = expert_gate.shape[0]
    group_size = local_tokens * lax.axis_size("row")
    tokens = group_size * exp_count
    group_start = exp_index * group_size

    def part_of(array, side, axis):
        width = array.shape[axis] // 2
        return lax.dynamic_slice_in_dim(array, side * width, width, axis)

    def split_exchange(array, axis):
        return part_of(array, col_index, axis), swap_core(part_of(array, 1 - col_index, axis))

    def own_rows(array):
        return lax.dynamic_slice_in_dim(array, group_start, group_size, 0)

    col = col_index.reshape(1)
    top = expert_ids.shape[1]
    _, places = sequence_layout(sequence_lengths[0], group_size)
    cosine, sine = rope_tables(places)
    first_key = jnp.arange(group_size, dtype=jnp.int32) - places

    def widened(array, width):
        return jnp.pad(array.astype(jnp.float32), ((0, 0), (0, width - array.shape[1])))

    tables = jnp.concatenate(
        [
            widened(expert_ids, 8),
            widened(expert_weights, 8),
            widened(first_key[:, None], 16),
            cosine,
            sine,
            jnp.zeros((group_size, 32), jnp.float32),
        ],
        axis=1,
    )
    latent_turned = latent_weight.T
    gate_turned, up_turned = expert_gate.swapaxes(1, 2), expert_up.swapaxes(1, 2)
    gain_own = jnp.broadcast_to(attention_gain.astype(jnp.float32), (8, half_width))
    latent_gains = jnp.broadcast_to(latent_gain.astype(jnp.float32), (8, R))

    gain_two = feedforward_gain.astype(jnp.float32)
    (
        own_normed, own_scale, inverse_one, hidden_state, normed_two, scale_two, mixer_input,
        tables_all, grad_all, query_other, latent_other, gain_other,
        gate_other, up_other, down_other, shared_gate_other, shared_up_other, shared_down_other,
    ) = prologue(
        layer_input, gain_own, latent_gains, keyvalue_weight, output_weight,
        gain_two[None], tables, query_weight, latent_turned, output_grad,
        (gate_turned, up_turned, expert_down, shared_gate, shared_up, shared_down), 6,
    )
    scale_two = scale_two[:, :1]
    weights = (
        gain_own, gain_other, query_weight, query_other, latent_turned, latent_other,
        latent_gains, keyvalue_weight,
    )
    tables_all = tables_all.reshape(tokens, -1)
    (
        mixer, input_all, both_hidden, both_gating, both_upward, shared_hidden, shared_gating,
        shared_upward, mixer_turned,
    ) = run_units(
        mixer_input,
        tables_all,
        grad_all,
        layer_input,
        (
            gate_turned, gate_other, up_turned, up_other, expert_down, down_other,
            shared_gate, shared_gate_other, shared_up, shared_up_other,
            shared_down, shared_down_other,
        ),
        1,
    )
    fused = tokens <= 2048
    low = jnp.bfloat16

    def shape(*sizes, kind=low):
        return jax.ShapeDtypeStruct(sizes, kind)

    units, shared_units = gate_turned.shape[1], shared_gate.shape[1]

    def gate_jobs(inputs, outputs, total, *_):
        gating, upward, rows, rows_turned, own_gating, own_upward = inputs
        return [
            stacked_job(gating, rows, outputs[0], total),
            stacked_job(upward, rows, outputs[1], total),
            row_job(rows_turned, own_gating, outputs[2], total),
            row_job(rows_turned, own_upward, outputs[3], total),
        ]

    gate_operands = (
        both_gating, both_upward, mixer, mixer_turned, shared_gating, shared_upward
    )
    gate_shapes = [shape(per_device, units, half_width)] * 2 + [
        shape(half_width, shared_units)
    ] * 2
    products = (
        both_gating, both_upward, gate_turned, up_turned, shared_gating, shared_upward,
        shared_gate, shared_up,
    )
    if fused:
        mixer_grad, *gate_grads = scatter_products(
            products, True, 2, gate_jobs, gate_operands, gate_shapes
        )
    else:
        (mixer_grad,) = scatter_products(products, True, 2)
        gate_grads = run_jobs(gate_jobs, gate_operands, gate_shapes)

    upstream = output_grad.astype(jnp.float32)
    grad_norm_two, gain_two_grad = norm_backward(mixer_grad, normed_two, scale_two, gain_two)
    grad_hidden = upstream + grad_norm_two

    heads_width = keyvalue_weight.shape[1] // 2
    query_width = query_weight.shape[1] // 2

    def stream_jobs(inputs, outputs, total):
        hidden, own_hidden, grads, values = inputs[:4]
        return [
            expert_down_job(hidden, grads, outputs[0], total),
            shared_down_job(own_hidden, grads, outputs[1], total),
            *project_jobs(values, inputs[4:12], inputs[12], outputs[2:], 2),
        ]

    stream_operands = (
        both_hidden, shared_hidden, grad_all, input_all, *weights, tables_all
    )
    stream_shapes = [
        shape(*expert_down.shape),
        shape(*shared_down.shape),
        shape(tokens, query_width),
        shape(tokens, keyvalue_weight.shape[1]),
        shape(tokens, DR),
        shape(half_width, tokens),
        shape(R, tokens),
    ]
    stream_input = grad_hidden.astype(jnp.bfloat16)
    if fused:
        stream, results = gather_everywhere(
            stream_input, 3, stream_jobs, stream_operands, stream_shapes
        )
    else:
        stream, _ = gather_everywhere(stream_input, 3)
        results = run_jobs(stream_jobs, stream_operands, stream_shapes)
    (
        expert_down_grad, shared_down_grad, query_all, keyvalue_all, rope_key_all,
        attention_turned, compressed_turned,
    ) = results

    other_hidden = swap_core(
        lax.dynamic_slice_in_dim(shared_hidden, group_start, group_size, 1)
    )

    def attention_part(inputs, outputs, total, core, sems):
        arrays, (stream_ref, weight) = inputs[:4], inputs[4:]
        attended_ref, query_both, keyvalue_ref, rope_ref = outputs
        jobs = attention_jobs(
            arrays, stream_ref, weight,
            (attended_ref, query_both.at[0], keyvalue_ref, rope_ref), exp_count, 4,
        )

        def exchange():
            remote(query_both.at[0], query_both.at[1], sems, (0,), core).wait()

        return [*jobs, exchange]

    weight_shapes = [
        shape(*output_weight.shape), shape(*keyvalue_weight.shape), shape(*query_weight.shape)
    ]
    (
        produced, attended_turned, query_grads, grad_keyvalue, grad_rope
    ) = scatter_products(
        (
            both_hidden, expert_down, down_other, shared_hidden, other_hidden,
            shared_down, shared_down_other,
        ),
        False,
        4,
        attention_part,
        (
            tables_all, query_all, keyvalue_all, rope_key_all, stream, output_weight,
        ),
        [
            shape(heads_width, tokens),
            shape(2, tokens, query_width),
            shape(tokens, keyvalue_weight.shape[1]),
            shape(tokens, DR, kind=jnp.float32),
        ],
    )
    layer_result = (hidden_state + produced).astype(jnp.bfloat16)
    sums_in = jnp.pad(gain_two_grad[None], ((1, 6), (0, 0)))
    weight_operands = (attended_turned, stream, attention_turned, compressed_turned)
    input_grad, sums, latent_all, *weight_grads = tail(
        (
            layer_input, inverse_one, gain_own, grad_hidden, sums_in, own_normed, own_scale,
            latent_gains, keyvalue_weight, query_other, latent_turned,
            query_grads, grad_keyvalue, grad_rope, query_weight, *weight_operands,
        ),
        weight_shapes,
        fused,
        5,
    )
    if not fused:
        weight_grads = run_jobs(
            weight_jobs, (*weight_operands, query_grads, grad_keyvalue), weight_shapes
        )
    output_weight_grad, keyvalue_weight_grad, query_weight_grad = weight_grads
    latent_weight_grad = matmul(attention_turned, latent_all.reshape(tokens, -1))
    wide = [
        array.astype(jnp.float32)
        for array in (
            query_weight_grad, keyvalue_weight_grad, output_weight_grad, *gate_grads,
            shared_down_grad, expert_down_grad,
        )
    ]
    return (
        layer_result,
        input_grad,
        sums[0],
        wide[0],
        latent_weight_grad,
        sums[2, : latent_gain.shape[0]],
        wide[1],
        wide[2],
        sums[1],
        wide[5],
        wide[6],
        wide[7],
        wide[3].swapaxes(1, 2),
        wide[4].swapaxes(1, 2),
        wide[8],
    )


def solution(mesh):
    in_specs = (
        P(("exp", "row"), "col"),
        P("col"),
        P("col", "row"),
        P("col", None),
        P(),
        P(None, ("row", "col")),
        P(("row", "col"), None),
        P("col"),
        P("col", "row"),
        P("col", "row"),
        P(("row", "col"), None),
        P("exp", "col", "row"),
        P("exp", "col", "row"),
        P("exp", ("row", "col"), None),
        P("exp", None),
        P("exp", None),
        P("exp", None),
        P(("exp", "row"), "col"),
    )
    out_specs = (
        P(("exp", "row"), "col"),
        P(("exp", "row"), "col"),
        P("col"),
        P("col", "row"),
        P("col", None),
        P(),
        P(None, ("row", "col")),
        P(("row", "col"), None),
        P("col"),
        P("col", "row"),
        P("col", "row"),
        P(("row", "col"), None),
        P("exp", "col", "row"),
        P("exp", "col", "row"),
        P("exp", ("row", "col"), None),
    )
    return jax.shard_map(local, mesh=mesh, in_specs=in_specs, out_specs=out_specs, check_vma=False)
```
